32 devices in a mesh: wide: 8 (over z, x), narrow: 4 (over y, core).
Axes of the slice: x: 2, y: 2, z: 4, core: 2. Of those that a mesh axis runs over, the one named last changes fastest.
Arguments:
- tokens: bfloat16 [1024, 1024], P('wide'), may hold values from -6 to 6
- cotangent: bfloat16 [1024, 1024], P('wide'), may hold values from -6 to 6
- expert_ids: int32 [1024, 1], P('wide'), may hold values from 0 to 1; in each aligned block of 128 rows (0 to 127, 128 to 255, ...) at most 128 rows name the same one
- route_prob: float32 [1024], P('wide'), may hold values from 0.2 to 1
- gate_weight: bfloat16 [2048, 2816], P('wide', 'narrow'), may hold values from -0.1875 to 0.1875
- up_weight: bfloat16 [2048, 2816], P('wide', 'narrow'), may hold values from -0.1875 to 0.1875
- down_weight: bfloat16 [2048, 2816], P('wide', 'narrow'), may hold values from -0.109375 to 0.109375
Outputs:
- output: bfloat16 [1024, 1024], P('wide', 'narrow')
- tokens_grad: bfloat16 [1024, 1024], P('wide', 'narrow')
- prob_grad: float32 [1024], P('wide')
- gate_grad: float32 [2048, 2816], P('wide', 'narrow')
- up_grad: float32 [2048, 2816], P('wide', 'narrow')
- down_grad: float32 [2048, 2816], P('wide', 'narrow')
The draws below stay inside these ranges and needn't reach their ends.
Inputs may be any that keep to these rules, and one draw needn't show every extreme that they name: `expert_ids`: among the 128 tokens of one index of wide, no expert is chosen by more than 128 tokens, and in some such groups one expert is chosen by exactly 128.
All inputs are finite; a program needn't handle non-finite values.
Results may differ from the reference program's by a relative error of at most 0.01.
Values may be sent and summed in bfloat16 or wider, within the bound.
No kernel may reach another device: no remote copies, remote signals or barrier semaphores. Data moves between devices by JAX's collectives and lax.ppermute only.
A program may use at most 64 MiB of HBM per device.

```python
import math
import jax
import jax.numpy as jnp
import numpy as np
from jax import lax

D = 1024
FF = 2816
TOK_DEV = 128
EXPERTS = 2
CAP = 128
TOKENS = 1024
N_NARROW = 4


def level_of(rng, dims, split, low, top_value):
    level = 1.0
    for dim, parts in split:
        draws = jax.random.uniform(jax.random.fold_in(jax.random.fold_in(rng, 6), dim), (parts,), jnp.float32, low / len(split), top_value / len(split))
        level = level * jnp.repeat(jnp.exp(draws), dims[dim] // parts).reshape((-1,) + (1,) * (len(dims) - 1 - dim))
    return level


def shared_out(key, own, number, rows, number_of, top, limit, lean):
    sequence = jax.random.permutation(key, number_of)
    packed, common = portions_of(number_of, rows * top, limit, lean, True), portions_of(number_of, rows * top, limit, lean, False)
    places = jnp.arange(number_of)

    def named(lengths, rotation):
        used = int((lengths > 0).sum())
        fixed = max(1, used // 4)
        shifted = fixed + (places - fixed + rotation * (used - fixed)) % max(1, number_of - fixed)
        return jnp.zeros((number_of,), jnp.int32).at[sequence[jnp.where(places < fixed, places, shifted)]].set(jnp.asarray(lengths, jnp.int32))

    lengths = jnp.where(number % 4 == 0, named(packed, number // 4), named(common, number - number // 4 - 1))
    mixed = jax.random.permutation(jax.random.fold_in(own, 3), number_of)
    source_of, receiver = mixed[0:number_of // 2 * 2:2], mixed[1:number_of // 2 * 2:2]
    slack = jnp.minimum(lengths[source_of] - 1, limit - lengths[receiver]) // 2
    slack = jnp.where((source_of == sequence[0]) | (receiver == sequence[0]) | (lengths[receiver] == 0), 0, jnp.maximum(slack, 0))
    shifted = jax.random.randint(jax.random.fold_in(own, 4), (number_of // 2,), 0, 1 << 20) % (slack + 1)
    lengths = lengths.at[source_of].add(-shifted).at[receiver].add(shifted)
    labels = jnp.searchsorted(jnp.cumsum(lengths), jnp.arange(rows * top), side="right").astype(jnp.int32)
    table = labels.reshape(top, rows).T
    table = table[jax.random.permutation(jax.random.fold_in(own, 1), rows)]
    rotation = jax.random.randint(jax.random.fold_in(own, 2), (rows, 1), 0, top)
    return jnp.take_along_axis(table, (jnp.arange(top)[None, :] + rotation) % top, axis=1)


def portions_of(amount, total, limit, lean, full):
    weights = [(1 << 20) // math.isqrt(rank ** lean) + 1 for rank in range(1, amount + 1)]
    largest = limit if full else min(limit, max(-(-total // amount), total * weights[0] // sum(weights)))
    least = 1 if total - largest >= amount - 1 else 0
    given, spare = [largest] + [least] * (amount - 1), total - largest - least * (amount - 1)
    while spare > 0:
        candidates = [i for i in range(1, amount) if given[i] < largest] or [i for i in range(1, amount) if given[i] < limit]
        mass, budget = sum([weights[i] for i in candidates]), spare
        for i in candidates:
            extra = min(limit - given[i], max(1, budget * weights[i] // mass), spare)
            given[i] = given[i] + extra
            spare = spare - extra
    return np.array(given)


def bell_draw(stream_key, dims, width, most, shards=(), kind=jnp.bfloat16):
    factor_of = level_of(stream_key, dims, shards, -0.22, 0.18) if shards else 1.0
    entries = jax.random.normal(stream_key, dims, jnp.float32) * width * factor_of
    return jnp.minimum(jnp.maximum(entries, -most), most).astype(kind)


def setup_inputs(seed: int = 0) -> dict:
    splits = jax.random.split(jax.random.key(seed), 8)
    tokens = bell_draw(splits[0], (TOKENS, D), 1.0, 6.0, ((0, 8),))
    cotangent = bell_draw(splits[1], (TOKENS, D), 1.0, 6.0, ((0, 8),))
    expert_ids_keys = jax.random.split(jax.random.fold_in(splits[2], 1), TOKENS // TOK_DEV)
    expert_ids_turns = jax.random.permutation(jax.random.fold_in(splits[2], 3), TOKENS // TOK_DEV)
    expert_ids = jax.vmap(lambda own, number: shared_out(jax.random.fold_in(splits[2], 2), own, number, TOK_DEV, EXPERTS, 1, CAP, 2))(expert_ids_keys, expert_ids_turns).reshape((TOKENS, 1))
    route_prob = jnp.clip(0.2 + 0.8 * jax.random.uniform(splits[3], (TOKENS,), jnp.float32) ** level_of(splits[3], (TOKENS,), ((0, 8),), -0.2, 0.2), 0.2, 1.0)
    gate_weight = bell_draw(splits[4], (EXPERTS * D, FF), D ** -0.5, 0.1875, ((0, 8), (1, 4)))
    up_weight = bell_draw(splits[5], (EXPERTS * D, FF), D ** -0.5, 0.1875, ((0, 8), (1, 4)))
    down_weight = bell_draw(splits[6], (EXPERTS * D, FF), FF ** -0.5, 0.109375, ((0, 8), (1, 4)))
    return dict(tokens=tokens, cotangent=cotangent, expert_ids=expert_ids, route_prob=route_prob, gate_weight=gate_weight, up_weight=up_weight, down_weight=down_weight)


def rounded_term(value):
    return lax.optimization_barrier(value.astype(jnp.bfloat16)).astype(jnp.float32)


def reference(tokens, cotangent, expert_ids, route_prob, gate_weight, up_weight, down_weight):
    block_rows = 128
    block_total = TOKENS // block_rows + EXPERTS
    padded_rows = block_total * block_rows
    fourth = FF // N_NARROW
    chosen = expert_ids[:, 0].astype(jnp.int32)
    sorted_order = jnp.argsort(chosen, stable=True).astype(jnp.int32)
    counts = jnp.sum((chosen[:, None] == jnp.arange(EXPERTS, dtype=jnp.int32)[None, :]).astype(jnp.int32), axis=0)
    starts = jnp.cumsum(counts) - counts
    rounded = (counts + block_rows - 1) // block_rows * block_rows
    offsets = jnp.cumsum(rounded) - rounded
    sorted_ids = chosen[sorted_order]
    slot_sorted = (offsets[sorted_ids] + jnp.arange(TOKENS, dtype=jnp.int32) - starts[sorted_ids]).astype(jnp.int32)
    source = jnp.full((padded_rows,), TOKENS, jnp.int32).at[slot_sorted].set(sorted_order)
    slot_token = jnp.zeros((TOKENS,), jnp.int32).at[sorted_order].set(slot_sorted)
    block_start = jnp.arange(block_total, dtype=jnp.int32) * block_rows
    block_expert = jnp.minimum(jnp.sum(((offsets + rounded)[None, :] <= block_start[:, None]).astype(jnp.int32), axis=1), EXPERTS - 1).astype(jnp.int32)
    scaled = (route_prob[:, None] * cotangent.astype(jnp.float32)).astype(jnp.bfloat16)
    blank_row = jnp.zeros((1, D), jnp.bfloat16)
    padded_in = jnp.concatenate([tokens, blank_row], 0)
    padded_cot = jnp.concatenate([scaled, blank_row], 0)
    gate_all = gate_weight.reshape(EXPERTS, D, FF)
    up_all = up_weight.reshape(EXPERTS, D, FF)
    down_all = down_weight.reshape(EXPERTS, D, FF)

    def block_step(state_tuple, block_index):
        gate_acc, up_acc, down_acc = state_tuple
        expert = block_expert[block_index]
        picks = lax.dynamic_slice_in_dim(source, block_index * block_rows, block_rows)
        rows_in = padded_in[picks]
        rows_cot = padded_cot[picks]
        gate_mat = gate_all[expert]
        up_mat = up_all[expert]
        down_mat = down_all[expert]
        gate_val = jnp.dot(rows_in, gate_mat, preferred_element_type=jnp.float32)
        up_val = jnp.dot(rows_in, up_mat, preferred_element_type=jnp.float32)
        gate_sigma = jax.nn.sigmoid(gate_val)
        active = gate_val * gate_sigma
        hidden = (active * up_val).astype(jnp.bfloat16)
        d_hidden = jnp.dot(rows_cot, down_mat, preferred_element_type=jnp.float32)
        d_gate = (d_hidden * up_val * gate_sigma * (1.0 + gate_val * (1.0 - gate_sigma))).astype(jnp.bfloat16)
        d_up = (d_hidden * active).astype(jnp.bfloat16)
        ffn_sum = jnp.zeros((block_rows, D), jnp.float32)
        grad_sum = jnp.zeros((block_rows, D), jnp.float32)
        for quarter in range(N_NARROW):
            low = quarter * fourth
            high = low + fourth
            ffn_sum = ffn_sum + rounded_term(jnp.dot(hidden[:, low:high], down_mat[:, low:high].T, preferred_element_type=jnp.float32))
            term = jnp.dot(d_gate[:, low:high], gate_mat[:, low:high].T, preferred_element_type=jnp.float32)
            term = term + jnp.dot(d_up[:, low:high], up_mat[:, low:high].T, preferred_element_type=jnp.float32)
            grad_sum = grad_sum + rounded_term(term)
        gate_acc = gate_acc.at[expert].add(jnp.dot(rows_in.T, d_gate, preferred_element_type=jnp.float32))
        up_acc = up_acc.at[expert].add(jnp.dot(rows_in.T, d_up, preferred_element_type=jnp.float32))
        down_acc = down_acc.at[expert].add(jnp.dot(rows_cot.T, hidden, preferred_element_type=jnp.float32))
        return (gate_acc, up_acc, down_acc), (ffn_sum.astype(jnp.bfloat16), grad_sum.astype(jnp.bfloat16))

    zero_grads = jnp.zeros((EXPERTS, D, FF), jnp.float32)
    state_tuple, outputs = lax.scan(block_step, (zero_grads, zero_grads, zero_grads), jnp.arange(block_total, dtype=jnp.int32))
    ffn_rows = outputs[0].reshape(padded_rows, D)[slot_token]
    grad_rows = outputs[1].reshape(padded_rows, D)[slot_token]
    output = (route_prob[:, None] * ffn_rows.astype(jnp.float32)).astype(jnp.bfloat16)
    prob_grad = jnp.sum(ffn_rows.astype(jnp.float32) * cotangent.astype(jnp.float32), axis=1)
    gate_grad = state_tuple[0].reshape(EXPERTS * D, FF)
    up_grad = state_tuple[1].reshape(EXPERTS * D, FF)
    down_grad = state_tuple[2].reshape(EXPERTS * D, FF)
    return (output, grad_rows, prob_grad, gate_grad, up_grad, down_grad)
```

```python
import functools

import jax
import jax.numpy as jnp
from jax import lax
from jax.experimental import pallas as pl
from jax.experimental.pallas import tpu as pltpu
from jax.sharding import PartitionSpec as P

VMEM = pl.BlockSpec(memory_space=pltpu.VMEM)
PARAMS = pltpu.CompilerParams(vmem_limit_bytes=48 * 1024 * 1024)


def partner(x, axis, mask):
    return lax.ppermute(x, axis, [(i, i ^ mask) for i in range(lax.axis_size(axis))])


def dot_nn(left, right):
    return lax.dot_general(
        left, right, (((1,), (0,)), ((), ())), preferred_element_type=jnp.float32
    )


def dot_nt(left, right):
    return lax.dot_general(
        left, right, (((1,), (1,)), ((), ())), preferred_element_type=jnp.float32
    )


def at_quarter(index, width):
    return pl.ds(pl.multiple_of(index * width, width), width)


def halves_kernel(gate, up, down, keep, give):
    half = keep.shape[1]
    x_bit = lax.axis_index("wide") % 2
    keep_rows = pl.ds(pl.multiple_of(x_bit * half, 16), half)
    give_rows = pl.ds(pl.multiple_of((1 - x_bit) * half, 16), half)
    for i, ref in enumerate((gate, up, down)):
        keep[i] = ref[keep_rows, :]
        give[i] = ref[give_rows, :]


def split_halves(gate, up, down):
    hidden, width = gate.shape
    shape = jax.ShapeDtypeStruct((3, hidden // 2, width), jnp.bfloat16)
    return pl.pallas_call(
        halves_kernel,
        out_shape=(shape, shape),
        in_specs=[VMEM] * 3,
        out_specs=[VMEM] * 2,
        compiler_params=PARAMS,
    )(gate, up, down)


def route_kernel(tokens, cotangent, ids, prob, own, same, other):
    rows, features = tokens.shape
    width = same.shape[2]
    mine = lax.axis_index("wide") // 4
    column = at_quarter(lax.axis_index("narrow"), width)
    chosen = jnp.transpose(jnp.broadcast_to(ids[...], (128, rows)).astype(jnp.float32))[:, :1]
    weight = jnp.transpose(jnp.broadcast_to(prob[...], (128, rows)))[:, :1]
    is_mine = chosen == mine.astype(jnp.float32)
    here = jnp.where(is_mine, 1.0, 0.0)
    for i, ref in enumerate((tokens, cotangent)):
        factor = here if i == 0 else here * weight
        own[i] = (ref[...].astype(jnp.float32) * factor).astype(jnp.bfloat16)
        part = ref[:, column].astype(jnp.float32)
        if i == 1:
            part = part * weight
        same[i] = (part * here).astype(jnp.bfloat16)
        other[i] = (part * (1.0 - here)).astype(jnp.bfloat16)


def route_rows(tokens, cotangent, ids, prob, width):
    rows, features = tokens.shape
    return pl.pallas_call(
        route_kernel,
        out_shape=(
            jax.ShapeDtypeStruct((2, rows, features), jnp.bfloat16),
            jax.ShapeDtypeStruct((2, rows, width), jnp.bfloat16),
            jax.ShapeDtypeStruct((2, rows, width), jnp.bfloat16),
        ),
        in_specs=[VMEM] * 4,
        out_specs=[VMEM] * 3,
        compiler_params=PARAMS,
    )(tokens, cotangent, ids, prob)


def forward_kernel(has_own, *refs):
    own = refs[0] if has_own else None
    pieces, weights = refs[has_own : has_own + 4], refs[has_own + 4 : has_own + 8]
    kept, sent, grads, x_all, s_all, w_all = refs[has_own + 8 :]
    blocks, _, slots, width = pieces[0].shape
    member = lax.axis_index("wide") % 4
    place = lax.axis_index("narrow")
    for k, ref in enumerate(weights):
        column = at_quarter(member ^ k, width)
        for i in range(3):
            w_all[i, :, column] = ref[i]
    first = 0
    if has_own:
        x_all[:slots, :] = own[0]
        s_all[:slots, :] = own[1]
        first = slots
    for mask, ref in enumerate(pieces):
        column = at_quarter(place ^ mask, width)
        for block in range(blocks):
            rows = slice(first + block * slots, first + (block + 1) * slots)
            x_all[rows, column] = ref[block, 0]
            s_all[rows, column] = ref[block, 1]
    total = x_all.shape[0]
    tile = min(256, total)

    @pl.loop(0, total // tile)
    def _(step):
        rows = pl.ds(pl.multiple_of(step * tile, tile), tile)
        x_tile, s_tile = x_all[rows, :], s_all[rows, :]
        gate = dot_nt(w_all[0], x_tile)
        up = dot_nt(w_all[1], x_tile)
        d_hidden = dot_nt(w_all[2], s_tile)
        sigma = jax.nn.sigmoid(gate)
        active = gate * sigma
        hidden = (active * up).astype(jnp.bfloat16)
        d_gate = (d_hidden * up * sigma * (1.0 + gate * (1.0 - sigma))).astype(jnp.bfloat16)
        d_up = (d_hidden * active).astype(jnp.bfloat16)
        grads[0, :, rows] = d_gate
        grads[1, :, rows] = d_up
        grads[2, :, rows] = hidden
        hidden_t, d_gate_t, d_up_t = hidden.T, d_gate.T, d_up.T
        for mask in range(4):
            column = at_quarter(place ^ mask, width)
            out_part = dot_nn(hidden_t, w_all[2, :, column])
            in_part = dot_nn(d_gate_t, w_all[0, :, column]) + dot_nn(d_up_t, w_all[1, :, column])
            target = sent if mask % 2 else kept
            target[mask // 2, 0, rows, :] = out_part.astype(target.dtype)
            target[mask // 2, 1, rows, :] = in_part.astype(target.dtype)


def forward(own, pieces, weights):
    blocks, _, slots, width = pieces[0].shape
    half = weights[0].shape[1]
    has_own = own is not None
    total = (blocks + has_own) * slots
    features = 4 * width
    return pl.pallas_call(
        functools.partial(forward_kernel, int(has_own)),
        out_shape=(
            jax.ShapeDtypeStruct((2, 2, total, width), jnp.float32),
            jax.ShapeDtypeStruct((2, 2, total, width), jnp.bfloat16),
            jax.ShapeDtypeStruct((3, half, total), jnp.bfloat16),
            jax.ShapeDtypeStruct((total, features), jnp.bfloat16),
            jax.ShapeDtypeStruct((total, features), jnp.bfloat16),
        ),
        in_specs=[VMEM] * (8 + has_own),
        out_specs=[VMEM] * 5,
        scratch_shapes=[pltpu.VMEM((3, half, features), jnp.bfloat16)],
        compiler_params=PARAMS,
    )(*([own] if has_own else []), *pieces, *weights)


def grads_kernel(grads, x_all, s_all, *outs):
    half, total = grads.shape[1:]
    width = outs[0].shape[2]
    member = lax.axis_index("wide") % 4
    left = grads[0:2].reshape(2 * half, total)
    for k in (1, 2, 3, 0):
        column = at_quarter(member ^ k, width)
        both = dot_nn(left, x_all[:, column])
        outs[k][0] = both[:half].astype(outs[k].dtype)
        outs[k][1] = both[half:].astype(outs[k].dtype)
        outs[k][2] = dot_nn(grads[2], s_all[:, column]).astype(outs[k].dtype)


def weight_grads(grads, x_all, s_all):
    half = grads.shape[1]
    width = x_all.shape[1] // 4
    return pl.pallas_call(
        grads_kernel,
        out_shape=tuple(
            jax.ShapeDtypeStruct((3, half, width), jnp.bfloat16 if k else jnp.float32)
            for k in range(4)
        ),
        in_specs=[VMEM] * 3,
        out_specs=[VMEM] * 4,
        compiler_params=PARAMS,
    )(grads, x_all, s_all)


def join_kernel(own, got_x, got_z, got_d, *outs):
    half = own.shape[1]
    x_bit = lax.axis_index("wide") % 2
    keep_rows = pl.ds(pl.multiple_of(x_bit * half, 16), half)
    give_rows = pl.ds(pl.multiple_of((1 - x_bit) * half, 16), half)
    for i, ref in enumerate(outs):
        ref[keep_rows, :] = own[i] + got_z[i].astype(jnp.float32)
        ref[give_rows, :] = got_x[i].astype(jnp.float32) + got_d[i].astype(jnp.float32)


def join_grads(own, got_x, got_z, got_d):
    _, half, width = own.shape
    shape = jax.ShapeDtypeStruct((2 * half, width), jnp.float32)
    return pl.pallas_call(
        join_kernel,
        out_shape=(shape,) * 3,
        in_specs=[VMEM] * 4,
        out_specs=[VMEM] * 3,
        compiler_params=PARAMS,
    )(own, got_x, got_z, got_d)


def shards(tokens, cotangent, expert_ids, route_prob, gate_weight, up_weight, down_weight):
    wide_count = lax.axis_size("wide")
    narrow_count = lax.axis_size("narrow")
    expert_count = wide_count // 4
    tok_rows, features = tokens.shape
    width = features // narrow_count
    slots = min(4 * tok_rows // expert_count, tok_rows)
    direct = expert_count == 2 and slots == tok_rows
    place = lax.axis_index("narrow")
    masks = (1, 4, 5)
    groups = [
        [4 * e + 2 * b + a for e in range(expert_count) for a in range(2)] for b in range(2)
    ]

    if direct:
        own, same, other = route_rows(
            tokens, cotangent, expert_ids.T, route_prob[None, :], width
        )
        mine = jnp.stack(
            [partner(part, "wide", mask) for mask, part in zip(masks, (same, other, other))]
        )
    else:
        own = None
        chosen = expert_ids[:, 0]
        onehot = (chosen[:, None] == jnp.arange(expert_count, dtype=jnp.int32)[None, :]).astype(
            jnp.int32
        )
        rank = jnp.sum((jnp.cumsum(onehot, axis=0) - onehot) * onehot, axis=1)
        slot_place = chosen * slots + rank
        source = (
            jnp.full((expert_count * slots,), tok_rows, jnp.int32)
            .at[slot_place]
            .set(jnp.arange(tok_rows, dtype=jnp.int32))
        )
        scaled = (route_prob[:, None] * cotangent.astype(jnp.float32)).astype(jnp.bfloat16)
        both = jnp.stack([tokens, scaled])
        both = lax.dynamic_slice_in_dim(both, place * width, width, 2)
        both = jnp.concatenate([both, jnp.zeros((2, 1, width), jnp.bfloat16)], 1)
        routed = both[:, source].reshape(2, expert_count, slots, width).transpose(1, 0, 2, 3)
        routed = jnp.repeat(routed, 2, axis=0)
        mine = lax.all_to_all(
            routed, "wide", split_axis=0, concat_axis=0, axis_index_groups=groups, tiled=True
        )

    keep, give = split_halves(gate_weight.T, up_weight.T, down_weight.T)
    weights = (
        keep,
        partner(give, "wide", 1),
        partner(keep, "wide", 2),
        partner(give, "wide", 3),
    )
    across = partner(mine, "narrow", 2)
    pieces = (mine, partner(mine, "narrow", 1), across, partner(across, "narrow", 1))
    kept, sent, grads, x_all, s_all = forward(own, pieces, weights)

    got = partner(sent, "narrow", 1)
    grad_own, grad_x, grad_z, grad_d = weight_grads(grads, x_all, s_all)
    got_x = partner(grad_x, "wide", 1)
    got_z = partner(grad_z, "wide", 2)
    got_d = partner(grad_d, "wide", 3)

    across = partner((kept[1] + got[1].astype(jnp.float32)).astype(jnp.bfloat16), "narrow", 2)
    result = kept[0] + got[0].astype(jnp.float32) + across.astype(jnp.float32)
    if direct:
        total = result[:, :slots]
        for k, mask in enumerate(masks):
            rows = result[:, (k + 1) * slots : (k + 2) * slots].astype(jnp.bfloat16)
            total = total + partner(rows, "wide", mask).astype(jnp.float32)
    else:
        parts = result.astype(jnp.bfloat16).reshape(2, 2 * expert_count, slots, width)
        back = lax.all_to_all(
            parts, "wide", split_axis=1, concat_axis=1, axis_index_groups=groups, tiled=True
        )
        back = back.reshape(2, expert_count, 2, slots, width).astype(jnp.float32).sum(2)
        total = back.reshape(2, expert_count * slots, width)[:, slot_place]
    ffn = total[0].astype(jnp.bfloat16).astype(jnp.float32)
    tokens_grad = total[1].astype(jnp.bfloat16)
    output = (route_prob[:, None] * ffn).astype(jnp.bfloat16)
    cot_columns = lax.dynamic_slice_in_dim(cotangent, place * width, width, 1)
    prob_grad = lax.psum(jnp.sum(ffn * cot_columns.astype(jnp.float32), axis=1), "narrow")
    gate_grad, up_grad, down_grad = join_grads(grad_own, got_x, got_z, got_d)
    return (output, tokens_grad, prob_grad, gate_grad.T, up_grad.T, down_grad.T)


def solution(mesh):
    in_specs = (
        P("wide", None),
        P("wide", None),
        P("wide", None),
        P("wide"),
        P("wide", "narrow"),
        P("wide", "narrow"),
        P("wide", "narrow"),
    )
    out_specs = (
        P("wide", "narrow"),
        P("wide", "narrow"),
        P("wide"),
        P("wide", "narrow"),
        P("wide", "narrow"),
        P("wide", "narrow"),
    )
    return jax.shard_map(shards, mesh=mesh, in_specs=in_specs, out_specs=out_specs, check_vma=False)
```

```python
import functools

import jax
import jax.numpy as jnp
from jax import lax
from jax.experimental import pallas as pl
from jax.experimental.pallas import tpu as pltpu
from jax.sharding import PartitionSpec as P

VMEM = pl.BlockSpec(memory_space=pltpu.VMEM)
HBM = pl.BlockSpec(memory_space=pltpu.HBM)
PARAMS = pltpu.CompilerParams(vmem_limit_bytes=32 * 1024 * 1024)
PROLOGUE_PARAMS = pltpu.CompilerParams(vmem_limit_bytes=61 * 1024 * 1024)


def partner(x, axis, mask):
    return lax.ppermute(x, axis, [(i, i ^ mask) for i in range(lax.axis_size(axis))])


def dot_nn(left, right):
    return lax.dot_general(
        left, right, (((1,), (0,)), ((), ())), preferred_element_type=jnp.float32
    )


def dot_nt(left, right):
    return lax.dot_general(
        left, right, (((1,), (1,)), ((), ())), preferred_element_type=jnp.float32
    )


def at_quarter(index, width):
    return pl.ds(pl.multiple_of(index * width, width), width)


def prologue_kernel(routed, gate, up, down, *refs):
    if routed:
        tokens, cotangent, ids, prob, keep, give, own, same, other = refs[:9]
        held, ids_row, prob_row, sems = refs[9:]
        parts = ((tokens, held.at[0]), (cotangent, held.at[1]), (ids, ids_row), (prob, prob_row))
    else:
        keep, give, sems = refs
        parts = ()
    half = keep.shape[1]
    x_bit = lax.axis_index("wide") % 2
    keep_rows = pl.ds(pl.multiple_of(x_bit * half, 16), half)
    give_rows = pl.ds(pl.multiple_of((1 - x_bit) * half, 16), half)
    for i, ref in enumerate((gate, up, down)):
        parts += ((ref.at[keep_rows, :], keep.at[i]), (ref.at[give_rows, :], give.at[i]))
    copies = [pltpu.make_async_copy(src, dst, sems.at[i]) for i, (src, dst) in enumerate(parts)]
    for copy in copies:
        copy.start()
    if routed:
        for copy in copies[:4]:
            copy.wait()
        rows = held.shape[1]
        width = same.shape[2]
        mine = lax.axis_index("wide") // 4
        column = at_quarter(lax.axis_index("narrow"), width)
        chosen = jnp.broadcast_to(ids_row[...], (128, rows)).astype(jnp.float32).T[:, :1]
        weight = jnp.broadcast_to(prob_row[...], (128, rows)).T[:, :1]
        here = jnp.where(chosen == mine.astype(jnp.float32), 1.0, 0.0)
        for i in range(2):
            factor = weight if i else jnp.ones_like(weight)
            own[i] = (held[i].astype(jnp.float32) * (factor * here)).astype(jnp.bfloat16)
            part = held[i, :, column].astype(jnp.float32)
            same[i] = (part * (factor * here)).astype(jnp.bfloat16)
            other[i] = (part * (factor * (1.0 - here))).astype(jnp.bfloat16)
    for copy in copies[len(copies) - 6 :]:
        copy.wait()


def prologue(weights, token_args, width):
    hidden, quarter = weights[0].shape
    half = jax.ShapeDtypeStruct((3, hidden // 2, quarter), jnp.bfloat16)
    outs, scratch = (half, half), []
    if token_args:
        rows, features = token_args[0].shape
        part = jax.ShapeDtypeStruct((2, rows, width), jnp.bfloat16)
        outs += (jax.ShapeDtypeStruct((2, rows, features), jnp.bfloat16), part, part)
        scratch = [
            pltpu.VMEM((2, rows, features), jnp.bfloat16),
            pltpu.VMEM((1, rows), jnp.int32),
            pltpu.VMEM((1, rows), jnp.float32),
        ]
    return pl.pallas_call(
        functools.partial(prologue_kernel, bool(token_args)),
        out_shape=outs,
        in_specs=[HBM] * (3 + len(token_args)),
        out_specs=[VMEM] * len(outs),
        scratch_shapes=scratch + [pltpu.SemaphoreType.DMA((10,))],
        compiler_params=PROLOGUE_PARAMS,
    )(*weights, *token_args)


def gather_kernel(has_own, *refs):
    own = refs[0] if has_own else None
    pieces, weights = refs[has_own : has_own + 4], refs[has_own + 4 : has_own + 7]
    x_all, s_all, w_all, part = refs[has_own + 7 :]
    blocks, _, slots, width = pieces[0].shape
    member = lax.axis_index("wide") % 4
    place = lax.axis_index("narrow")
    for k, ref in enumerate(weights):
        column = at_quarter(member ^ k, width)
        for i in range(3):
            w_all[i, :, column] = ref[i]
    first = 0
    if has_own:
        x_all[:slots, :] = own[0]
        s_all[:slots, :] = own[1]
        first = slots
    for mask, ref in enumerate(pieces):
        column = at_quarter(place ^ mask, width)
        for block in range(blocks):
            rows = slice(first + block * slots, first + (block + 1) * slots)
            x_all[rows, column] = ref[block, 0]
            s_all[rows, column] = ref[block, 1]
    total = x_all.shape[0]
    tile = min(256, total)

    @pl.loop(0, total // tile)
    def _(step):
        rows = pl.ds(pl.multiple_of(step * tile, tile), tile)
        for i in range(3):
            held = s_all if i == 2 else x_all
            sums = None
            for k in range(3):
                column = at_quarter(member ^ k, width)
                term = dot_nt(w_all[i, :, column], held[rows, column])
                sums = term if sums is None else sums + term
            part[i, :, rows] = sums


def gather_parts(own, pieces, weights):
    blocks, _, slots, width = pieces[0].shape
    half = weights[0].shape[1]
    has_own = own is not None
    total = (blocks + has_own) * slots
    features = 4 * width
    return pl.pallas_call(
        functools.partial(gather_kernel, int(has_own)),
        out_shape=(
            jax.ShapeDtypeStruct((total, features), jnp.bfloat16),
            jax.ShapeDtypeStruct((total, features), jnp.bfloat16),
            jax.ShapeDtypeStruct((3, half, features), jnp.bfloat16),
            jax.ShapeDtypeStruct((3, half, total), jnp.float32),
        ),
        in_specs=[VMEM] * (7 + has_own),
        out_specs=[VMEM] * 4,
        compiler_params=PARAMS,
        cost_estimate=pl.CostEstimate(
            flops=6 * 2 * half * 3 * width * total, bytes_accessed=0, transcendentals=0
        ),
    )(*([own] if has_own else []), *pieces, *weights)


def main_kernel(x_all, s_all, w_part, part, last, kept, sent, own, to_x, to_z, to_d, grads, w_all):
    outs = (own, to_x, to_z, to_d)
    half, width = last.shape[1:]
    member = lax.axis_index("wide") % 4
    place = lax.axis_index("narrow")
    last_column = at_quarter(member ^ 3, width)
    w_all[...] = w_part[...]
    for i in range(3):
        w_all[i, :, last_column] = last[i]
    total = x_all.shape[0]
    tile = min(256, total)

    @pl.loop(0, total // tile)
    def _(step):
        rows = pl.ds(pl.multiple_of(step * tile, tile), tile)
        x_tile, s_tile = x_all[rows, last_column], s_all[rows, last_column]
        gate = part[0, :, rows] + dot_nt(last[0], x_tile)
        up = part[1, :, rows] + dot_nt(last[1], x_tile)
        d_hidden = part[2, :, rows] + dot_nt(last[2], s_tile)
        sigma = jax.nn.sigmoid(gate)
        active = gate * sigma
        hidden = (active * up).astype(jnp.bfloat16)
        d_gate = (d_hidden * up * sigma * (1.0 + gate * (1.0 - sigma))).astype(jnp.bfloat16)
        d_up = (d_hidden * active).astype(jnp.bfloat16)
        grads[0, :, rows] = d_gate
        grads[1, :, rows] = d_up
        grads[2, :, rows] = hidden
        hidden_t, d_gate_t, d_up_t = hidden.T, d_gate.T, d_up.T
        for mask in range(4):
            column = at_quarter(place ^ mask, width)
            out_part = dot_nn(hidden_t, w_all[2, :, column])
            in_part = dot_nn(d_gate_t, w_all[0, :, column]) + dot_nn(d_up_t, w_all[1, :, column])
            target = sent if mask % 2 else kept
            target[mask // 2, 0, rows, :] = out_part.astype(target.dtype)
            target[mask // 2, 1, rows, :] = in_part.astype(target.dtype)

    left = grads[0:2].reshape(2 * half, total)
    for k in (3, 2, 1, 0):
        column = at_quarter(member ^ k, width)
        both = dot_nn(left, x_all[:, column])
        outs[k][0] = both[:half].astype(outs[k].dtype)
        outs[k][1] = both[half:].astype(outs[k].dtype)
        outs[k][2] = dot_nn(grads[2], s_all[:, column]).astype(outs[k].dtype)


def main(x_all, s_all, w_part, part, last):
    total, features = x_all.shape
    _, half, width = last.shape
    return pl.pallas_call(
        main_kernel,
        out_shape=(
            jax.ShapeDtypeStruct((2, 2, total, width), jnp.float32),
            jax.ShapeDtypeStruct((2, 2, total, width), jnp.bfloat16),
        )
        + tuple(
            jax.ShapeDtypeStruct((3, half, width), jnp.bfloat16 if k > 1 else jnp.float32)
            for k in range(4)
        ),
        in_specs=[VMEM] * 5,
        out_specs=[VMEM] * 6,
        scratch_shapes=[
            pltpu.VMEM((3, half, total), jnp.bfloat16),
            pltpu.VMEM((3, half, features), jnp.bfloat16),
        ],
        compiler_params=PARAMS,
        cost_estimate=pl.CostEstimate(
            flops=12 * 2 * half * features * total, bytes_accessed=0, transcendentals=0
        ),
    )(x_all, s_all, w_part, part, last)


def join_kernel(own, got_x, got_z, *outs):
    half = own.shape[1]
    x_bit = lax.axis_index("wide") % 2
    keep_rows = pl.ds(pl.multiple_of(x_bit * half, 16), half)
    give_rows = pl.ds(pl.multiple_of((1 - x_bit) * half, 16), half)
    for i, ref in enumerate(outs):
        ref[keep_rows, :] = own[i] + got_z[i].astype(jnp.float32)
        ref[give_rows, :] = got_x[i].astype(jnp.float32)


def join_grads(own, got_x, got_z):
    _, half, width = own.shape
    shape = jax.ShapeDtypeStruct((2 * half, width), jnp.float32)
    return pl.pallas_call(
        join_kernel,
        out_shape=(shape,) * 3,
        in_specs=[VMEM] * 3,
        out_specs=[VMEM] * 3,
        compiler_params=PARAMS,
    )(own, got_x, got_z)


def shards(tokens, cotangent, expert_ids, route_prob, gate_weight, up_weight, down_weight):
    wide_count = lax.axis_size("wide")
    narrow_count = lax.axis_size("narrow")
    expert_count = wide_count // 4
    tok_rows, features = tokens.shape
    width = features // narrow_count
    slots = min(4 * tok_rows // expert_count, tok_rows)
    direct = expert_count == 2 and slots == tok_rows
    place = lax.axis_index("narrow")
    masks = (1, 4, 5)
    groups = [
        [4 * e + 2 * b + a for e in range(expert_count) for a in range(2)] for b in range(2)
    ]

    weights = (gate_weight.T, up_weight.T, down_weight.T)
    if direct:
        keep, give, own, same, other = prologue(
            weights, (tokens, cotangent, expert_ids.T, route_prob[None, :]), width
        )
        mine = jnp.stack(
            [partner(part, "wide", mask) for mask, part in zip(masks, (same, other, other))]
        )
    else:
        own = None
        keep, give = prologue(weights, (), width)
        chosen = expert_ids[:, 0]
        onehot = (chosen[:, None] == jnp.arange(expert_count, dtype=jnp.int32)[None, :]).astype(
            jnp.int32
        )
        rank = jnp.sum((jnp.cumsum(onehot, axis=0) - onehot) * onehot, axis=1)
        slot_place = chosen * slots + rank
        source = (
            jnp.full((expert_count * slots,), tok_rows, jnp.int32)
            .at[slot_place]
            .set(jnp.arange(tok_rows, dtype=jnp.int32))
        )
        scaled = (route_prob[:, None] * cotangent.astype(jnp.float32)).astype(jnp.bfloat16)
        both = jnp.stack([tokens, scaled])
        both = lax.dynamic_slice_in_dim(both, place * width, width, 2)
        both = jnp.concatenate([both, jnp.zeros((2, 1, width), jnp.bfloat16)], 1)
        routed = both[:, source].reshape(2, expert_count, slots, width).transpose(1, 0, 2, 3)
        routed = jnp.repeat(routed, 2, axis=0)
        mine = lax.all_to_all(
            routed, "wide", split_axis=0, concat_axis=0, axis_index_groups=groups, tiled=True
        )

    from_x = partner(give, "wide", 1)
    from_z = partner(keep, "wide", 2)
    from_d = partner(from_x, "wide", 2)
    across = partner(mine, "narrow", 2)
    pieces = (mine, partner(mine, "narrow", 1), across, partner(across, "narrow", 1))
    held = gather_parts(own, pieces, (keep, from_x, from_z))
    kept, sent, grad_own, grad_x, grad_z, grad_d = main(*held, from_d)

    got = partner(sent, "narrow", 1)
    got_d = partner(grad_d, "wide", 2)
    grad_x = (grad_x + got_d.astype(jnp.float32)).astype(jnp.bfloat16)
    grad_x, grad_z = lax.optimization_barrier((grad_x, grad_z))
    got_x = partner(grad_x, "wide", 1)
    got_z = partner(grad_z, "wide", 2)

    across = partner((kept[1] + got[1].astype(jnp.float32)).astype(jnp.bfloat16), "narrow", 2)
    result = kept[0] + got[0].astype(jnp.float32) + across.astype(jnp.float32)
    if direct:
        total = result[:, :slots]
        for k, mask in enumerate(masks):
            rows = result[:, (k + 1) * slots : (k + 2) * slots].astype(jnp.bfloat16)
            total = total + partner(rows, "wide", mask).astype(jnp.float32)
    else:
        parts = result.astype(jnp.bfloat16).reshape(2, 2 * expert_count, slots, width)
        back = lax.all_to_all(
            parts, "wide", split_axis=1, concat_axis=1, axis_index_groups=groups, tiled=True
        )
        back = back.reshape(2, expert_count, 2, slots, width).astype(jnp.float32).sum(2)
        total = back.reshape(2, expert_count * slots, width)[:, slot_place]
    ffn = total[0].astype(jnp.bfloat16).astype(jnp.float32)
    tokens_grad = total[1].astype(jnp.bfloat16)
    output = (route_prob[:, None] * ffn).astype(jnp.bfloat16)
    cot_columns = lax.dynamic_slice_in_dim(cotangent, place * width, width, 1)
    prob_grad = lax.psum(jnp.sum(ffn * cot_columns.astype(jnp.float32), axis=1), "narrow")
    gate_grad, up_grad, down_grad = join_grads(grad_own, got_x, got_z)
    return (output, tokens_grad, prob_grad, gate_grad.T, up_grad.T, down_grad.T)


def solution(mesh):
    in_specs = (
        P("wide", None),
        P("wide", None),
        P("wide", None),
        P("wide"),
        P("wide", "narrow"),
        P("wide", "narrow"),
        P("wide", "narrow"),
    )
    out_specs = (
        P("wide", "narrow"),
        P("wide", "narrow"),
        P("wide"),
        P("wide", "narrow"),
        P("wide", "narrow"),
        P("wide", "narrow"),
    )
    return jax.shard_map(shards, mesh=mesh, in_specs=in_specs, out_specs=out_specs, check_vma=False)
```

```python
import functools

import jax
import jax.numpy as jnp
from jax import lax
from jax.experimental import pallas as pl
from jax.experimental.pallas import tpu as pltpu
from jax.sharding import PartitionSpec as P

VMEM = pl.BlockSpec(memory_space=pltpu.VMEM)
HBM = pl.BlockSpec(memory_space=pltpu.HBM)
EXTRA = 16
PARAMS = pltpu.CompilerParams(vmem_limit_bytes=32 * 1024 * 1024)
PROLOGUE_PARAMS = pltpu.CompilerParams(vmem_limit_bytes=61 * 1024 * 1024)


def partner(x, axis, mask):
    return lax.ppermute(x, axis, [(i, i ^ mask) for i in range(lax.axis_size(axis))])


def dot_nn(left, right):
    return lax.dot_general(
        left, right, (((1,), (0,)), ((), ())), preferred_element_type=jnp.float32
    )


def dot_nt(left, right):
    return lax.dot_general(
        left, right, (((1,), (1,)), ((), ())), preferred_element_type=jnp.float32
    )


def at_quarter(index, width):
    return pl.ds(pl.multiple_of(index * width, width), width)


def packet_rows(rows):
    return 2 * rows + EXTRA


def put_pair(ref, first, value):
    count, lanes = value.shape
    high = value.astype(jnp.bfloat16).astype(jnp.float32)
    both = jnp.concatenate([high, value - high], 0)
    both = jnp.concatenate([both, jnp.zeros((EXTRA - 2 * count, lanes), jnp.float32)], 0)
    ref[first : first + EXTRA, :lanes] = both.astype(ref.dtype)


def get_pair(ref, first, count):
    both = ref[first : first + EXTRA, :].astype(jnp.float32)
    return both[:count] + both[count : 2 * count]


def prologue_kernel(routed, gate, up, down, *refs):
    if routed:
        tokens, cotangent, ids, prob, keep, give, own, same, other = refs[:9]
        held, ids_row, prob_row, sems = refs[9:]
        parts = ((tokens, held.at[0]), (cotangent, held.at[1]), (ids, ids_row), (prob, prob_row))
    else:
        keep, give, sems = refs
        parts = ()
    half = keep.shape[1]
    x_bit = lax.axis_index("wide") % 2
    keep_rows = pl.ds(pl.multiple_of(x_bit * half, 16), half)
    give_rows = pl.ds(pl.multiple_of((1 - x_bit) * half, 16), half)
    for i, ref in enumerate((gate, up, down)):
        parts += ((ref.at[keep_rows, :], keep.at[i]), (ref.at[give_rows, :], give.at[i]))
    copies = [pltpu.make_async_copy(src, dst, sems.at[i]) for i, (src, dst) in enumerate(parts)]
    for copy in copies:
        copy.start()
    if routed:
        for copy in copies[:4]:
            copy.wait()
        rows = held.shape[1]
        width = same.shape[2]
        mine = lax.axis_index("wide") // 4
        column = at_quarter(lax.axis_index("narrow"), width)
        chosen = jnp.broadcast_to(ids_row[...], (128, rows)).astype(jnp.float32).T[:, :1]
        weight = jnp.broadcast_to(prob_row[...], (128, rows)).T[:, :1]
        here = jnp.where(chosen == mine.astype(jnp.float32), 1.0, 0.0)
        for i in range(2):
            factor = weight if i else jnp.ones_like(weight)
            own[i] = (held[i].astype(jnp.float32) * (factor * here)).astype(jnp.bfloat16)
            part = held[i, :, column].astype(jnp.float32)
            same[i] = (part * (factor * here)).astype(jnp.bfloat16)
            other[i] = (part * (factor * (1.0 - here))).astype(jnp.bfloat16)
    for copy in copies[len(copies) - 6 :]:
        copy.wait()


def prologue(weights, token_args, width):
    hidden, quarter = weights[0].shape
    half = jax.ShapeDtypeStruct((3, hidden // 2, quarter), jnp.bfloat16)
    outs, scratch = (half, half), []
    if token_args:
        rows, features = token_args[0].shape
        part = jax.ShapeDtypeStruct((2, rows, width), jnp.bfloat16)
        outs += (jax.ShapeDtypeStruct((2, rows, features), jnp.bfloat16), part, part)
        scratch = [
            pltpu.VMEM((2, rows, features), jnp.bfloat16),
            pltpu.VMEM((1, rows), jnp.int32),
            pltpu.VMEM((1, rows), jnp.float32),
        ]
    return pl.pallas_call(
        functools.partial(prologue_kernel, bool(token_args)),
        out_shape=outs,
        in_specs=[HBM] * (3 + len(token_args)),
        out_specs=[HBM] * 2 + [VMEM] * (len(outs) - 2),
        scratch_shapes=scratch + [pltpu.SemaphoreType.DMA((10,))],
        compiler_params=PROLOGUE_PARAMS,
    )(*weights, *token_args)


def gather_kernel(has_own, *refs):
    own = refs[0] if has_own else None
    pieces, weights = refs[has_own : has_own + 4], refs[has_own + 4 : has_own + 7]
    x_all, s_all, w_all, part = refs[has_own + 7 :]
    blocks, _, slots, width = pieces[0].shape
    member = lax.axis_index("wide") % 4
    place = lax.axis_index("narrow")
    for k, ref in enumerate(weights):
        column = at_quarter(member ^ k, width)
        for i in range(3):
            w_all[i, :, column] = ref[i]
    first = 0
    if has_own:
        x_all[:slots, :] = own[0]
        s_all[:slots, :] = own[1]
        first = slots
    for mask, ref in enumerate(pieces):
        column = at_quarter(place ^ mask, width)
        for block in range(blocks):
            rows = slice(first + block * slots, first + (block + 1) * slots)
            x_all[rows, column] = ref[block, 0]
            s_all[rows, column] = ref[block, 1]
    total = x_all.shape[0]
    tile = min(256, total)

    @pl.loop(0, total // tile)
    def _(step):
        rows = pl.ds(pl.multiple_of(step * tile, tile), tile)
        for i in range(3):
            held = s_all if i == 2 else x_all
            sums = None
            for k in range(3):
                column = at_quarter(member ^ k, width)
                term = dot_nt(w_all[i, :, column], held[rows, column])
                sums = term if sums is None else sums + term
            part[i, :, rows] = sums


def gather_parts(own, pieces, weights):
    blocks, _, slots, width = pieces[0].shape
    half = weights[0].shape[1]
    has_own = own is not None
    total = (blocks + has_own) * slots
    features = 4 * width
    return pl.pallas_call(
        functools.partial(gather_kernel, int(has_own)),
        out_shape=(
            jax.ShapeDtypeStruct((total, features), jnp.bfloat16),
            jax.ShapeDtypeStruct((total, features), jnp.bfloat16),
            jax.ShapeDtypeStruct((3, half, features), jnp.bfloat16),
            jax.ShapeDtypeStruct((3, half, total), jnp.float32),
        ),
        in_specs=[VMEM] * (7 + has_own),
        out_specs=[VMEM] * 4,
        compiler_params=PARAMS,
        cost_estimate=pl.CostEstimate(
            flops=6 * 2 * half * 3 * width * total, bytes_accessed=0, transcendentals=0
        ),
    )(*([own] if has_own else []), *pieces, *weights)


def main_kernel(x_all, s_all, w_part, part, last, kept, sent, *refs):
    outs, (grads, w_all) = refs[:4], refs[4:]
    half, width = last.shape[1:]
    member = lax.axis_index("wide") % 4
    place = lax.axis_index("narrow")
    last_column = at_quarter(member ^ 3, width)
    w_all[...] = w_part[...]
    for i in range(3):
        w_all[i, :, last_column] = last[i]
    total = x_all.shape[0]
    tile = min(width, total)
    kept[:, 2 * total :, :] = jnp.zeros_like(kept[:, 2 * total :, :])
    sent[:, 2 * total :, :] = jnp.zeros_like(sent[:, 2 * total :, :])

    routers = []
    for step in range(total // tile):
        rows = slice(step * tile, (step + 1) * tile)
        x_tile, s_tile = x_all[rows, last_column], s_all[rows, last_column]
        gate = part[0, :, rows] + dot_nt(last[0], x_tile)
        up = part[1, :, rows] + dot_nt(last[1], x_tile)
        d_hidden = part[2, :, rows] + dot_nt(last[2], s_tile)
        sigma = jax.nn.sigmoid(gate)
        active = gate * sigma
        hidden = (active * up).astype(jnp.bfloat16)
        d_gate = (d_hidden * up * sigma * (1.0 + gate * (1.0 - sigma))).astype(jnp.bfloat16)
        d_up = (d_hidden * active).astype(jnp.bfloat16)
        grads[0, :, rows] = d_gate
        grads[1, :, rows] = d_up
        grads[2, :, rows] = hidden
        hidden_t, d_gate_t, d_up_t = hidden.T, d_gate.T, d_up.T
        for mask in range(4):
            column = at_quarter(place ^ mask, width)
            out_part = dot_nn(hidden_t, w_all[2, :, column])
            in_part = dot_nn(d_gate_t, w_all[0, :, column]) + dot_nn(d_up_t, w_all[1, :, column])
            target = sent if mask % 2 else kept
            target[mask // 2, rows, :] = out_part.astype(target.dtype)
            lower = slice(total + step * tile, total + (step + 1) * tile)
            target[mask // 2, lower, :] = in_part.astype(target.dtype)
        router = jnp.sum(hidden.astype(jnp.float32) * d_hidden, axis=0, keepdims=True)
        kept[0, 2 * total + step : 2 * total + step + 1, :tile] = router
        routers.append(router)
    put_pair(sent.at[0], 2 * total, jnp.concatenate(routers, 0))

    left = grads[0:2].reshape(2 * half, total)
    for k in (3, 2, 1, 0):
        column = at_quarter(member ^ k, width)
        both = dot_nn(left, x_all[:, column])
        outs[k][0] = both[:half].astype(outs[k].dtype)
        outs[k][1] = both[half:].astype(outs[k].dtype)
        outs[k][2] = dot_nn(grads[2], s_all[:, column]).astype(outs[k].dtype)


def main(x_all, s_all, w_part, part, last):
    total, features = x_all.shape
    _, half, width = last.shape
    return pl.pallas_call(
        main_kernel,
        out_shape=(
            jax.ShapeDtypeStruct((2, packet_rows(total), width), jnp.float32),
            jax.ShapeDtypeStruct((2, packet_rows(total), width), jnp.bfloat16),
        )
        + tuple(
            jax.ShapeDtypeStruct((3, half, width), jnp.bfloat16 if k else jnp.float32)
            for k in range(4)
        ),
        in_specs=[VMEM] * 5,
        out_specs=[VMEM] * 6,
        scratch_shapes=[
            pltpu.VMEM((3, half, total), jnp.bfloat16),
            pltpu.VMEM((3, half, features), jnp.bfloat16),
        ],
        compiler_params=PARAMS,
        cost_estimate=pl.CostEstimate(
            flops=12 * 2 * half * features * total, bytes_accessed=0, transcendentals=0
        ),
    )(x_all, s_all, w_part, part, last)


def join_kernel(own, got_x, got_z, got_d, *outs):
    half = own.shape[1]
    x_bit = lax.axis_index("wide") % 2
    keep_rows = pl.ds(pl.multiple_of(x_bit * half, 16), half)
    give_rows = pl.ds(pl.multiple_of((1 - x_bit) * half, 16), half)
    for i, ref in enumerate(outs):
        ref[keep_rows, :] = own[i] + got_z[i].astype(jnp.float32)
        ref[give_rows, :] = got_x[i].astype(jnp.float32) + got_d[i].astype(jnp.float32)


def join_grads(own, got_x, got_z, got_d):
    _, half, width = own.shape
    shape = jax.ShapeDtypeStruct((2 * half, width), jnp.float32)
    return pl.pallas_call(
        join_kernel,
        out_shape=(shape,) * 3,
        in_specs=[VMEM] * 4,
        out_specs=[VMEM] * 3,
        compiler_params=PARAMS,
    )(own, got_x, got_z, got_d)


def cross_kernel(kept, got, sent):
    total = (kept.shape[1] - EXTRA) // 2
    tile = min(kept.shape[2], total)
    count = total // tile
    body = slice(0, 2 * total)
    sent[body, :] = (kept[1, body, :] + got[1, body, :].astype(jnp.float32)).astype(sent.dtype)
    sent[2 * total :, :] = jnp.zeros_like(sent[2 * total :, :])
    router = kept[0, 2 * total : 2 * total + count, :] + get_pair(got.at[0], 2 * total, count)
    put_pair(sent, 2 * total, router)


def cross_part(kept, got):
    return pl.pallas_call(
        cross_kernel,
        out_shape=jax.ShapeDtypeStruct(got.shape[1:], got.dtype),
        in_specs=[VMEM] * 2,
        out_specs=VMEM,
        compiler_params=PARAMS,
    )(kept, got)


def result_kernel(kept, got, across, *outs):
    total = (kept.shape[1] - EXTRA) // 2
    width = kept.shape[2]
    count = total // min(width, total)
    router = kept[0, 2 * total : 2 * total + count, :] + get_pair(got.at[0], 2 * total, count)
    router = router + get_pair(across, 2 * total, count)
    slots = (outs[0].shape[0] - EXTRA) // 2
    for block, out in enumerate(outs):
        for part in range(2):
            rows = slice(part * total + block * slots, part * total + (block + 1) * slots)
            value = kept[0, rows, :] + got[0, rows, :].astype(jnp.float32)
            value = value + across[rows, :].astype(jnp.float32)
            out[part * slots : (part + 1) * slots, :] = value.astype(out.dtype)
        out[2 * slots :, :] = jnp.zeros_like(out[2 * slots :, :])
        if slots == total:
            out[2 * slots : 2 * slots + count, :] = router
        else:
            lane = block * slots % width
            mine = router[block * slots // width :, lane : lane + slots][:1]
            if block:
                put_pair(out, 2 * slots, mine)
            else:
                out[2 * slots : 2 * slots + 1, :slots] = mine


def result_parts(kept, got, across, blocks):
    total = (kept.shape[1] - EXTRA) // 2
    shape = (packet_rows(total // blocks), kept.shape[2])
    return pl.pallas_call(
        result_kernel,
        out_shape=tuple(
            jax.ShapeDtypeStruct(shape, jnp.bfloat16 if k else jnp.float32) for k in range(blocks)
        ),
        in_specs=[VMEM] * 3,
        out_specs=[VMEM] * blocks,
        compiler_params=PARAMS,
    )(kept, got, across)


def finish_kernel(prob, own, *refs):
    got, (output, tokens_grad, prob_grad) = refs[:-3], refs[-3:]
    slots, width = output.shape
    ffn, grad = own[:slots, :], own[slots : 2 * slots, :]
    router = own[2 * slots : 2 * slots + 1, :]
    for ref in got:
        ffn = ffn + ref[:slots, :].astype(jnp.float32)
        grad = grad + ref[slots : 2 * slots, :].astype(jnp.float32)
        router = router + get_pair(ref, 2 * slots, 1)
    weight = jnp.broadcast_to(prob[...], (128, slots)).T[:, :1]
    output[...] = (ffn.astype(jnp.bfloat16).astype(jnp.float32) * weight).astype(jnp.bfloat16)
    tokens_grad[...] = grad.astype(jnp.bfloat16)
    prob_grad[...] = router[:, :slots] / prob[...]


def finish(prob, own, got):
    slots, width = (own.shape[0] - EXTRA) // 2, own.shape[1]
    part = jax.ShapeDtypeStruct((slots, width), jnp.bfloat16)
    return pl.pallas_call(
        finish_kernel,
        out_shape=(part, part, jax.ShapeDtypeStruct((1, slots), jnp.float32)),
        in_specs=[VMEM] * (2 + len(got)),
        out_specs=[VMEM] * 3,
        compiler_params=PARAMS,
    )(prob, own, *got)


def shards(tokens, cotangent, expert_ids, route_prob, gate_weight, up_weight, down_weight):
    wide_count = lax.axis_size("wide")
    narrow_count = lax.axis_size("narrow")
    expert_count = wide_count // 4
    tok_rows, features = tokens.shape
    width = features // narrow_count
    slots = min(4 * tok_rows // expert_count, tok_rows)
    direct = expert_count == 2 and slots == tok_rows
    place = lax.axis_index("narrow")
    masks = (1, 4, 5)
    groups = [
        [4 * e + 2 * b + a for e in range(expert_count) for a in range(2)] for b in range(2)
    ]

    weights = (gate_weight.T, up_weight.T, down_weight.T)
    if direct:
        keep, give, own, same, other = prologue(
            weights, (tokens, cotangent, expert_ids.T, route_prob[None, :]), width
        )
        mine = jnp.stack(
            [partner(part, "wide", mask) for mask, part in zip(masks, (same, other, other))]
        )
    else:
        own = None
        keep, give = prologue(weights, (), width)
        chosen = expert_ids[:, 0]
        onehot = (chosen[:, None] == jnp.arange(expert_count, dtype=jnp.int32)[None, :]).astype(
            jnp.int32
        )
        rank = jnp.sum((jnp.cumsum(onehot, axis=0) - onehot) * onehot, axis=1)
        slot_place = chosen * slots + rank
        source = (
            jnp.full((expert_count * slots,), tok_rows, jnp.int32)
            .at[slot_place]
            .set(jnp.arange(tok_rows, dtype=jnp.int32))
        )
        scaled = (route_prob[:, None] * cotangent.astype(jnp.float32)).astype(jnp.bfloat16)
        both = jnp.stack([tokens, scaled])
        both = lax.dynamic_slice_in_dim(both, place * width, width, 2)
        both = jnp.concatenate([both, jnp.zeros((2, 1, width), jnp.bfloat16)], 1)
        routed = both[:, source].reshape(2, expert_count, slots, width).transpose(1, 0, 2, 3)
        routed = jnp.repeat(routed, 2, axis=0)
        mine = lax.all_to_all(
            routed, "wide", split_axis=0, concat_axis=0, axis_index_groups=groups, tiled=True
        )

    from_x, from_z = lax.optimization_barrier(
        (partner(give, "wide", 1), partner(keep, "wide", 2))
    )
    from_d = partner(from_x, "wide", 2)
    across = partner(mine, "narrow", 2)
    pieces = (mine, partner(mine, "narrow", 1), across, partner(across, "narrow", 1))
    held = gather_parts(own, pieces, (keep, from_x, from_z))
    kept, sent, grad_own, grad_x, grad_z, grad_d = main(*held, from_d)

    got = partner(sent, "narrow", 1)
    got_x = partner(grad_x, "wide", 1)
    got_z = partner(grad_z, "wide", 2)
    got_d = partner(grad_d, "wide", 3)
    across = partner(cross_part(kept, got), "narrow", 2)
    if direct:
        parts = result_parts(kept, got, across, len(masks) + 1)
        back = [partner(part, "wide", mask) for mask, part in zip(masks, parts[1:])]
        output, tokens_grad, prob_grad = finish(route_prob[None, :], parts[0], back)
        prob_grad = prob_grad[0]
    else:
        (result,) = result_parts(kept, got, across, 1)
        total = (result.shape[0] - EXTRA) // 2
        parts = result[: 2 * total].astype(jnp.bfloat16)
        parts = parts.reshape(2, 2 * expert_count, slots, width)
        back = lax.all_to_all(
            parts, "wide", split_axis=1, concat_axis=1, axis_index_groups=groups, tiled=True
        )
        back = back.reshape(2, expert_count, 2, slots, width).astype(jnp.float32).sum(2)
        back = back.reshape(2, expert_count * slots, width)[:, slot_place]
        router = result[2 * total : 2 * total + total // min(width, total), : min(width, total)]
        router = router.reshape(2 * expert_count, slots)
        high = lax.reduce_precision(router, 8, 7)
        pair = jnp.stack([high, router - high], 1).astype(jnp.bfloat16)
        pair = lax.all_to_all(
            pair, "wide", split_axis=0, concat_axis=0, axis_index_groups=groups, tiled=True
        )
        router = pair.reshape(expert_count, 4, slots).astype(jnp.float32).sum(1)
        prob_grad = router.reshape(expert_count * slots)[slot_place] / route_prob
        ffn = back[0].astype(jnp.bfloat16).astype(jnp.float32)
        output = (route_prob[:, None] * ffn).astype(jnp.bfloat16)
        tokens_grad = back[1].astype(jnp.bfloat16)
    gate_grad, up_grad, down_grad = join_grads(grad_own, got_x, got_z, got_d)
    return (output, tokens_grad, prob_grad, gate_grad.T, up_grad.T, down_grad.T)


def solution(mesh):
    in_specs = (
        P("wide", None),
        P("wide", None),
        P("wide", None),
        P("wide"),
        P("wide", "narrow"),
        P("wide", "narrow"),
        P("wide", "narrow"),
    )
    out_specs = (
        P("wide", "narrow"),
        P("wide", "narrow"),
        P("wide"),
        P("wide", "narrow"),
        P("wide", "narrow"),
        P("wide", "narrow"),
    )
    return jax.shard_map(shards, mesh=mesh, in_specs=in_specs, out_specs=out_specs, check_vma=False)
```

```python
import functools

import jax
import jax.numpy as jnp
from jax import lax
from jax.experimental import pallas as pl
from jax.experimental.pallas import tpu as pltpu
from jax.sharding import PartitionSpec as P

VMEM = pl.BlockSpec(memory_space=pltpu.VMEM)
HBM = pl.BlockSpec(memory_space=pltpu.HBM)
EXTRA = 16
PARAMS = pltpu.CompilerParams(vmem_limit_bytes=32 * 1024 * 1024)


def partner(x, axis, mask):
    return lax.ppermute(x, axis, [(i, i ^ mask) for i in range(lax.axis_size(axis))])


def dot_nn(left, right):
    return lax.dot_general(
        left, right, (((1,), (0,)), ((), ())), preferred_element_type=jnp.float32
    )


def dot_nt(left, right):
    return lax.dot_general(
        left, right, (((1,), (1,)), ((), ())), preferred_element_type=jnp.float32
    )


def at_quarter(index, width):
    return pl.ds(pl.multiple_of(index * width, width), width)


def packet_rows(rows):
    return 2 * rows + EXTRA


def put_pair(ref, first, value):
    count, lanes = value.shape
    high = value.astype(jnp.bfloat16).astype(jnp.float32)
    both = jnp.concatenate([high, value - high], 0)
    both = jnp.concatenate([both, jnp.zeros((EXTRA - 2 * count, lanes), jnp.float32)], 0)
    ref[first : first + EXTRA, :lanes] = both.astype(ref.dtype)


def get_pair(ref, first, count):
    both = ref[first : first + EXTRA, :].astype(jnp.float32)
    return both[:count] + both[count : 2 * count]


def prologue_kernel(routed, gate, up, down, *refs):
    if routed:
        tokens, cotangent, ids, prob, keep, give, own, same, other = refs[:9]
        held, ids_row, prob_row, sems = refs[9:]
        parts = ((tokens, held.at[0]), (cotangent, held.at[1]), (ids, ids_row), (prob, prob_row))
    else:
        keep, give, sems = refs
        parts = ()
    half = keep.shape[1]
    x_bit = lax.axis_index("wide") % 2
    keep_rows = pl.ds(pl.multiple_of(x_bit * half, 16), half)
    give_rows = pl.ds(pl.multiple_of((1 - x_bit) * half, 16), half)
    for i, ref in enumerate((gate, up, down)):
        parts += ((ref.at[keep_rows, :], keep.at[i]), (ref.at[give_rows, :], give.at[i]))
    copies = [pltpu.make_async_copy(src, dst, sems.at[i]) for i, (src, dst) in enumerate(parts)]
    for copy in copies:
        copy.start()
    if routed:
        for copy in copies[:4]:
            copy.wait()
        rows = held.shape[1]
        width = same.shape[2]
        mine = lax.axis_index("wide") // 4
        column = at_quarter(lax.axis_index("narrow"), width)
        chosen = jnp.broadcast_to(ids_row[...], (128, rows)).astype(jnp.float32).T[:, :1]
        weight = jnp.broadcast_to(prob_row[...], (128, rows)).T[:, :1]
        here = jnp.where(chosen == mine.astype(jnp.float32), 1.0, 0.0)
        for i in range(2):
            factor = weight if i else jnp.ones_like(weight)
            own[i] = (held[i].astype(jnp.float32) * (factor * here)).astype(jnp.bfloat16)
            part = held[i, :, column].astype(jnp.float32)
            same[i] = (part * (factor * here)).astype(jnp.bfloat16)
            other[i] = (part * (factor * (1.0 - here))).astype(jnp.bfloat16)
    for copy in copies[len(copies) - 6 :]:
        copy.wait()


def prologue(weights, token_args, width):
    hidden, quarter = weights[0].shape
    half = jax.ShapeDtypeStruct((3, hidden // 2, quarter), jnp.bfloat16)
    outs, scratch = (half, half), []
    if token_args:
        rows, features = token_args[0].shape
        part = jax.ShapeDtypeStruct((2, rows, width), jnp.bfloat16)
        outs += (jax.ShapeDtypeStruct((2, rows, features), jnp.bfloat16), part, part)
        scratch = [
            pltpu.VMEM((2, rows, features), jnp.bfloat16),
            pltpu.VMEM((1, rows), jnp.int32),
            pltpu.VMEM((1, rows), jnp.float32),
        ]
    return pl.pallas_call(
        functools.partial(prologue_kernel, bool(token_args)),
        out_shape=outs,
        in_specs=[HBM] * (3 + len(token_args)),
        out_specs=[VMEM] * len(outs),
        scratch_shapes=scratch + [pltpu.SemaphoreType.DMA((10,))],
        compiler_params=PARAMS,
    )(*[pltpu.with_memory_space_constraint(x, pltpu.HBM) for x in (*weights, *token_args)])


def gather_kernel(has_own, *refs):
    own = refs[0] if has_own else None
    pieces, weights = refs[has_own : has_own + 4], refs[has_own + 4 : has_own + 7]
    x_all, s_all, w_all, part = refs[has_own + 7 :]
    blocks, _, slots, width = pieces[0].shape
    member = lax.axis_index("wide") % 4
    place = lax.axis_index("narrow")
    for k, ref in enumerate(weights):
        column = at_quarter(member ^ k, width)
        for i in range(3):
            w_all[i, :, column] = ref[i]
    first = 0
    if has_own:
        x_all[:slots, :] = own[0]
        s_all[:slots, :] = own[1]
        first = slots
    for mask, ref in enumerate(pieces):
        column = at_quarter(place ^ mask, width)
        for block in range(blocks):
            rows = slice(first + block * slots, first + (block + 1) * slots)
            x_all[rows, column] = ref[block, 0]
            s_all[rows, column] = ref[block, 1]
    total = x_all.shape[0]
    tile = min(256, total)

    @pl.loop(0, total // tile)
    def _(step):
        rows = pl.ds(pl.multiple_of(step * tile, tile), tile)
        for i in range(3):
            held = s_all if i == 2 else x_all
            sums = None
            for k in range(3):
                column = at_quarter(member ^ k, width)
                term = dot_nt(w_all[i, :, column], held[rows, column])
                sums = term if sums is None else sums + term
            part[i, :, rows] = sums


def gather_parts(own, pieces, weights):
    blocks, _, slots, width = pieces[0].shape
    half = weights[0].shape[1]
    has_own = own is not None
    total = (blocks + has_own) * slots
    features = 4 * width
    return pl.pallas_call(
        functools.partial(gather_kernel, int(has_own)),
        out_shape=(
            jax.ShapeDtypeStruct((total, features), jnp.bfloat16),
            jax.ShapeDtypeStruct((total, features), jnp.bfloat16),
            jax.ShapeDtypeStruct((3, half, features), jnp.bfloat16),
            jax.ShapeDtypeStruct((3, half, total), jnp.float32),
        ),
        in_specs=[VMEM] * (7 + has_own),
        out_specs=[VMEM] * 4,
        compiler_params=PARAMS,
        cost_estimate=pl.CostEstimate(flops=1, bytes_accessed=1, transcendentals=0),
    )(*([own] if has_own else []), *pieces, *weights)


def inner_kernel(x_all, s_all, part, last, units, router, *outs):
    half, width = last.shape[1:]
    member = lax.axis_index("wide") % 4
    last_column = at_quarter(member ^ 3, width)
    total = x_all.shape[0]
    tile = min(width, total)
    for step in range(total // tile):
        rows = slice(step * tile, (step + 1) * tile)
        x_tile, s_tile = x_all[rows, last_column], s_all[rows, last_column]
        gate = part[0, :, rows] + dot_nt(last[0], x_tile)
        up = part[1, :, rows] + dot_nt(last[1], x_tile)
        d_hidden = part[2, :, rows] + dot_nt(last[2], s_tile)
        sigma = jax.nn.sigmoid(gate)
        active = gate * sigma
        hidden = (active * up).astype(jnp.bfloat16)
        d_gate = (d_hidden * up * sigma * (1.0 + gate * (1.0 - sigma))).astype(jnp.bfloat16)
        d_up = (d_hidden * active).astype(jnp.bfloat16)
        units[0, :, rows] = d_gate
        units[1, :, rows] = d_up
        units[2, :, rows] = hidden
        router[step : step + 1, :] = jnp.sum(
            hidden.astype(jnp.float32) * d_hidden, axis=0, keepdims=True
        )

    left = units[0:2].reshape(2 * half, total)
    for k in (3, 2, 1, 0):
        column = at_quarter(member ^ k, width)
        both = dot_nn(left, x_all[:, column])
        outs[k][0] = both[:half].astype(outs[k].dtype)
        outs[k][1] = both[half:].astype(outs[k].dtype)
        outs[k][2] = dot_nn(units[2], s_all[:, column]).astype(outs[k].dtype)


def inner(x_all, s_all, part, last):
    total, features = x_all.shape
    _, half, width = last.shape
    tile = min(width, total)
    return pl.pallas_call(
        inner_kernel,
        out_shape=(
            jax.ShapeDtypeStruct((3, half, total), jnp.bfloat16),
            jax.ShapeDtypeStruct((total // tile, tile), jnp.float32),
        )
        + tuple(
            jax.ShapeDtypeStruct((3, half, width), jnp.bfloat16 if k > 1 else jnp.float32)
            for k in range(4)
        ),
        in_specs=[VMEM] * 4,
        out_specs=[VMEM] * 6,
        compiler_params=PARAMS,
        cost_estimate=pl.CostEstimate(
            flops=8 * half * features * total, bytes_accessed=0, transcendentals=0
        ),
    )(x_all, s_all, part, last)


def outer_kernel(units, router, w_part, last, kept, sent, w_all):
    half, width = last.shape[1:]
    place = lax.axis_index("narrow")
    w_all[...] = w_part[...]
    last_column = at_quarter(lax.axis_index("wide") % 4 ^ 3, width)
    for i in range(3):
        w_all[i, :, last_column] = last[i]
    total = units.shape[2]
    count, tile = router.shape
    for ref in (kept, sent):
        ref[:, 2 * total :, :] = jnp.zeros_like(ref[:, 2 * total :, :])
    kept[0, 2 * total : 2 * total + count, :tile] = router[...]
    put_pair(sent.at[0], 2 * total, router[...])
    for step in range(count):
        rows = slice(step * tile, (step + 1) * tile)
        lower = slice(total + step * tile, total + (step + 1) * tile)
        d_gate, d_up, hidden = (units[i, :, rows].T for i in range(3))
        for mask in range(4):
            column = at_quarter(place ^ mask, width)
            target = sent if mask % 2 else kept
            out_part = dot_nn(hidden, w_all[2, :, column])
            in_part = dot_nn(d_gate, w_all[0, :, column]) + dot_nn(d_up, w_all[1, :, column])
            target[mask // 2, rows, :] = out_part.astype(target.dtype)
            target[mask // 2, lower, :] = in_part.astype(target.dtype)


def outer(units, router, w_part, last):
    _, half, total = units.shape
    width = last.shape[2]
    features = w_part.shape[2]
    return pl.pallas_call(
        outer_kernel,
        out_shape=(
            jax.ShapeDtypeStruct((2, packet_rows(total), width), jnp.float32),
            jax.ShapeDtypeStruct((2, packet_rows(total), width), jnp.bfloat16),
        ),
        in_specs=[VMEM] * 4,
        out_specs=[VMEM] * 2,
        scratch_shapes=[pltpu.VMEM((3, half, features), jnp.bfloat16)],
        compiler_params=PARAMS,
        cost_estimate=pl.CostEstimate(
            flops=6 * half * features * total, bytes_accessed=0, transcendentals=0
        ),
    )(units, router, w_part, last)


def join_kernel(own, got_x, got_z, *outs):
    half = own.shape[1]
    x_bit = lax.axis_index("wide") % 2
    keep_rows = pl.ds(pl.multiple_of(x_bit * half, 16), half)
    give_rows = pl.ds(pl.multiple_of((1 - x_bit) * half, 16), half)
    for i, ref in enumerate(outs):
        ref[keep_rows, :] = own[i] + got_z[i].astype(jnp.float32)
        ref[give_rows, :] = got_x[i].astype(jnp.float32)


def join_grads(own, got_x, got_z):
    _, half, width = own.shape
    shape = jax.ShapeDtypeStruct((2 * half, width), jnp.float32)
    return pl.pallas_call(
        join_kernel,
        out_shape=(shape,) * 3,
        in_specs=[VMEM] * 3,
        out_specs=[VMEM] * 3,
        compiler_params=PARAMS,
    )(own, got_x, got_z)


def cross_kernel(kept, got, sent):
    total = (kept.shape[1] - EXTRA) // 2
    tile = min(kept.shape[2], total)
    count = total // tile
    body = slice(0, 2 * total)
    sent[body, :] = (kept[1, body, :] + got[1, body, :].astype(jnp.float32)).astype(sent.dtype)
    sent[2 * total :, :] = jnp.zeros_like(sent[2 * total :, :])
    router = kept[0, 2 * total : 2 * total + count, :] + get_pair(got.at[0], 2 * total, count)
    put_pair(sent, 2 * total, router)


def cross_part(kept, got):
    return pl.pallas_call(
        cross_kernel,
        out_shape=jax.ShapeDtypeStruct(got.shape[1:], got.dtype),
        in_specs=[VMEM] * 2,
        out_specs=VMEM,
        compiler_params=PARAMS,
    )(kept, got)


def result_kernel(kept, got, across, *outs):
    total = (kept.shape[1] - EXTRA) // 2
    width = kept.shape[2]
    count = total // min(width, total)
    router = kept[0, 2 * total : 2 * total + count, :] + get_pair(got.at[0], 2 * total, count)
    router = router + get_pair(across, 2 * total, count)
    slots = (outs[0].shape[0] - EXTRA) // 2
    for block, out in enumerate(outs):
        for part in range(2):
            rows = slice(part * total + block * slots, part * total + (block + 1) * slots)
            value = kept[0, rows, :] + got[0, rows, :].astype(jnp.float32)
            value = value + across[rows, :].astype(jnp.float32)
            out[part * slots : (part + 1) * slots, :] = value.astype(out.dtype)
        out[2 * slots :, :] = jnp.zeros_like(out[2 * slots :, :])
        if slots == total:
            out[2 * slots : 2 * slots + count, :] = router
        else:
            lane = block * slots % width
            mine = router[block * slots // width :, lane : lane + slots][:1]
            if block:
                put_pair(out, 2 * slots, mine)
            else:
                out[2 * slots : 2 * slots + 1, :slots] = mine


def result_parts(kept, got, across, blocks):
    total = (kept.shape[1] - EXTRA) // 2
    shape = (packet_rows(total // blocks), kept.shape[2])
    return pl.pallas_call(
        result_kernel,
        out_shape=tuple(
            jax.ShapeDtypeStruct(shape, jnp.bfloat16 if k else jnp.float32) for k in range(blocks)
        ),
        in_specs=[VMEM] * 3,
        out_specs=[VMEM] * blocks,
        compiler_params=PARAMS,
    )(kept, got, across)


def finish_kernel(prob, own, *refs):
    got, (output, tokens_grad, prob_grad) = refs[:-3], refs[-3:]
    slots, width = output.shape
    ffn, grad = own[:slots, :], own[slots : 2 * slots, :]
    router = own[2 * slots : 2 * slots + 1, :]
    for ref in got:
        ffn = ffn + ref[:slots, :].astype(jnp.float32)
        grad = grad + ref[slots : 2 * slots, :].astype(jnp.float32)
        router = router + get_pair(ref, 2 * slots, 1)
    weight = jnp.broadcast_to(prob[...], (128, slots)).T[:, :1]
    output[...] = (ffn.astype(jnp.bfloat16).astype(jnp.float32) * weight).astype(jnp.bfloat16)
    tokens_grad[...] = grad.astype(jnp.bfloat16)
    prob_grad[...] = router[:, :slots] / prob[...]


def finish(prob, own, got):
    slots, width = (own.shape[0] - EXTRA) // 2, own.shape[1]
    part = jax.ShapeDtypeStruct((slots, width), jnp.bfloat16)
    return pl.pallas_call(
        finish_kernel,
        out_shape=(part, part, jax.ShapeDtypeStruct((1, slots), jnp.float32)),
        in_specs=[VMEM] * (2 + len(got)),
        out_specs=[VMEM] * 3,
        compiler_params=PARAMS,
    )(prob, own, *got)


def shards(tokens, cotangent, expert_ids, route_prob, gate_weight, up_weight, down_weight):
    wide_count = lax.axis_size("wide")
    narrow_count = lax.axis_size("narrow")
    expert_count = wide_count // 4
    tok_rows, features = tokens.shape
    width = features // narrow_count
    slots = min(4 * tok_rows // expert_count, tok_rows)
    direct = expert_count == 2 and slots == tok_rows
    place = lax.axis_index("narrow")
    masks = (1, 4, 5)
    groups = [
        [4 * e + 2 * b + a for e in range(expert_count) for a in range(2)] for b in range(2)
    ]

    weights = (gate_weight.T, up_weight.T, down_weight.T)
    if direct:
        keep, give, own, same, other = prologue(
            weights, (tokens, cotangent, expert_ids.T, route_prob[None, :]), width
        )
        mine = jnp.stack(
            [partner(part, "wide", mask) for mask, part in zip(masks, (same, other, other))]
        )
    else:
        own = None
        keep, give = prologue(weights, (), width)
        chosen = expert_ids[:, 0]
        onehot = (chosen[:, None] == jnp.arange(expert_count, dtype=jnp.int32)[None, :]).astype(
            jnp.int32
        )
        rank = jnp.sum((jnp.cumsum(onehot, axis=0) - onehot) * onehot, axis=1)
        slot_place = chosen * slots + rank
        source = (
            jnp.full((expert_count * slots,), tok_rows, jnp.int32)
            .at[slot_place]
            .set(jnp.arange(tok_rows, dtype=jnp.int32))
        )
        scaled = (route_prob[:, None] * cotangent.astype(jnp.float32)).astype(jnp.bfloat16)
        both = jnp.stack([tokens, scaled])
        both = lax.dynamic_slice_in_dim(both, place * width, width, 2)
        both = jnp.concatenate([both, jnp.zeros((2, 1, width), jnp.bfloat16)], 1)
        routed = both[:, source].reshape(2, expert_count, slots, width).transpose(1, 0, 2, 3)
        routed = jnp.repeat(routed, 2, axis=0)
        mine = lax.all_to_all(
            routed, "wide", split_axis=0, concat_axis=0, axis_index_groups=groups, tiled=True
        )

    mine, from_x, from_z = lax.optimization_barrier(
        (mine, partner(give, "wide", 1), partner(keep, "wide", 2))
    )
    from_d = partner(from_x, "wide", 2)
    across = partner(mine, "narrow", 2)
    pieces = (mine, partner(mine, "narrow", 1), across, partner(across, "narrow", 1))
    x_all, s_all, w_part, part = gather_parts(own, pieces, (keep, from_x, from_z))
    units, router, grad_own, grad_x, grad_z, grad_d = inner(x_all, s_all, part, from_d)
    kept, sent = outer(units, router, w_part, from_d)

    got = partner(sent, "narrow", 1)
    got_d = partner(grad_d, "wide", 2)
    grad_x = (grad_x + got_d.astype(jnp.float32)).astype(jnp.bfloat16)
    grad_x, grad_z = lax.optimization_barrier((grad_x, grad_z))
    got_x = partner(grad_x, "wide", 1)
    got_z = partner(grad_z, "wide", 2)
    across = partner(cross_part(kept, got), "narrow", 2)
    if direct:
        parts = result_parts(kept, got, across, len(masks) + 1)
        back = [partner(part, "wide", mask) for mask, part in zip(masks, parts[1:])]
        output, tokens_grad, prob_grad = finish(route_prob[None, :], parts[0], back)
        prob_grad = prob_grad[0]
    else:
        (result,) = result_parts(kept, got, across, 1)
        total = (result.shape[0] - EXTRA) // 2
        parts = result[: 2 * total].astype(jnp.bfloat16)
        parts = parts.reshape(2, 2 * expert_count, slots, width)
        back = lax.all_to_all(
            parts, "wide", split_axis=1, concat_axis=1, axis_index_groups=groups, tiled=True
        )
        back = back.reshape(2, expert_count, 2, slots, width).astype(jnp.float32).sum(2)
        back = back.reshape(2, expert_count * slots, width)[:, slot_place]
        router = result[2 * total : 2 * total + total // min(width, total), : min(width, total)]
        router = router.reshape(2 * expert_count, slots)
        high = lax.reduce_precision(router, 8, 7)
        pair = jnp.stack([high, router - high], 1).astype(jnp.bfloat16)
        pair = lax.all_to_all(
            pair, "wide", split_axis=0, concat_axis=0, axis_index_groups=groups, tiled=True
        )
        router = pair.reshape(expert_count, 4, slots).astype(jnp.float32).sum(1)
        prob_grad = router.reshape(expert_count * slots)[slot_place] / route_prob
        ffn = back[0].astype(jnp.bfloat16).astype(jnp.float32)
        output = (route_prob[:, None] * ffn).astype(jnp.bfloat16)
        tokens_grad = back[1].astype(jnp.bfloat16)
    gate_grad, up_grad, down_grad = join_grads(grad_own, got_x, got_z)
    return (output, tokens_grad, prob_grad, gate_grad.T, up_grad.T, down_grad.T)


def solution(mesh):
    in_specs = (
        P("wide", None),
        P("wide", None),
        P("wide", None),
        P("wide"),
        P("wide", "narrow"),
        P("wide", "narrow"),
        P("wide", "narrow"),
    )
    out_specs = (
        P("wide", "narrow"),
        P("wide", "narrow"),
        P("wide"),
        P("wide", "narrow"),
        P("wide", "narrow"),
        P("wide", "narrow"),
    )
    return jax.shard_map(shards, mesh=mesh, in_specs=in_specs, out_specs=out_specs, check_vma=False)
```

```python
import functools

import jax
import jax.numpy as jnp
from jax import lax
from jax.experimental import pallas as pl
from jax.experimental.pallas import tpu as pltpu
from jax.sharding import PartitionSpec as P

VMEM = pl.BlockSpec(memory_space=pltpu.VMEM)
HBM = pl.BlockSpec(memory_space=pltpu.HBM)
EXTRA = 16
PARAMS = pltpu.CompilerParams(vmem_limit_bytes=32 * 1024 * 1024)


def partner(x, axis, mask):
    return lax.ppermute(x, axis, [(i, i ^ mask) for i in range(lax.axis_size(axis))])


def dot_nn(left, right):
    return lax.dot_general(
        left, right, (((1,), (0,)), ((), ())), preferred_element_type=jnp.float32
    )


def dot_nt(left, right):
    return lax.dot_general(
        left, right, (((1,), (1,)), ((), ())), preferred_element_type=jnp.float32
    )


def at_quarter(index, width):
    return pl.ds(pl.multiple_of(index * width, width), width)


def packet_rows(rows):
    return 2 * rows + EXTRA


def put_pair(ref, first, value):
    count, lanes = value.shape
    high = value.astype(jnp.bfloat16).astype(jnp.float32)
    both = jnp.concatenate([high, value - high], 0)
    both = jnp.concatenate([both, jnp.zeros((EXTRA - 2 * count, lanes), jnp.float32)], 0)
    ref[first : first + EXTRA, :lanes] = both.astype(ref.dtype)


def get_pair(ref, first, count):
    both = ref[first : first + EXTRA, :].astype(jnp.float32)
    return both[:count] + both[count : 2 * count]


def prologue_kernel(routed, gate, up, down, *refs):
    if routed:
        tokens, cotangent, ids, prob, keep, give, own, same, other = refs[:9]
        held, ids_row, prob_row, sems = refs[9:]
        parts = ((tokens, held.at[0]), (cotangent, held.at[1]), (ids, ids_row), (prob, prob_row))
    else:
        keep, give, sems = refs
        parts = ()
    half = keep.shape[1]
    x_bit = lax.axis_index("wide") % 2
    keep_rows = pl.ds(pl.multiple_of(x_bit * half, 16), half)
    give_rows = pl.ds(pl.multiple_of((1 - x_bit) * half, 16), half)
    for i, ref in enumerate((gate, up, down)):
        parts += ((ref.at[keep_rows, :], keep.at[i]), (ref.at[give_rows, :], give.at[i]))
    copies = [pltpu.make_async_copy(src, dst, sems.at[i]) for i, (src, dst) in enumerate(parts)]
    for copy in copies:
        copy.start()
    if routed:
        for copy in copies[:4]:
            copy.wait()
        rows = held.shape[1]
        width = same.shape[2]
        mine = lax.axis_index("wide") // 4
        column = at_quarter(lax.axis_index("narrow"), width)
        chosen = jnp.broadcast_to(ids_row[...], (128, rows)).astype(jnp.float32).T[:, :1]
        weight = jnp.broadcast_to(prob_row[...], (128, rows)).T[:, :1]
        here = jnp.where(chosen == mine.astype(jnp.float32), 1.0, 0.0)
        for i in range(2):
            factor = weight if i else jnp.ones_like(weight)
            own[i] = (held[i].astype(jnp.float32) * (factor * here)).astype(jnp.bfloat16)
            part = held[i, :, column].astype(jnp.float32)
            same[i] = (part * (factor * here)).astype(jnp.bfloat16)
            other[i] = (part * (factor * (1.0 - here))).astype(jnp.bfloat16)
    for copy in copies[len(copies) - 6 :]:
        copy.wait()


def prologue(weights, token_args, width):
    hidden, quarter = weights[0].shape
    half = jax.ShapeDtypeStruct((3, hidden // 2, quarter), jnp.bfloat16)
    outs, scratch = (half, half), []
    if token_args:
        rows, features = token_args[0].shape
        part = jax.ShapeDtypeStruct((2, rows, width), jnp.bfloat16)
        outs += (jax.ShapeDtypeStruct((2, rows, features), jnp.bfloat16), part, part)
        scratch = [
            pltpu.VMEM((2, rows, features), jnp.bfloat16),
            pltpu.VMEM((1, rows), jnp.int32),
            pltpu.VMEM((1, rows), jnp.float32),
        ]
    return pl.pallas_call(
        functools.partial(prologue_kernel, bool(token_args)),
        out_shape=outs,
        in_specs=[HBM] * (3 + len(token_args)),
        out_specs=[VMEM] * len(outs),
        scratch_shapes=scratch + [pltpu.SemaphoreType.DMA((10,))],
        compiler_params=PARAMS,
    )(*[pltpu.with_memory_space_constraint(x, pltpu.HBM) for x in (*weights, *token_args)])


def gather_kernel(has_own, *refs):
    own = refs[0] if has_own else None
    pieces, weights = refs[has_own : has_own + 4], refs[has_own + 4 : has_own + 7]
    x_all, s_all, w_all, part = refs[has_own + 7 :]
    blocks, _, slots, width = pieces[0].shape
    member = lax.axis_index("wide") % 4
    place = lax.axis_index("narrow")
    for k, ref in enumerate(weights):
        column = at_quarter(member ^ k, width)
        for i in range(3):
            w_all[i, :, column] = ref[i]
    first = 0
    if has_own:
        x_all[:slots, :] = own[0]
        s_all[:slots, :] = own[1]
        first = slots
    for mask, ref in enumerate(pieces):
        column = at_quarter(place ^ mask, width)
        for block in range(blocks):
            rows = slice(first + block * slots, first + (block + 1) * slots)
            x_all[rows, column] = ref[block, 0]
            s_all[rows, column] = ref[block, 1]
    total = x_all.shape[0]
    tile = min(256, total)

    @pl.loop(0, total // tile)
    def _(step):
        rows = pl.ds(pl.multiple_of(step * tile, tile), tile)
        for i in range(3):
            held = s_all if i == 2 else x_all
            sums = None
            for k in range(3):
                column = at_quarter(member ^ k, width)
                term = dot_nt(w_all[i, :, column], held[rows, column])
                sums = term if sums is None else sums + term
            part[i, :, rows] = sums


def gather_parts(own, pieces, weights):
    blocks, _, slots, width = pieces[0].shape
    half = weights[0].shape[1]
    has_own = own is not None
    total = (blocks + has_own) * slots
    features = 4 * width
    return pl.pallas_call(
        functools.partial(gather_kernel, int(has_own)),
        out_shape=(
            jax.ShapeDtypeStruct((total, features), jnp.bfloat16),
            jax.ShapeDtypeStruct((total, features), jnp.bfloat16),
            jax.ShapeDtypeStruct((3, half, features), jnp.bfloat16),
            jax.ShapeDtypeStruct((3, half, total), jnp.float32),
        ),
        in_specs=[VMEM] * (7 + has_own),
        out_specs=[VMEM] * 4,
        compiler_params=PARAMS,
        cost_estimate=pl.CostEstimate(flops=1, bytes_accessed=1, transcendentals=0),
    )(*([own] if has_own else []), *pieces, *weights)


def outer_kernel(x_all, s_all, w_part, part, last, units, kept, sent, w_all):
    width = last.shape[2]
    place = lax.axis_index("narrow")
    last_column = at_quarter(lax.axis_index("wide") % 4 ^ 3, width)
    w_all[...] = w_part[...]
    for i in range(3):
        w_all[i, :, last_column] = last[i]
    total = x_all.shape[0]
    tile = min(width, total)
    for ref in (kept, sent):
        ref[:, 2 * total :, :] = jnp.zeros_like(ref[:, 2 * total :, :])
    routers = []
    for step in range(total // tile):
        rows = slice(step * tile, (step + 1) * tile)
        lower = slice(total + step * tile, total + (step + 1) * tile)
        x_tile, s_tile = x_all[rows, last_column], s_all[rows, last_column]
        gate = part[0, :, rows] + dot_nt(last[0], x_tile)
        up = part[1, :, rows] + dot_nt(last[1], x_tile)
        d_hidden = part[2, :, rows] + dot_nt(last[2], s_tile)
        sigma = jax.nn.sigmoid(gate)
        active = gate * sigma
        hidden = (active * up).astype(jnp.bfloat16)
        d_gate = (d_hidden * up * sigma * (1.0 + gate * (1.0 - sigma))).astype(jnp.bfloat16)
        d_up = (d_hidden * active).astype(jnp.bfloat16)
        units[0, :, rows] = d_gate
        units[1, :, rows] = d_up
        units[2, :, rows] = hidden
        router = jnp.sum(hidden.astype(jnp.float32) * d_hidden, axis=0, keepdims=True)
        kept[0, 2 * total + step : 2 * total + step + 1, :tile] = router
        routers.append(router)
        hidden_t, d_gate_t, d_up_t = hidden.T, d_gate.T, d_up.T
        for mask in range(4):
            column = at_quarter(place ^ mask, width)
            target = sent if mask % 2 else kept
            out_part = dot_nn(hidden_t, w_all[2, :, column])
            in_part = dot_nn(d_gate_t, w_all[0, :, column]) + dot_nn(d_up_t, w_all[1, :, column])
            target[mask // 2, rows, :] = out_part.astype(target.dtype)
            target[mask // 2, lower, :] = in_part.astype(target.dtype)
    put_pair(sent.at[0], 2 * total, jnp.concatenate(routers, 0))


def outer(x_all, s_all, w_part, part, last):
    total, features = x_all.shape
    _, half, width = last.shape
    return pl.pallas_call(
        outer_kernel,
        out_shape=(
            jax.ShapeDtypeStruct((3, half, total), jnp.bfloat16),
            jax.ShapeDtypeStruct((2, packet_rows(total), width), jnp.float32),
            jax.ShapeDtypeStruct((2, packet_rows(total), width), jnp.bfloat16),
        ),
        in_specs=[VMEM] * 5,
        out_specs=[VMEM] * 3,
        scratch_shapes=[pltpu.VMEM((3, half, features), jnp.bfloat16)],
        compiler_params=PARAMS,
        cost_estimate=pl.CostEstimate(
            flops=8 * half * features * total, bytes_accessed=0, transcendentals=0
        ),
    )(x_all, s_all, w_part, part, last)


def grads_kernel(units, x_all, s_all, *outs):
    half, total = units.shape[1:]
    width = outs[0].shape[2]
    member = lax.axis_index("wide") % 4
    left = units[0:2].reshape(2 * half, total)
    for k in (3, 2, 1, 0):
        column = at_quarter(member ^ k, width)
        both = dot_nn(left, x_all[:, column])
        outs[k][0] = both[:half].astype(outs[k].dtype)
        outs[k][1] = both[half:].astype(outs[k].dtype)
        outs[k][2] = dot_nn(units[2], s_all[:, column]).astype(outs[k].dtype)


def weight_grads(units, x_all, s_all):
    half, total = units.shape[1:]
    features = x_all.shape[1]
    return pl.pallas_call(
        grads_kernel,
        out_shape=tuple(
            jax.ShapeDtypeStruct((3, half, features // 4), jnp.bfloat16 if k > 1 else jnp.float32)
            for k in range(4)
        ),
        in_specs=[VMEM] * 3,
        out_specs=[VMEM] * 4,
        compiler_params=PARAMS,
        cost_estimate=pl.CostEstimate(
            flops=6 * half * features * total, bytes_accessed=0, transcendentals=0
        ),
    )(units, x_all, s_all)


def join_kernel(own, got_x, got_z, *outs):
    half = own.shape[1]
    x_bit = lax.axis_index("wide") % 2
    keep_rows = pl.ds(pl.multiple_of(x_bit * half, 16), half)
    give_rows = pl.ds(pl.multiple_of((1 - x_bit) * half, 16), half)
    for i, ref in enumerate(outs):
        ref[keep_rows, :] = own[i] + got_z[i].astype(jnp.float32)
        ref[give_rows, :] = got_x[i].astype(jnp.float32)


def join_grads(own, got_x, got_z):
    _, half, width = own.shape
    shape = jax.ShapeDtypeStruct((2 * half, width), jnp.float32)
    return pl.pallas_call(
        join_kernel,
        out_shape=(shape,) * 3,
        in_specs=[VMEM] * 3,
        out_specs=[VMEM] * 3,
        compiler_params=PARAMS,
    )(own, got_x, got_z)


def cross_kernel(kept, got, sent):
    total = (kept.shape[1] - EXTRA) // 2
    tile = min(kept.shape[2], total)
    count = total // tile
    body = slice(0, 2 * total)
    sent[body, :] = (kept[1, body, :] + got[1, body, :].astype(jnp.float32)).astype(sent.dtype)
    sent[2 * total :, :] = jnp.zeros_like(sent[2 * total :, :])
    router = kept[0, 2 * total : 2 * total + count, :] + get_pair(got.at[0], 2 * total, count)
    put_pair(sent, 2 * total, router)


def cross_part(kept, got):
    return pl.pallas_call(
        cross_kernel,
        out_shape=jax.ShapeDtypeStruct(got.shape[1:], got.dtype),
        in_specs=[VMEM] * 2,
        out_specs=VMEM,
        compiler_params=PARAMS,
    )(kept, got)


def result_kernel(kept, got, across, out):
    total = (kept.shape[1] - EXTRA) // 2
    count = total // min(kept.shape[2], total)
    body, tail = slice(0, 2 * total), slice(2 * total, 2 * total + count)
    value = kept[0, body, :] + got[0, body, :].astype(jnp.float32)
    out[body, :] = value + across[body, :].astype(jnp.float32)
    out[2 * total :, :] = jnp.zeros_like(out[2 * total :, :])
    router = kept[0, tail, :] + get_pair(got.at[0], 2 * total, count)
    out[tail, :] = router + get_pair(across, 2 * total, count)


def result_parts(kept, got, across):
    return pl.pallas_call(
        result_kernel,
        out_shape=jax.ShapeDtypeStruct(kept.shape[1:], jnp.float32),
        in_specs=[VMEM] * 3,
        out_specs=VMEM,
        compiler_params=PARAMS,
    )(kept, got, across)


def first_kernel(kept, got, to_y, to_x):
    total = (kept.shape[1] - EXTRA) // 2
    slots = total // 4
    count = total // min(kept.shape[2], total)
    body = slice(0, total)
    to_y[body, :] = (kept[1, body, :] + got[1, body, :].astype(jnp.float32)).astype(to_y.dtype)
    put_pair(
        to_y,
        total,
        kept[0, 2 * total : 2 * total + count, :] + get_pair(got.at[0], 2 * total, count),
    )
    for part in range(2):
        for block in range(2):
            rows = slice(total + (2 * block + 1) * slots, total + (2 * block + 2) * slots)
            value = kept[part, rows, :] + got[part, rows, :].astype(jnp.float32)
            to_x[part, block * slots : (block + 1) * slots, :] = value.astype(to_x.dtype)


def first_parts(kept, got):
    total, width = (kept.shape[1] - EXTRA) // 2, kept.shape[2]
    return pl.pallas_call(
        first_kernel,
        out_shape=(
            jax.ShapeDtypeStruct((total + EXTRA, width), jnp.bfloat16),
            jax.ShapeDtypeStruct((2, total // 2, width), jnp.bfloat16),
        ),
        in_specs=[VMEM] * 2,
        out_specs=[VMEM] * 2,
        compiler_params=PARAMS,
    )(kept, got)


def ffn_kernel(kept, got, from_y, held, to_x):
    total = (kept.shape[1] - EXTRA) // 2
    slots, width = total // 4, kept.shape[2]
    count = total // min(width, total)
    router = kept[0, 2 * total : 2 * total + count, :] + get_pair(got.at[0], 2 * total, count)
    router = router + get_pair(from_y, total, count)
    pairs = []
    for block in range(4):
        rows = slice(block * slots, (block + 1) * slots)
        value = kept[0, rows, :] + got[0, rows, :].astype(jnp.float32)
        value = value + from_y[rows, :].astype(jnp.float32)
        out = to_x if block % 2 else held
        place = block // 2
        out[place * slots : (place + 1) * slots, :] = value.astype(out.dtype)
        lane = block * slots % width
        pairs.append(router[block * slots // width :, lane : lane + slots][:1])
    held[2 * slots :, :] = jnp.zeros_like(held[2 * slots :, :])
    to_x[2 * slots :, :] = jnp.zeros_like(to_x[2 * slots :, :])
    held[2 * slots : 2 * slots + 1, :slots] = pairs[0]
    held[2 * slots + 1 : 2 * slots + 2, :slots] = pairs[2]
    put_pair(to_x, 2 * slots, jnp.concatenate([pairs[1], pairs[3]], 0))


def ffn_parts(kept, got, from_y):
    total, width = (kept.shape[1] - EXTRA) // 2, kept.shape[2]
    shape = (total // 2 + EXTRA, width)
    return pl.pallas_call(
        ffn_kernel,
        out_shape=(
            jax.ShapeDtypeStruct(shape, jnp.float32),
            jax.ShapeDtypeStruct(shape, jnp.bfloat16),
        ),
        in_specs=[VMEM] * 3,
        out_specs=[VMEM] * 2,
        compiler_params=PARAMS,
    )(kept, got, from_y)


def input_kernel(kept, got, from_x, held, to_y):
    total = (kept.shape[1] - EXTRA) // 2
    slots = total // 4
    for part, out in enumerate((held, to_y)):
        for block in range(2):
            rows = slice(total + 2 * block * slots, total + (2 * block + 1) * slots)
            here = slice(block * slots, (block + 1) * slots)
            value = kept[part, rows, :] + got[part, rows, :].astype(jnp.float32)
            out[here, :] = (value + from_x[part, here, :].astype(jnp.float32)).astype(out.dtype)


def input_parts(kept, got, from_x):
    shape = from_x.shape[1:]
    return pl.pallas_call(
        input_kernel,
        out_shape=(
            jax.ShapeDtypeStruct(shape, jnp.float32),
            jax.ShapeDtypeStruct(shape, jnp.bfloat16),
        ),
        in_specs=[VMEM] * 3,
        out_specs=[VMEM] * 2,
        compiler_params=PARAMS,
    )(kept, got, from_x)


def last_kernel(ffn, from_x, grad, from_y, held, to_z):
    slots = grad.shape[0] // 2
    router = ffn[2 * slots : 2 * slots + 2, :] + get_pair(from_x, 2 * slots, 2)
    for block, out in enumerate((held, to_z)):
        rows = slice(block * slots, (block + 1) * slots)
        out[:slots, :] = (ffn[rows, :] + from_x[rows, :].astype(jnp.float32)).astype(out.dtype)
        out[slots : 2 * slots, :] = (grad[rows, :] + from_y[rows, :].astype(jnp.float32)).astype(
            out.dtype
        )
    held[2 * slots :, :] = jnp.broadcast_to(router[:1], (EXTRA, router.shape[1]))
    put_pair(to_z, 2 * slots, router[1:])


def last_parts(ffn, from_x, grad, from_y):
    return pl.pallas_call(
        last_kernel,
        out_shape=(
            jax.ShapeDtypeStruct(ffn.shape, jnp.float32),
            jax.ShapeDtypeStruct(ffn.shape, jnp.bfloat16),
        ),
        in_specs=[VMEM] * 4,
        out_specs=[VMEM] * 2,
        compiler_params=PARAMS,
        cost_estimate=pl.CostEstimate(flops=10**10, bytes_accessed=0, transcendentals=0),
    )(ffn, from_x, grad, from_y)


def finish_kernel(prob, own, *refs):
    got, (output, tokens_grad, prob_grad) = refs[:-3], refs[-3:]
    slots, width = output.shape
    ffn, grad = own[:slots, :], own[slots : 2 * slots, :]
    router = own[2 * slots : 2 * slots + 1, :]
    for ref in got:
        ffn = ffn + ref[:slots, :].astype(jnp.float32)
        grad = grad + ref[slots : 2 * slots, :].astype(jnp.float32)
        router = router + get_pair(ref, 2 * slots, 1)
    weight = jnp.broadcast_to(prob[...], (128, slots)).T[:, :1]
    output[...] = (ffn.astype(jnp.bfloat16).astype(jnp.float32) * weight).astype(jnp.bfloat16)
    tokens_grad[...] = grad.astype(jnp.bfloat16)
    prob_grad[...] = router[:, :slots] / prob[...]


def finish(prob, own, got):
    slots, width = (own.shape[0] - EXTRA) // 2, own.shape[1]
    part = jax.ShapeDtypeStruct((slots, width), jnp.bfloat16)
    return pl.pallas_call(
        finish_kernel,
        out_shape=(part, part, jax.ShapeDtypeStruct((1, slots), jnp.float32)),
        in_specs=[VMEM] * (2 + len(got)),
        out_specs=[VMEM] * 3,
        compiler_params=PARAMS,
    )(prob, own, *got)


def shards(tokens, cotangent, expert_ids, route_prob, gate_weight, up_weight, down_weight):
    wide_count = lax.axis_size("wide")
    narrow_count = lax.axis_size("narrow")
    expert_count = wide_count // 4
    tok_rows, features = tokens.shape
    width = features // narrow_count
    slots = min(4 * tok_rows // expert_count, tok_rows)
    direct = expert_count == 2 and slots == tok_rows
    place = lax.axis_index("narrow")
    masks = (1, 4, 5)
    groups = [
        [4 * e + 2 * b + a for e in range(expert_count) for a in range(2)] for b in range(2)
    ]

    weights = (gate_weight.T, up_weight.T, down_weight.T)
    if direct:
        keep, give, own, same, other = prologue(
            weights, (tokens, cotangent, expert_ids.T, route_prob[None, :]), width
        )
        mine = jnp.stack(
            [partner(part, "wide", mask) for mask, part in zip(masks, (same, other, other))]
        )
    else:
        own = None
        keep, give = prologue(weights, (), width)
        chosen = expert_ids[:, 0]
        onehot = (chosen[:, None] == jnp.arange(expert_count, dtype=jnp.int32)[None, :]).astype(
            jnp.int32
        )
        rank = jnp.sum((jnp.cumsum(onehot, axis=0) - onehot) * onehot, axis=1)
        slot_place = chosen * slots + rank
        source = (
            jnp.full((expert_count * slots,), tok_rows, jnp.int32)
            .at[slot_place]
            .set(jnp.arange(tok_rows, dtype=jnp.int32))
        )
        scaled = (route_prob[:, None] * cotangent.astype(jnp.float32)).astype(jnp.bfloat16)
        both = jnp.stack([tokens, scaled])
        both = lax.dynamic_slice_in_dim(both, place * width, width, 2)
        both = jnp.concatenate([both, jnp.zeros((2, 1, width), jnp.bfloat16)], 1)
        routed = both[:, source].reshape(2, expert_count, slots, width).transpose(1, 0, 2, 3)
        routed = jnp.repeat(routed, 2, axis=0)
        mine = lax.all_to_all(
            routed, "wide", split_axis=0, concat_axis=0, axis_index_groups=groups, tiled=True
        )

    mine, from_x, from_z = lax.optimization_barrier(
        (mine, partner(give, "wide", 1), partner(keep, "wide", 2))
    )
    from_d = partner(from_x, "wide", 2)
    across = partner(mine, "narrow", 2)
    pieces = (mine, partner(mine, "narrow", 1), across, partner(across, "narrow", 1))
    x_all, s_all, w_part, part = gather_parts(own, pieces, (keep, from_x, from_z))
    units, kept, sent = outer(x_all, s_all, w_part, part, from_d)
    got = partner(sent, "narrow", 1)
    grad_own, grad_x, grad_z, grad_d = weight_grads(units, x_all, s_all)
    got_d = partner(grad_d, "wide", 2)
    if direct:
        to_y, to_x = first_parts(kept, got)
        ffn_held, ffn_x = ffn_parts(kept, got, partner(to_y, "narrow", 2))
        grad_held, grad_y = input_parts(kept, got, partner(to_x, "wide", 1))
        grad_x, _, _ = lax.optimization_barrier((grad_x, ffn_x, grad_y))
        held, to_z = last_parts(
            ffn_held, partner(ffn_x, "wide", 1), grad_held, partner(grad_y, "narrow", 2)
        )
        output, tokens_grad, prob_grad = finish(
            route_prob[None, :], held, [partner(to_z, "wide", 4)]
        )
        prob_grad = prob_grad[0]
    else:
        across = partner(cross_part(kept, got), "narrow", 2)
        result = result_parts(kept, got, across)
        total = (result.shape[0] - EXTRA) // 2
        parts = result[: 2 * total].astype(jnp.bfloat16)
        parts = parts.reshape(2, 2 * expert_count, slots, width)
        back = lax.all_to_all(
            parts, "wide", split_axis=1, concat_axis=1, axis_index_groups=groups, tiled=True
        )
        back = back.reshape(2, expert_count, 2, slots, width).astype(jnp.float32).sum(2)
        back = back.reshape(2, expert_count * slots, width)[:, slot_place]
        router = result[2 * total : 2 * total + total // min(width, total), : min(width, total)]
        router = router.reshape(2 * expert_count, slots)
        high = lax.reduce_precision(router, 8, 7)
        pair = jnp.stack([high, router - high], 1).astype(jnp.bfloat16)
        pair = lax.all_to_all(
            pair, "wide", split_axis=0, concat_axis=0, axis_index_groups=groups, tiled=True
        )
        router = pair.reshape(expert_count, 4, slots).astype(jnp.float32).sum(1)
        prob_grad = router.reshape(expert_count * slots)[slot_place] / route_prob
        ffn = back[0].astype(jnp.bfloat16).astype(jnp.float32)
        output = (route_prob[:, None] * ffn).astype(jnp.bfloat16)
        tokens_grad = back[1].astype(jnp.bfloat16)
    grad_x = (grad_x + got_d.astype(jnp.float32)).astype(jnp.bfloat16)
    grad_x, grad_z = lax.optimization_barrier((grad_x, grad_z))
    got_x = partner(grad_x, "wide", 1)
    got_z = partner(grad_z, "wide", 2)
    gate_grad, up_grad, down_grad = join_grads(grad_own, got_x, got_z)
    return (output, tokens_grad, prob_grad, gate_grad.T, up_grad.T, down_grad.T)


def solution(mesh):
    in_specs = (
        P("wide", None),
        P("wide", None),
        P("wide", None),
        P("wide"),
        P("wide", "narrow"),
        P("wide", "narrow"),
        P("wide", "narrow"),
    )
    out_specs = (
        P("wide", "narrow"),
        P("wide", "narrow"),
        P("wide"),
        P("wide", "narrow"),
        P("wide", "narrow"),
        P("wide", "narrow"),
    )
    return jax.shard_map(shards, mesh=mesh, in_specs=in_specs, out_specs=out_specs, check_vma=False)
```

```python
import functools

import jax
import jax.numpy as jnp
from jax import lax
from jax.experimental import pallas as pl
from jax.experimental.pallas import tpu as pltpu
from jax.sharding import PartitionSpec as P

VMEM = pl.BlockSpec(memory_space=pltpu.VMEM)
HBM = pl.BlockSpec(memory_space=pltpu.HBM)
EXTRA = 16
PARAMS = pltpu.CompilerParams(vmem_limit_bytes=32 * 1024 * 1024)


def partner(x, axis, mask):
    return lax.ppermute(x, axis, [(i, i ^ mask) for i in range(lax.axis_size(axis))])


def dot_nn(left, right):
    return lax.dot_general(
        left, right, (((1,), (0,)), ((), ())), preferred_element_type=jnp.float32
    )


def dot_nt(left, right):
    return lax.dot_general(
        left, right, (((1,), (1,)), ((), ())), preferred_element_type=jnp.float32
    )


def at_quarter(index, width):
    return pl.ds(pl.multiple_of(index * width, width), width)


def packet_rows(rows):
    return 2 * rows + EXTRA


def put_pair(ref, first, value):
    count, lanes = value.shape
    high = value.astype(jnp.bfloat16).astype(jnp.float32)
    both = jnp.concatenate([high, value - high], 0)
    both = jnp.concatenate([both, jnp.zeros((EXTRA - 2 * count, lanes), jnp.float32)], 0)
    ref[first : first + EXTRA, :lanes] = both.astype(ref.dtype)


def get_pair(ref, first, count):
    both = ref[first : first + EXTRA, :].astype(jnp.float32)
    return both[:count] + both[count : 2 * count]


def prologue_kernel(routed, gate, up, down, *refs):
    if routed:
        tokens, cotangent, ids, prob, keep, give, own, same, other = refs[:9]
        held, ids_row, prob_row, sems = refs[9:]
        parts = ((tokens, held.at[0]), (cotangent, held.at[1]), (ids, ids_row), (prob, prob_row))
    else:
        keep, give, sems = refs
        parts = ()
    half = keep.shape[1]
    x_bit = lax.axis_index("wide") % 2
    keep_rows = pl.ds(pl.multiple_of(x_bit * half, 16), half)
    give_rows = pl.ds(pl.multiple_of((1 - x_bit) * half, 16), half)
    for i, ref in enumerate((gate, up, down)):
        parts += ((ref.at[keep_rows, :], keep.at[i]), (ref.at[give_rows, :], give.at[i]))
    copies = [pltpu.make_async_copy(src, dst, sems.at[i]) for i, (src, dst) in enumerate(parts)]
    for copy in copies:
        copy.start()
    if routed:
        for copy in copies[:4]:
            copy.wait()
        rows = held.shape[1]
        width = same.shape[2]
        mine = lax.axis_index("wide") // 4
        column = at_quarter(lax.axis_index("narrow"), width)
        chosen = jnp.broadcast_to(ids_row[...], (128, rows)).astype(jnp.float32).T[:, :1]
        weight = jnp.broadcast_to(prob_row[...], (128, rows)).T[:, :1]
        here = jnp.where(chosen == mine.astype(jnp.float32), 1.0, 0.0)
        for i in range(2):
            factor = weight if i else jnp.ones_like(weight)
            own[i] = (held[i].astype(jnp.float32) * (factor * here)).astype(jnp.bfloat16)
            part = held[i, :, column].astype(jnp.float32)
            same[i] = (part * (factor * here)).astype(jnp.bfloat16)
            other[i] = (part * (factor * (1.0 - here))).astype(jnp.bfloat16)
    for copy in copies[len(copies) - 6 :]:
        copy.wait()


def prologue(weights, token_args, width):
    hidden, quarter = weights[0].shape
    half = jax.ShapeDtypeStruct((3, hidden // 2, quarter), jnp.bfloat16)
    outs, scratch = (half, half), []
    if token_args:
        rows, features = token_args[0].shape
        part = jax.ShapeDtypeStruct((2, rows, width), jnp.bfloat16)
        outs += (jax.ShapeDtypeStruct((2, rows, features), jnp.bfloat16), part, part)
        scratch = [
            pltpu.VMEM((2, rows, features), jnp.bfloat16),
            pltpu.VMEM((1, rows), jnp.int32),
            pltpu.VMEM((1, rows), jnp.float32),
        ]
    return pl.pallas_call(
        functools.partial(prologue_kernel, bool(token_args)),
        out_shape=outs,
        in_specs=[HBM] * (3 + len(token_args)),
        out_specs=[VMEM] * len(outs),
        scratch_shapes=scratch + [pltpu.SemaphoreType.DMA((10,))],
        compiler_params=PARAMS,
    )(*[pltpu.with_memory_space_constraint(x, pltpu.HBM) for x in (*weights, *token_args)])


def gather_kernel(has_own, *refs):
    own = refs[0] if has_own else None
    pieces, weights = refs[has_own : has_own + 4], refs[has_own + 4 : has_own + 7]
    x_all, s_all, w_all, part = refs[has_own + 7 :]
    blocks, _, slots, width = pieces[0].shape
    member = lax.axis_index("wide") % 4
    place = lax.axis_index("narrow")
    for k, ref in enumerate(weights):
        column = at_quarter(member ^ k, width)
        for i in range(3):
            w_all[i, :, column] = ref[i]
    first = 0
    if has_own:
        x_all[:slots, :] = own[0]
        s_all[:slots, :] = own[1]
        first = slots
    for mask, ref in enumerate(pieces):
        column = at_quarter(place ^ mask, width)
        for block in range(blocks):
            rows = slice(first + block * slots, first + (block + 1) * slots)
            x_all[rows, column] = ref[block, 0]
            s_all[rows, column] = ref[block, 1]
    total = x_all.shape[0]
    tile = min(256, total)

    @pl.loop(0, total // tile)
    def _(step):
        rows = pl.ds(pl.multiple_of(step * tile, tile), tile)
        for i in range(3):
            held = s_all if i == 2 else x_all
            sums = None
            for k in range(3):
                column = at_quarter(member ^ k, width)
                term = dot_nt(w_all[i, :, column], held[rows, column])
                sums = term if sums is None else sums + term
            part[i, :, rows] = sums


def gather_parts(own, pieces, weights):
    blocks, _, slots, width = pieces[0].shape
    half = weights[0].shape[1]
    has_own = own is not None
    total = (blocks + has_own) * slots
    features = 4 * width
    return pl.pallas_call(
        functools.partial(gather_kernel, int(has_own)),
        out_shape=(
            jax.ShapeDtypeStruct((total, features), jnp.bfloat16),
            jax.ShapeDtypeStruct((total, features), jnp.bfloat16),
            jax.ShapeDtypeStruct((3, half, features), jnp.bfloat16),
            jax.ShapeDtypeStruct((3, half, total), jnp.float32),
        ),
        in_specs=[VMEM] * (7 + has_own),
        out_specs=[VMEM] * 4,
        compiler_params=PARAMS,
        cost_estimate=pl.CostEstimate(flops=1, bytes_accessed=1, transcendentals=0),
    )(*([own] if has_own else []), *pieces, *weights)


def outer_kernel(x_all, s_all, w_part, part, last, units, kept, sent, w_all):
    width = last.shape[2]
    place = lax.axis_index("narrow")
    last_column = at_quarter(lax.axis_index("wide") % 4 ^ 3, width)
    w_all[...] = w_part[...]
    for i in range(3):
        w_all[i, :, last_column] = last[i]
    total = x_all.shape[0]
    tile = min(width, total)
    for ref in (kept, sent):
        ref[:, 2 * total :, :] = jnp.zeros_like(ref[:, 2 * total :, :])
    routers = []
    for step in range(total // tile):
        rows = slice(step * tile, (step + 1) * tile)
        lower = slice(total + step * tile, total + (step + 1) * tile)
        x_tile, s_tile = x_all[rows, last_column], s_all[rows, last_column]
        gate = part[0, :, rows] + dot_nt(last[0], x_tile)
        up = part[1, :, rows] + dot_nt(last[1], x_tile)
        d_hidden = part[2, :, rows] + dot_nt(last[2], s_tile)
        sigma = jax.nn.sigmoid(gate)
        active = gate * sigma
        hidden = (active * up).astype(jnp.bfloat16)
        d_gate = (d_hidden * up * sigma * (1.0 + gate * (1.0 - sigma))).astype(jnp.bfloat16)
        d_up = (d_hidden * active).astype(jnp.bfloat16)
        units[0, :, rows] = d_gate
        units[1, :, rows] = d_up
        units[2, :, rows] = hidden
        router = jnp.sum(hidden.astype(jnp.float32) * d_hidden, axis=0, keepdims=True)
        kept[0, 2 * total + step : 2 * total + step + 1, :tile] = router
        routers.append(router)
        hidden_t, d_gate_t, d_up_t = hidden.T, d_gate.T, d_up.T
        for mask in range(4):
            column = at_quarter(place ^ mask, width)
            target = sent if mask % 2 else kept
            out_part = dot_nn(hidden_t, w_all[2, :, column])
            in_part = dot_nn(d_gate_t, w_all[0, :, column]) + dot_nn(d_up_t, w_all[1, :, column])
            target[mask // 2, rows, :] = out_part.astype(target.dtype)
            target[mask // 2, lower, :] = in_part.astype(target.dtype)
    put_pair(sent.at[0], 2 * total, jnp.concatenate(routers, 0))


def outer(x_all, s_all, w_part, part, last):
    total, features = x_all.shape
    _, half, width = last.shape
    return pl.pallas_call(
        outer_kernel,
        out_shape=(
            jax.ShapeDtypeStruct((3, half, total), jnp.bfloat16),
            jax.ShapeDtypeStruct((2, packet_rows(total), width), jnp.float32),
            jax.ShapeDtypeStruct((2, packet_rows(total), width), jnp.bfloat16),
        ),
        in_specs=[VMEM] * 5,
        out_specs=[VMEM] * 3,
        scratch_shapes=[pltpu.VMEM((3, half, features), jnp.bfloat16)],
        compiler_params=PARAMS,
        cost_estimate=pl.CostEstimate(
            flops=8 * half * features * total, bytes_accessed=0, transcendentals=0
        ),
    )(x_all, s_all, w_part, part, last)


def grads_kernel(units, x_all, s_all, *outs):
    half, total = units.shape[1:]
    width = outs[0].shape[2]
    member = lax.axis_index("wide") % 4
    left = units[0:2].reshape(2 * half, total)
    for k in (3, 2, 1, 0):
        column = at_quarter(member ^ k, width)
        both = dot_nn(left, x_all[:, column])
        outs[k][0] = both[:half].astype(outs[k].dtype)
        outs[k][1] = both[half:].astype(outs[k].dtype)
        outs[k][2] = dot_nn(units[2], s_all[:, column]).astype(outs[k].dtype)


def weight_grads(units, x_all, s_all):
    half, total = units.shape[1:]
    features = x_all.shape[1]
    return pl.pallas_call(
        grads_kernel,
        out_shape=tuple(
            jax.ShapeDtypeStruct((3, half, features // 4), jnp.bfloat16 if k > 1 else jnp.float32)
            for k in range(4)
        ),
        in_specs=[VMEM] * 3,
        out_specs=[VMEM] * 4,
        compiler_params=PARAMS,
        cost_estimate=pl.CostEstimate(
            flops=6 * half * features * total, bytes_accessed=0, transcendentals=0
        ),
    )(units, x_all, s_all)


def write_rows(held, outs, sems, first):
    rows = pl.ds(pl.multiple_of(first, 16), held.shape[1])
    copies = [
        pltpu.make_async_copy(held.at[i], out.at[rows, :], sems.at[i]) for i, out in enumerate(outs)
    ]
    return copies


def keep_kernel(own, got, out_0, out_1, out_2, held, sems):
    first = lax.axis_index("wide") % 2 * held.shape[1]
    copies = write_rows(held, (out_0, out_1, out_2), sems, first)
    for i, copy in enumerate(copies):
        held[i] = own[i] + got[i].astype(jnp.float32)
        copy.start()
    for copy in copies:
        copy.wait()


def give_kernel(in_0, in_1, in_2, got, out_0, out_1, out_2, held, sems):
    first = (1 - lax.axis_index("wide") % 2) * held.shape[1]
    copies = write_rows(held, (out_0, out_1, out_2), sems, first)
    for i, copy in enumerate(copies):
        held[i] = got[i].astype(jnp.float32)
        copy.start()
    for copy in copies:
        copy.wait()


def join_grads(own, got_x, got_z):
    _, half, width = own.shape
    shape = jax.ShapeDtypeStruct((2 * half, width), jnp.float32)
    scratch = [pltpu.VMEM(own.shape, jnp.float32), pltpu.SemaphoreType.DMA((3,))]
    kept = pl.pallas_call(
        keep_kernel,
        out_shape=(shape,) * 3,
        in_specs=[VMEM] * 2,
        out_specs=[HBM] * 3,
        scratch_shapes=scratch,
        compiler_params=PARAMS,
        cost_estimate=pl.CostEstimate(flops=1, bytes_accessed=0, transcendentals=0),
    )(own, got_z)
    return pl.pallas_call(
        give_kernel,
        out_shape=(shape,) * 3,
        in_specs=[HBM] * 3 + [VMEM],
        out_specs=[HBM] * 3,
        scratch_shapes=scratch,
        input_output_aliases={0: 0, 1: 1, 2: 2},
        compiler_params=PARAMS,
    )(*kept, got_x)


def cross_kernel(kept, got, sent):
    total = (kept.shape[1] - EXTRA) // 2
    tile = min(kept.shape[2], total)
    count = total // tile
    body = slice(0, 2 * total)
    sent[body, :] = (kept[1, body, :] + got[1, body, :].astype(jnp.float32)).astype(sent.dtype)
    sent[2 * total :, :] = jnp.zeros_like(sent[2 * total :, :])
    router = kept[0, 2 * total : 2 * total + count, :] + get_pair(got.at[0], 2 * total, count)
    put_pair(sent, 2 * total, router)


def cross_part(kept, got):
    return pl.pallas_call(
        cross_kernel,
        out_shape=jax.ShapeDtypeStruct(got.shape[1:], got.dtype),
        in_specs=[VMEM] * 2,
        out_specs=VMEM,
        compiler_params=PARAMS,
    )(kept, got)


def result_kernel(kept, got, across, out):
    total = (kept.shape[1] - EXTRA) // 2
    count = total // min(kept.shape[2], total)
    body, tail = slice(0, 2 * total), slice(2 * total, 2 * total + count)
    value = kept[0, body, :] + got[0, body, :].astype(jnp.float32)
    out[body, :] = value + across[body, :].astype(jnp.float32)
    out[2 * total :, :] = jnp.zeros_like(out[2 * total :, :])
    router = kept[0, tail, :] + get_pair(got.at[0], 2 * total, count)
    out[tail, :] = router + get_pair(across, 2 * total, count)


def result_parts(kept, got, across):
    return pl.pallas_call(
        result_kernel,
        out_shape=jax.ShapeDtypeStruct(kept.shape[1:], jnp.float32),
        in_specs=[VMEM] * 3,
        out_specs=VMEM,
        compiler_params=PARAMS,
    )(kept, got, across)


def first_kernel(kept, got, to_y, to_x):
    total = (kept.shape[1] - EXTRA) // 2
    slots = total // 4
    count = total // min(kept.shape[2], total)
    body = slice(0, total)
    to_y[body, :] = (kept[1, body, :] + got[1, body, :].astype(jnp.float32)).astype(to_y.dtype)
    put_pair(
        to_y,
        total,
        kept[0, 2 * total : 2 * total + count, :] + get_pair(got.at[0], 2 * total, count),
    )
    for part in range(2):
        for block in range(2):
            rows = slice(total + (2 * block + 1) * slots, total + (2 * block + 2) * slots)
            value = kept[part, rows, :] + got[part, rows, :].astype(jnp.float32)
            to_x[part, block * slots : (block + 1) * slots, :] = value.astype(to_x.dtype)


def first_parts(kept, got):
    total, width = (kept.shape[1] - EXTRA) // 2, kept.shape[2]
    return pl.pallas_call(
        first_kernel,
        out_shape=(
            jax.ShapeDtypeStruct((total + EXTRA, width), jnp.bfloat16),
            jax.ShapeDtypeStruct((2, total // 2, width), jnp.bfloat16),
        ),
        in_specs=[VMEM] * 2,
        out_specs=[VMEM] * 2,
        compiler_params=PARAMS,
    )(kept, got)


def ffn_kernel(kept, got, from_y, held, to_x):
    total = (kept.shape[1] - EXTRA) // 2
    slots, width = total // 4, kept.shape[2]
    count = total // min(width, total)
    router = kept[0, 2 * total : 2 * total + count, :] + get_pair(got.at[0], 2 * total, count)
    router = router + get_pair(from_y, total, count)
    pairs = []
    for block in range(4):
        rows = slice(block * slots, (block + 1) * slots)
        value = kept[0, rows, :] + got[0, rows, :].astype(jnp.float32)
        value = value + from_y[rows, :].astype(jnp.float32)
        out = to_x if block % 2 else held
        place = block // 2
        out[place * slots : (place + 1) * slots, :] = value.astype(out.dtype)
        lane = block * slots % width
        pairs.append(router[block * slots // width :, lane : lane + slots][:1])
    held[2 * slots :, :] = jnp.zeros_like(held[2 * slots :, :])
    to_x[2 * slots :, :] = jnp.zeros_like(to_x[2 * slots :, :])
    held[2 * slots : 2 * slots + 1, :slots] = pairs[0]
    held[2 * slots + 1 : 2 * slots + 2, :slots] = pairs[2]
    put_pair(to_x, 2 * slots, jnp.concatenate([pairs[1], pairs[3]], 0))


def ffn_parts(kept, got, from_y):
    total, width = (kept.shape[1] - EXTRA) // 2, kept.shape[2]
    shape = (total // 2 + EXTRA, width)
    return pl.pallas_call(
        ffn_kernel,
        out_shape=(
            jax.ShapeDtypeStruct(shape, jnp.float32),
            jax.ShapeDtypeStruct(shape, jnp.bfloat16),
        ),
        in_specs=[VMEM] * 3,
        out_specs=[VMEM] * 2,
        compiler_params=PARAMS,
    )(kept, got, from_y)


def input_kernel(kept, got, from_x, held, to_y):
    total = (kept.shape[1] - EXTRA) // 2
    slots = total // 4
    for part, out in enumerate((held, to_y)):
        for block in range(2):
            rows = slice(total + 2 * block * slots, total + (2 * block + 1) * slots)
            here = slice(block * slots, (block + 1) * slots)
            value = kept[part, rows, :] + got[part, rows, :].astype(jnp.float32)
            out[here, :] = (value + from_x[part, here, :].astype(jnp.float32)).astype(out.dtype)


def input_parts(kept, got, from_x):
    shape = from_x.shape[1:]
    return pl.pallas_call(
        input_kernel,
        out_shape=(
            jax.ShapeDtypeStruct(shape, jnp.float32),
            jax.ShapeDtypeStruct(shape, jnp.bfloat16),
        ),
        in_specs=[VMEM] * 3,
        out_specs=[VMEM] * 2,
        compiler_params=PARAMS,
    )(kept, got, from_x)


def last_kernel(ffn, from_x, grad, from_y, held, to_z):
    slots = grad.shape[0] // 2
    router = ffn[2 * slots : 2 * slots + 2, :] + get_pair(from_x, 2 * slots, 2)
    for block, out in enumerate((held, to_z)):
        rows = slice(block * slots, (block + 1) * slots)
        out[:slots, :] = (ffn[rows, :] + from_x[rows, :].astype(jnp.float32)).astype(out.dtype)
        out[slots : 2 * slots, :] = (grad[rows, :] + from_y[rows, :].astype(jnp.float32)).astype(
            out.dtype
        )
    held[2 * slots :, :] = jnp.broadcast_to(router[:1], (EXTRA, router.shape[1]))
    put_pair(to_z, 2 * slots, router[1:])


def last_parts(ffn, from_x, grad, from_y):
    return pl.pallas_call(
        last_kernel,
        out_shape=(
            jax.ShapeDtypeStruct(ffn.shape, jnp.float32),
            jax.ShapeDtypeStruct(ffn.shape, jnp.bfloat16),
        ),
        in_specs=[VMEM] * 4,
        out_specs=[VMEM] * 2,
        compiler_params=PARAMS,
        cost_estimate=pl.CostEstimate(flops=10**10, bytes_accessed=0, transcendentals=0),
    )(ffn, from_x, grad, from_y)


def finish_kernel(prob, own, *refs):
    got, (output, tokens_grad, prob_grad) = refs[:-3], refs[-3:]
    slots, width = output.shape
    ffn, grad = own[:slots, :], own[slots : 2 * slots, :]
    router = own[2 * slots : 2 * slots + 1, :]
    for ref in got:
        ffn = ffn + ref[:slots, :].astype(jnp.float32)
        grad = grad + ref[slots : 2 * slots, :].astype(jnp.float32)
        router = router + get_pair(ref, 2 * slots, 1)
    weight = jnp.broadcast_to(prob[...], (128, slots)).T[:, :1]
    output[...] = (ffn.astype(jnp.bfloat16).astype(jnp.float32) * weight).astype(jnp.bfloat16)
    tokens_grad[...] = grad.astype(jnp.bfloat16)
    prob_grad[...] = router[:, :slots] / prob[...]


def finish(prob, own, got):
    slots, width = (own.shape[0] - EXTRA) // 2, own.shape[1]
    part = jax.ShapeDtypeStruct((slots, width), jnp.bfloat16)
    return pl.pallas_call(
        finish_kernel,
        out_shape=(part, part, jax.ShapeDtypeStruct((1, slots), jnp.float32)),
        in_specs=[VMEM] * (2 + len(got)),
        out_specs=[VMEM] * 3,
        compiler_params=PARAMS,
    )(prob, own, *got)


def shards(tokens, cotangent, expert_ids, route_prob, gate_weight, up_weight, down_weight):
    wide_count = lax.axis_size("wide")
    narrow_count = lax.axis_size("narrow")
    expert_count = wide_count // 4
    tok_rows, features = tokens.shape
    width = features // narrow_count
    slots = min(4 * tok_rows // expert_count, tok_rows)
    direct = expert_count == 2 and slots == tok_rows
    place = lax.axis_index("narrow")
    masks = (1, 4, 5)
    groups = [
        [4 * e + 2 * b + a for e in range(expert_count) for a in range(2)] for b in range(2)
    ]

    weights = (gate_weight.T, up_weight.T, down_weight.T)
    if direct:
        keep, give, own, same, other = prologue(
            weights, (tokens, cotangent, expert_ids.T, route_prob[None, :]), width
        )
        mine = jnp.stack(
            [partner(part, "wide", mask) for mask, part in zip(masks, (same, other, other))]
        )
    else:
        own = None
        keep, give = prologue(weights, (), width)
        chosen = expert_ids[:, 0]
        onehot = (chosen[:, None] == jnp.arange(expert_count, dtype=jnp.int32)[None, :]).astype(
            jnp.int32
        )
        rank = jnp.sum((jnp.cumsum(onehot, axis=0) - onehot) * onehot, axis=1)
        slot_place = chosen * slots + rank
        source = (
            jnp.full((expert_count * slots,), tok_rows, jnp.int32)
            .at[slot_place]
            .set(jnp.arange(tok_rows, dtype=jnp.int32))
        )
        scaled = (route_prob[:, None] * cotangent.astype(jnp.float32)).astype(jnp.bfloat16)
        both = jnp.stack([tokens, scaled])
        both = lax.dynamic_slice_in_dim(both, place * width, width, 2)
        both = jnp.concatenate([both, jnp.zeros((2, 1, width), jnp.bfloat16)], 1)
        routed = both[:, source].reshape(2, expert_count, slots, width).transpose(1, 0, 2, 3)
        routed = jnp.repeat(routed, 2, axis=0)
        mine = lax.all_to_all(
            routed, "wide", split_axis=0, concat_axis=0, axis_index_groups=groups, tiled=True
        )

    mine, from_x, from_z = lax.optimization_barrier(
        (mine, partner(give, "wide", 1), partner(keep, "wide", 2))
    )
    from_d = partner(from_x, "wide", 2)
    across = partner(mine, "narrow", 2)
    pieces = (mine, partner(mine, "narrow", 1), across, partner(across, "narrow", 1))
    x_all, s_all, w_part, part = gather_parts(own, pieces, (keep, from_x, from_z))
    units, kept, sent = outer(x_all, s_all, w_part, part, from_d)
    got = partner(sent, "narrow", 1)
    grad_own, grad_x, grad_z, grad_d = weight_grads(units, x_all, s_all)
    got_d = partner(grad_d, "wide", 2)
    if direct:
        to_y, to_x = first_parts(kept, got)
        ffn_held, ffn_x = ffn_parts(kept, got, partner(to_y, "narrow", 2))
        grad_held, grad_y = input_parts(kept, got, partner(to_x, "wide", 1))
        grad_x, grad_z, _, _ = lax.optimization_barrier((grad_x, grad_z, ffn_x, grad_y))
        held, to_z = last_parts(
            ffn_held, partner(ffn_x, "wide", 1), grad_held, partner(grad_y, "narrow", 2)
        )
        output, tokens_grad, prob_grad = finish(
            route_prob[None, :], held, [partner(to_z, "wide", 4)]
        )
        prob_grad = prob_grad[0]
    else:
        across = partner(cross_part(kept, got), "narrow", 2)
        result = result_parts(kept, got, across)
        total = (result.shape[0] - EXTRA) // 2
        parts = result[: 2 * total].astype(jnp.bfloat16)
        parts = parts.reshape(2, 2 * expert_count, slots, width)
        back = lax.all_to_all(
            parts, "wide", split_axis=1, concat_axis=1, axis_index_groups=groups, tiled=True
        )
        back = back.reshape(2, expert_count, 2, slots, width).astype(jnp.float32).sum(2)
        back = back.reshape(2, expert_count * slots, width)[:, slot_place]
        router = result[2 * total : 2 * total + total // min(width, total), : min(width, total)]
        router = router.reshape(2 * expert_count, slots)
        high = lax.reduce_precision(router, 8, 7)
        pair = jnp.stack([high, router - high], 1).astype(jnp.bfloat16)
        pair = lax.all_to_all(
            pair, "wide", split_axis=0, concat_axis=0, axis_index_groups=groups, tiled=True
        )
        router = pair.reshape(expert_count, 4, slots).astype(jnp.float32).sum(1)
        prob_grad = router.reshape(expert_count * slots)[slot_place] / route_prob
        ffn = back[0].astype(jnp.bfloat16).astype(jnp.float32)
        output = (route_prob[:, None] * ffn).astype(jnp.bfloat16)
        tokens_grad = back[1].astype(jnp.bfloat16)
    grad_x = (grad_x + got_d.astype(jnp.float32)).astype(jnp.bfloat16)
    got_x = partner(grad_x, "wide", 1)
    got_z = partner(grad_z, "wide", 2)
    gate_grad, up_grad, down_grad = join_grads(grad_own, got_x, got_z)
    return (output, tokens_grad, prob_grad, gate_grad.T, up_grad.T, down_grad.T)


def solution(mesh):
    in_specs = (
        P("wide", None),
        P("wide", None),
        P("wide", None),
        P("wide"),
        P("wide", "narrow"),
        P("wide", "narrow"),
        P("wide", "narrow"),
    )
    out_specs = (
        P("wide", "narrow"),
        P("wide", "narrow"),
        P("wide"),
        P("wide", "narrow"),
        P("wide", "narrow"),
        P("wide", "narrow"),
    )
    return jax.shard_map(shards, mesh=mesh, in_specs=in_specs, out_specs=out_specs, check_vma=False)
```

```python
import functools

import jax
import jax.numpy as jnp
from jax import lax
from jax.experimental import pallas as pl
from jax.experimental.pallas import tpu as pltpu
from jax.sharding import PartitionSpec as P

VMEM = pl.BlockSpec(memory_space=pltpu.VMEM)
HBM = pl.BlockSpec(memory_space=pltpu.HBM)
EXTRA = 16
PARAMS = pltpu.CompilerParams(vmem_limit_bytes=32 * 1024 * 1024)


def partner(x, axis, mask):
    return lax.ppermute(x, axis, [(i, i ^ mask) for i in range(lax.axis_size(axis))])


def dot_nn(left, right):
    return lax.dot_general(
        left, right, (((1,), (0,)), ((), ())), preferred_element_type=jnp.float32
    )


def dot_nt(left, right):
    return lax.dot_general(
        left, right, (((1,), (1,)), ((), ())), preferred_element_type=jnp.float32
    )


def at_quarter(index, width):
    return pl.ds(pl.multiple_of(index * width, width), width)


def packet_rows(rows):
    return 2 * rows + EXTRA


def put_pair(ref, first, value):
    count, lanes = value.shape
    high = value.astype(jnp.bfloat16).astype(jnp.float32)
    both = jnp.concatenate([high, value - high], 0)
    both = jnp.concatenate([both, jnp.zeros((EXTRA - 2 * count, lanes), jnp.float32)], 0)
    ref[first : first + EXTRA, :lanes] = both.astype(ref.dtype)


def get_pair(ref, first, count):
    both = ref[first : first + EXTRA, :].astype(jnp.float32)
    return both[:count] + both[count : 2 * count]


def prologue_kernel(routed, gate, up, down, *refs):
    if routed:
        tokens, cotangent, ids, prob, keep, give, own, same, other = refs[:9]
        held, ids_row, prob_row, sems = refs[9:]
        parts = ((tokens, held.at[0]), (cotangent, held.at[1]), (ids, ids_row), (prob, prob_row))
    else:
        keep, give, sems = refs
        parts = ()
    half = keep.shape[1]
    x_bit = lax.axis_index("wide") % 2
    keep_rows = pl.ds(pl.multiple_of(x_bit * half, 16), half)
    give_rows = pl.ds(pl.multiple_of((1 - x_bit) * half, 16), half)
    for i, ref in enumerate((gate, up, down)):
        parts += ((ref.at[keep_rows, :], keep.at[i]), (ref.at[give_rows, :], give.at[i]))
    copies = [pltpu.make_async_copy(src, dst, sems.at[i]) for i, (src, dst) in enumerate(parts)]
    for copy in copies:
        copy.start()
    if routed:
        for copy in copies[:4]:
            copy.wait()
        rows = held.shape[1]
        width = same.shape[2]
        mine = lax.axis_index("wide") // 4
        column = at_quarter(lax.axis_index("narrow"), width)
        chosen = jnp.broadcast_to(ids_row[...], (128, rows)).astype(jnp.float32).T[:, :1]
        weight = jnp.broadcast_to(prob_row[...], (128, rows)).T[:, :1]
        here = jnp.where(chosen == mine.astype(jnp.float32), 1.0, 0.0)
        for i in range(2):
            factor = weight if i else jnp.ones_like(weight)
            own[i] = (held[i].astype(jnp.float32) * (factor * here)).astype(jnp.bfloat16)
            part = held[i, :, column].astype(jnp.float32)
            same[i] = (part * (factor * here)).astype(jnp.bfloat16)
            other[i] = (part * (factor * (1.0 - here))).astype(jnp.bfloat16)
    for copy in copies[len(copies) - 6 :]:
        copy.wait()


def prologue(weights, token_args, width):
    hidden, quarter = weights[0].shape
    half = jax.ShapeDtypeStruct((3, hidden // 2, quarter), jnp.bfloat16)
    outs, scratch = (half, half), []
    if token_args:
        rows, features = token_args[0].shape
        part = jax.ShapeDtypeStruct((2, rows, width), jnp.bfloat16)
        outs += (jax.ShapeDtypeStruct((2, rows, features), jnp.bfloat16), part, part)
        scratch = [
            pltpu.VMEM((2, rows, features), jnp.bfloat16),
            pltpu.VMEM((1, rows), jnp.int32),
            pltpu.VMEM((1, rows), jnp.float32),
        ]
    return pl.pallas_call(
        functools.partial(prologue_kernel, bool(token_args)),
        out_shape=outs,
        in_specs=[HBM] * (3 + len(token_args)),
        out_specs=[VMEM] * len(outs),
        scratch_shapes=scratch + [pltpu.SemaphoreType.DMA((10,))],
        compiler_params=PARAMS,
    )(*[pltpu.with_memory_space_constraint(x, pltpu.HBM) for x in (*weights, *token_args)])


def gather_kernel(has_own, *refs):
    own = refs[0] if has_own else None
    pieces, weights = refs[has_own : has_own + 4], refs[has_own + 4 : has_own + 7]
    x_all, s_all, w_all, part = refs[has_own + 7 :]
    blocks, _, slots, width = pieces[0].shape
    member = lax.axis_index("wide") % 4
    place = lax.axis_index("narrow")
    for k, ref in enumerate(weights):
        column = at_quarter(member ^ k, width)
        for i in range(3):
            w_all[i, :, column] = ref[i]
    first = 0
    if has_own:
        x_all[:slots, :] = own[0]
        s_all[:slots, :] = own[1]
        first = slots
    for mask, ref in enumerate(pieces):
        column = at_quarter(place ^ mask, width)
        for block in range(blocks):
            rows = slice(first + block * slots, first + (block + 1) * slots)
            x_all[rows, column] = ref[block, 0]
            s_all[rows, column] = ref[block, 1]
    total = x_all.shape[0]
    tile = min(256, total)

    @pl.loop(0, total // tile)
    def _(step):
        rows = pl.ds(pl.multiple_of(step * tile, tile), tile)
        for i in range(3):
            held = s_all if i == 2 else x_all
            sums = None
            for k in range(3):
                column = at_quarter(member ^ k, width)
                term = dot_nt(w_all[i, :, column], held[rows, column])
                sums = term if sums is None else sums + term
            part[i, :, rows] = sums


def gather_parts(own, pieces, weights):
    blocks, _, slots, width = pieces[0].shape
    half = weights[0].shape[1]
    has_own = own is not None
    total = (blocks + has_own) * slots
    features = 4 * width
    return pl.pallas_call(
        functools.partial(gather_kernel, int(has_own)),
        out_shape=(
            jax.ShapeDtypeStruct((total, features), jnp.bfloat16),
            jax.ShapeDtypeStruct((total, features), jnp.bfloat16),
            jax.ShapeDtypeStruct((3, half, features), jnp.bfloat16),
            jax.ShapeDtypeStruct((3, half, total), jnp.float32),
        ),
        in_specs=[VMEM] * (7 + has_own),
        out_specs=[VMEM] * 4,
        compiler_params=PARAMS,
        cost_estimate=pl.CostEstimate(flops=1, bytes_accessed=1, transcendentals=0),
    )(*([own] if has_own else []), *pieces, *weights)


def grad_parts(units, x_all, s_all, column, out):
    half, total = units.shape[1:]
    both = dot_nn(units[0:2].reshape(2 * half, total), x_all[:, column])
    out[0] = both[:half].astype(out.dtype)
    out[1] = both[half:].astype(out.dtype)
    out[2] = dot_nn(units[2], s_all[:, column]).astype(out.dtype)


def outer_kernel(x_all, s_all, w_part, part, last, units, kept, sent, to_d, w_all, sem):
    width = last.shape[2]
    copy = pltpu.make_async_copy(w_part, w_all, sem)
    copy.start()
    place = lax.axis_index("narrow")
    last_column = at_quarter(lax.axis_index("wide") % 4 ^ 3, width)
    total = x_all.shape[0]
    tile = min(width, total)
    for ref in (kept, sent):
        ref[:, 2 * total :, :] = jnp.zeros_like(ref[:, 2 * total :, :])
    routers = []
    for step in range(total // tile):
        rows = slice(step * tile, (step + 1) * tile)
        lower = slice(total + step * tile, total + (step + 1) * tile)
        x_tile, s_tile = x_all[rows, last_column], s_all[rows, last_column]
        gate = part[0, :, rows] + dot_nt(last[0], x_tile)
        up = part[1, :, rows] + dot_nt(last[1], x_tile)
        d_hidden = part[2, :, rows] + dot_nt(last[2], s_tile)
        sigma = 0.5 + 0.5 * jnp.tanh(0.5 * gate)
        active = gate * sigma
        hidden = (active * up).astype(jnp.bfloat16)
        slope = sigma + active * (1.0 - sigma)
        d_gate = (d_hidden * up * slope).astype(jnp.bfloat16)
        d_up = (d_hidden * active).astype(jnp.bfloat16)
        units[0, :, rows] = d_gate
        units[1, :, rows] = d_up
        units[2, :, rows] = hidden
        router = jnp.sum(hidden.astype(jnp.float32) * d_hidden, axis=0, keepdims=True)
        kept[0, 2 * total + step : 2 * total + step + 1, :tile] = router
        routers.append(router)
        hidden_t, d_gate_t, d_up_t = hidden.T, d_gate.T, d_up.T
        if step == 0:
            copy.wait()
            for i in range(3):
                w_all[i, :, last_column] = last[i]
        for mask in range(4):
            column = at_quarter(place ^ mask, width)
            target = sent if mask % 2 else kept
            out_part = dot_nn(hidden_t, w_all[2, :, column])
            in_part = dot_nn(d_gate_t, w_all[0, :, column]) + dot_nn(d_up_t, w_all[1, :, column])
            target[mask // 2, rows, :] = out_part.astype(target.dtype)
            target[mask // 2, lower, :] = in_part.astype(target.dtype)
    put_pair(sent.at[0], 2 * total, jnp.concatenate(routers, 0))
    grad_parts(units, x_all, s_all, last_column, to_d)


def outer(x_all, s_all, w_part, part, last):
    total, features = x_all.shape
    _, half, width = last.shape
    return pl.pallas_call(
        outer_kernel,
        out_shape=(
            jax.ShapeDtypeStruct((3, half, total), jnp.bfloat16),
            jax.ShapeDtypeStruct((2, packet_rows(total), width), jnp.float32),
            jax.ShapeDtypeStruct((2, packet_rows(total), width), jnp.bfloat16),
            jax.ShapeDtypeStruct(last.shape, jnp.bfloat16),
        ),
        in_specs=[VMEM] * 5,
        out_specs=[VMEM] * 4,
        scratch_shapes=[
            pltpu.VMEM((3, half, features), jnp.bfloat16),
            pltpu.SemaphoreType.DMA,
        ],
        compiler_params=PARAMS,
        cost_estimate=pl.CostEstimate(
            flops=8 * half * features * total, bytes_accessed=0, transcendentals=0
        ),
    )(x_all, s_all, w_part, part, last)


def grads_kernel(units, x_all, s_all, *outs):
    width = outs[0].shape[2]
    member = lax.axis_index("wide") % 4
    for k, out in enumerate(outs):
        grad_parts(units, x_all, s_all, at_quarter(member ^ k, width), out)


def weight_grads(units, x_all, s_all):
    half, total = units.shape[1:]
    features = x_all.shape[1]
    return pl.pallas_call(
        grads_kernel,
        out_shape=tuple(
            jax.ShapeDtypeStruct((3, half, features // 4), jnp.bfloat16 if k > 1 else jnp.float32)
            for k in range(3)
        ),
        in_specs=[VMEM] * 3,
        out_specs=[VMEM] * 3,
        compiler_params=PARAMS,
        cost_estimate=pl.CostEstimate(
            flops=5 * half * features * total, bytes_accessed=0, transcendentals=0
        ),
    )(units, x_all, s_all)


def join_kernel(own, got_x, out_0, out_1, out_2, held, sems):
    half = held.shape[1]
    x_bit = lax.axis_index("wide") % 2
    copies = []
    for part, held_part in enumerate((own, held)):
        first = (part * (1 - x_bit) + (1 - part) * x_bit) * half
        rows = pl.ds(pl.multiple_of(first, 16), half)
        for i, out in enumerate((out_0, out_1, out_2)):
            if part:
                held[i] = got_x[i].astype(jnp.float32)
            place = sems.at[3 * part + i]
            copies.append(pltpu.make_async_copy(held_part.at[i], out.at[rows, :], place))
            copies[-1].start()
    for copy in copies:
        copy.wait()


def join_grads(own, got_x):
    _, half, width = own.shape
    shape = jax.ShapeDtypeStruct((2 * half, width), jnp.float32)
    return pl.pallas_call(
        join_kernel,
        out_shape=(shape,) * 3,
        in_specs=[VMEM] * 2,
        out_specs=[HBM] * 3,
        scratch_shapes=[
            pltpu.VMEM(own.shape, jnp.float32),
            pltpu.SemaphoreType.DMA((6,)),
        ],
        compiler_params=PARAMS,
        cost_estimate=pl.CostEstimate(flops=1, bytes_accessed=0, transcendentals=0),
    )(own, got_x)


def cross_kernel(kept, got, sent):
    total = (kept.shape[1] - EXTRA) // 2
    tile = min(kept.shape[2], total)
    count = total // tile
    body = slice(0, 2 * total)
    sent[body, :] = (kept[1, body, :] + got[1, body, :].astype(jnp.float32)).astype(sent.dtype)
    sent[2 * total :, :] = jnp.zeros_like(sent[2 * total :, :])
    router = kept[0, 2 * total : 2 * total + count, :] + get_pair(got.at[0], 2 * total, count)
    put_pair(sent, 2 * total, router)


def cross_part(kept, got):
    return pl.pallas_call(
        cross_kernel,
        out_shape=jax.ShapeDtypeStruct(got.shape[1:], got.dtype),
        in_specs=[VMEM] * 2,
        out_specs=VMEM,
        compiler_params=PARAMS,
    )(kept, got)


def result_kernel(kept, got, across, out):
    total = (kept.shape[1] - EXTRA) // 2
    count = total // min(kept.shape[2], total)
    body, tail = slice(0, 2 * total), slice(2 * total, 2 * total + count)
    value = kept[0, body, :] + got[0, body, :].astype(jnp.float32)
    out[body, :] = value + across[body, :].astype(jnp.float32)
    out[2 * total :, :] = jnp.zeros_like(out[2 * total :, :])
    router = kept[0, tail, :] + get_pair(got.at[0], 2 * total, count)
    out[tail, :] = router + get_pair(across, 2 * total, count)


def result_parts(kept, got, across):
    return pl.pallas_call(
        result_kernel,
        out_shape=jax.ShapeDtypeStruct(kept.shape[1:], jnp.float32),
        in_specs=[VMEM] * 3,
        out_specs=VMEM,
        compiler_params=PARAMS,
    )(kept, got, across)


def first_kernel(kept, got, to_y, to_x):
    total = (kept.shape[1] - EXTRA) // 2
    slots = total // 4
    count = total // min(kept.shape[2], total)
    body = slice(0, total)
    to_y[body, :] = (kept[1, body, :] + got[1, body, :].astype(jnp.float32)).astype(to_y.dtype)
    put_pair(
        to_y,
        total,
        kept[0, 2 * total : 2 * total + count, :] + get_pair(got.at[0], 2 * total, count),
    )
    for part in range(2):
        for block in range(2):
            rows = slice(total + (2 * block + 1) * slots, total + (2 * block + 2) * slots)
            value = kept[part, rows, :] + got[part, rows, :].astype(jnp.float32)
            to_x[part, block * slots : (block + 1) * slots, :] = value.astype(to_x.dtype)


def first_parts(kept, got):
    total, width = (kept.shape[1] - EXTRA) // 2, kept.shape[2]
    return pl.pallas_call(
        first_kernel,
        out_shape=(
            jax.ShapeDtypeStruct((total + EXTRA, width), jnp.bfloat16),
            jax.ShapeDtypeStruct((2, total // 2, width), jnp.bfloat16),
        ),
        in_specs=[VMEM] * 2,
        out_specs=[VMEM] * 2,
        compiler_params=PARAMS,
    )(kept, got)


def ffn_kernel(kept, got, from_y, held, to_x):
    total = (kept.shape[1] - EXTRA) // 2
    slots, width = total // 4, kept.shape[2]
    count = total // min(width, total)
    router = kept[0, 2 * total : 2 * total + count, :] + get_pair(got.at[0], 2 * total, count)
    router = router + get_pair(from_y, total, count)
    pairs = []
    for block in range(4):
        rows = slice(block * slots, (block + 1) * slots)
        value = kept[0, rows, :] + got[0, rows, :].astype(jnp.float32)
        value = value + from_y[rows, :].astype(jnp.float32)
        out = to_x if block % 2 else held
        place = block // 2
        out[place * slots : (place + 1) * slots, :] = value.astype(out.dtype)
        lane = block * slots % width
        pairs.append(router[block * slots // width :, lane : lane + slots][:1])
    held[2 * slots :, :] = jnp.zeros_like(held[2 * slots :, :])
    to_x[2 * slots :, :] = jnp.zeros_like(to_x[2 * slots :, :])
    held[2 * slots : 2 * slots + 1, :slots] = pairs[0]
    held[2 * slots + 1 : 2 * slots + 2, :slots] = pairs[2]
    put_pair(to_x, 2 * slots, jnp.concatenate([pairs[1], pairs[3]], 0))


def ffn_parts(kept, got, from_y):
    total, width = (kept.shape[1] - EXTRA) // 2, kept.shape[2]
    shape = (total // 2 + EXTRA, width)
    return pl.pallas_call(
        ffn_kernel,
        out_shape=(
            jax.ShapeDtypeStruct(shape, jnp.float32),
            jax.ShapeDtypeStruct(shape, jnp.bfloat16),
        ),
        in_specs=[VMEM] * 3,
        out_specs=[VMEM] * 2,
        compiler_params=PARAMS,
    )(kept, got, from_y)


def input_kernel(kept, got, from_x, held, to_y):
    total = (kept.shape[1] - EXTRA) // 2
    slots = total // 4
    for part, out in enumerate((held, to_y)):
        for block in range(2):
            rows = slice(total + 2 * block * slots, total + (2 * block + 1) * slots)
            here = slice(block * slots, (block + 1) * slots)
            value = kept[part, rows, :] + got[part, rows, :].astype(jnp.float32)
            out[here, :] = (value + from_x[part, here, :].astype(jnp.float32)).astype(out.dtype)


def input_parts(kept, got, from_x):
    shape = from_x.shape[1:]
    return pl.pallas_call(
        input_kernel,
        out_shape=(
            jax.ShapeDtypeStruct(shape, jnp.float32),
            jax.ShapeDtypeStruct(shape, jnp.bfloat16),
        ),
        in_specs=[VMEM] * 3,
        out_specs=[VMEM] * 2,
        compiler_params=PARAMS,
    )(kept, got, from_x)


def last_kernel(ffn, from_x, grad, from_y, held, to_z):
    slots = grad.shape[0] // 2
    router = ffn[2 * slots : 2 * slots + 2, :] + get_pair(from_x, 2 * slots, 2)
    for block, out in enumerate((held, to_z)):
        rows = slice(block * slots, (block + 1) * slots)
        out[:slots, :] = (ffn[rows, :] + from_x[rows, :].astype(jnp.float32)).astype(out.dtype)
        out[slots : 2 * slots, :] = (grad[rows, :] + from_y[rows, :].astype(jnp.float32)).astype(
            out.dtype
        )
    held[2 * slots :, :] = jnp.broadcast_to(router[:1], (EXTRA, router.shape[1]))
    put_pair(to_z, 2 * slots, router[1:])


def last_parts(ffn, from_x, grad, from_y):
    return pl.pallas_call(
        last_kernel,
        out_shape=(
            jax.ShapeDtypeStruct(ffn.shape, jnp.float32),
            jax.ShapeDtypeStruct(ffn.shape, jnp.bfloat16),
        ),
        in_specs=[VMEM] * 4,
        out_specs=[VMEM] * 2,
        compiler_params=PARAMS,
        cost_estimate=pl.CostEstimate(flops=3 * 10**9, bytes_accessed=0, transcendentals=0),
    )(ffn, from_x, grad, from_y)


def finish_kernel(prob, own, *refs):
    got, (output, tokens_grad, prob_grad) = refs[:-3], refs[-3:]
    slots, width = output.shape
    ffn, grad = own[:slots, :], own[slots : 2 * slots, :]
    router = own[2 * slots : 2 * slots + 1, :]
    for ref in got:
        ffn = ffn + ref[:slots, :].astype(jnp.float32)
        grad = grad + ref[slots : 2 * slots, :].astype(jnp.float32)
        router = router + get_pair(ref, 2 * slots, 1)
    weight = jnp.broadcast_to(prob[...], (128, slots)).T[:, :1]
    output[...] = (ffn.astype(jnp.bfloat16).astype(jnp.float32) * weight).astype(jnp.bfloat16)
    tokens_grad[...] = grad.astype(jnp.bfloat16)
    prob_grad[...] = router[:, :slots] / prob[...]


def finish(prob, own, got):
    slots, width = (own.shape[0] - EXTRA) // 2, own.shape[1]
    part = jax.ShapeDtypeStruct((slots, width), jnp.bfloat16)
    return pl.pallas_call(
        finish_kernel,
        out_shape=(part, part, jax.ShapeDtypeStruct((1, slots), jnp.float32)),
        in_specs=[VMEM] * (2 + len(got)),
        out_specs=[VMEM] * 3,
        compiler_params=PARAMS,
    )(prob, own, *got)


def shards(tokens, cotangent, expert_ids, route_prob, gate_weight, up_weight, down_weight):
    wide_count = lax.axis_size("wide")
    narrow_count = lax.axis_size("narrow")
    expert_count = wide_count // 4
    tok_rows, features = tokens.shape
    width = features // narrow_count
    slots = min(4 * tok_rows // expert_count, tok_rows)
    direct = expert_count == 2 and slots == tok_rows
    place = lax.axis_index("narrow")
    masks = (1, 4, 5)
    groups = [
        [4 * e + 2 * b + a for e in range(expert_count) for a in range(2)] for b in range(2)
    ]

    weights = (gate_weight.T, up_weight.T, down_weight.T)
    if direct:
        keep, give, own, same, other = prologue(
            weights, (tokens, cotangent, expert_ids.T, route_prob[None, :]), width
        )
        mine = jnp.stack(
            [partner(part, "wide", mask) for mask, part in zip(masks, (same, other, other))]
        )
    else:
        own = None
        keep, give = prologue(weights, (), width)
        chosen = expert_ids[:, 0]
        onehot = (chosen[:, None] == jnp.arange(expert_count, dtype=jnp.int32)[None, :]).astype(
            jnp.int32
        )
        rank = jnp.sum((jnp.cumsum(onehot, axis=0) - onehot) * onehot, axis=1)
        slot_place = chosen * slots + rank
        source = (
            jnp.full((expert_count * slots,), tok_rows, jnp.int32)
            .at[slot_place]
            .set(jnp.arange(tok_rows, dtype=jnp.int32))
        )
        scaled = (route_prob[:, None] * cotangent.astype(jnp.float32)).astype(jnp.bfloat16)
        both = jnp.stack([tokens, scaled])
        both = lax.dynamic_slice_in_dim(both, place * width, width, 2)
        both = jnp.concatenate([both, jnp.zeros((2, 1, width), jnp.bfloat16)], 1)
        routed = both[:, source].reshape(2, expert_count, slots, width).transpose(1, 0, 2, 3)
        routed = jnp.repeat(routed, 2, axis=0)
        mine = lax.all_to_all(
            routed, "wide", split_axis=0, concat_axis=0, axis_index_groups=groups, tiled=True
        )

    from_x, from_z = lax.optimization_barrier(
        (partner(give, "wide", 1), partner(keep, "wide", 2))
    )
    from_d = partner(from_x, "wide", 2)
    across = partner(mine, "narrow", 2)
    pieces = (mine, partner(mine, "narrow", 1), across, partner(across, "narrow", 1))
    x_all, s_all, w_part, part = gather_parts(own, pieces, (keep, from_x, from_z))
    units, kept, sent, grad_d = outer(x_all, s_all, w_part, part, from_d)
    got = partner(sent, "narrow", 1)
    got_d = partner(grad_d, "wide", 2)
    if direct:
        to_y, to_x = first_parts(kept, got)
        units, _ = lax.optimization_barrier((units, to_y))
        ffn_held, ffn_x = ffn_parts(kept, got, partner(to_y, "narrow", 2))
        grad_held, grad_y = input_parts(kept, got, partner(to_x, "wide", 1))
        grad_own, grad_x, grad_z = weight_grads(units, x_all, s_all)
        grad_x, grad_z, _, _ = lax.optimization_barrier((grad_x, grad_z, ffn_x, grad_y))
        held, to_z = last_parts(
            ffn_held, partner(ffn_x, "wide", 1), grad_held, partner(grad_y, "narrow", 2)
        )
        output, tokens_grad, prob_grad = finish(
            route_prob[None, :], held, [partner(to_z, "wide", 4)]
        )
        prob_grad = prob_grad[0]
    else:
        grad_own, grad_x, grad_z = weight_grads(units, x_all, s_all)
        across = partner(cross_part(kept, got), "narrow", 2)
        result = result_parts(kept, got, across)
        total = (result.shape[0] - EXTRA) // 2
        parts = result[: 2 * total].astype(jnp.bfloat16)
        parts = parts.reshape(2, 2 * expert_count, slots, width)
        back = lax.all_to_all(
            parts, "wide", split_axis=1, concat_axis=1, axis_index_groups=groups, tiled=True
        )
        back = back.reshape(2, expert_count, 2, slots, width).astype(jnp.float32).sum(2)
        back = back.reshape(2, expert_count * slots, width)[:, slot_place]
        router = result[2 * total : 2 * total + total // min(width, total), : min(width, total)]
        router = router.reshape(2 * expert_count, slots)
        high = lax.reduce_precision(router, 8, 7)
        pair = jnp.stack([high, router - high], 1).astype(jnp.bfloat16)
        pair = lax.all_to_all(
            pair, "wide", split_axis=0, concat_axis=0, axis_index_groups=groups, tiled=True
        )
        router = pair.reshape(expert_count, 4, slots).astype(jnp.float32).sum(1)
        prob_grad = router.reshape(expert_count * slots)[slot_place] / route_prob
        ffn = back[0].astype(jnp.bfloat16).astype(jnp.float32)
        output = (route_prob[:, None] * ffn).astype(jnp.bfloat16)
        tokens_grad = back[1].astype(jnp.bfloat16)
    grad_x = (grad_x + got_d.astype(jnp.float32)).astype(jnp.bfloat16)
    got_x = partner(grad_x, "wide", 1)
    got_z = partner(grad_z, "wide", 2)
    gate_grad, up_grad, down_grad = join_grads(grad_own + got_z.astype(jnp.float32), got_x)
    return (output, tokens_grad, prob_grad, gate_grad.T, up_grad.T, down_grad.T)


def solution(mesh):
    in_specs = (
        P("wide", None),
        P("wide", None),
        P("wide", None),
        P("wide"),
        P("wide", "narrow"),
        P("wide", "narrow"),
        P("wide", "narrow"),
    )
    out_specs = (
        P("wide", "narrow"),
        P("wide", "narrow"),
        P("wide"),
        P("wide", "narrow"),
        P("wide", "narrow"),
        P("wide", "narrow"),
    )
    return jax.shard_map(shards, mesh=mesh, in_specs=in_specs, out_specs=out_specs, check_vma=False)
```

```python
import functools

import jax
import jax.numpy as jnp
from jax import lax
from jax.experimental import pallas as pl
from jax.experimental.pallas import tpu as pltpu
from jax.sharding import PartitionSpec as P

VMEM = pl.BlockSpec(memory_space=pltpu.VMEM)
HBM = pl.BlockSpec(memory_space=pltpu.HBM)
EXTRA = 16
PARAMS = pltpu.CompilerParams(vmem_limit_bytes=32 * 1024 * 1024)


def partner(x, axis, mask):
    return lax.ppermute(x, axis, [(i, i ^ mask) for i in range(lax.axis_size(axis))])


def dot_nn(left, right):
    return lax.dot_general(
        left, right, (((1,), (0,)), ((), ())), preferred_element_type=jnp.float32
    )


def dot_nt(left, right):
    return lax.dot_general(
        left, right, (((1,), (1,)), ((), ())), preferred_element_type=jnp.float32
    )


def at_quarter(index, width):
    return pl.ds(pl.multiple_of(index * width, width), width)


def packet_rows(rows):
    return 2 * rows + EXTRA


def put_pair(ref, first, value):
    count, lanes = value.shape
    high = value.astype(jnp.bfloat16).astype(jnp.float32)
    both = jnp.concatenate([high, value - high], 0)
    both = jnp.concatenate([both, jnp.zeros((EXTRA - 2 * count, lanes), jnp.float32)], 0)
    ref[first : first + EXTRA, :lanes] = both.astype(ref.dtype)


def get_pair(ref, first, count):
    both = ref[first : first + EXTRA, :].astype(jnp.float32)
    return both[:count] + both[count : 2 * count]


def prologue_kernel(routed, gate, up, down, *refs):
    if routed:
        tokens, cotangent, ids, prob, keep, give, own, same, other = refs[:9]
        held, ids_row, prob_row, sems = refs[9:]
        parts = ((tokens, held.at[0]), (cotangent, held.at[1]), (ids, ids_row), (prob, prob_row))
    else:
        keep, give, sems = refs
        parts = ()
    half = keep.shape[1]
    x_bit = lax.axis_index("wide") % 2
    keep_rows = pl.ds(pl.multiple_of(x_bit * half, 16), half)
    give_rows = pl.ds(pl.multiple_of((1 - x_bit) * half, 16), half)
    for i, ref in enumerate((gate, up, down)):
        parts += ((ref.at[keep_rows, :], keep.at[i]), (ref.at[give_rows, :], give.at[i]))
    copies = [pltpu.make_async_copy(src, dst, sems.at[i]) for i, (src, dst) in enumerate(parts)]
    for copy in copies:
        copy.start()
    if routed:
        for copy in copies[:4]:
            copy.wait()
        rows = held.shape[1]
        width = same.shape[2]
        mine = lax.axis_index("wide") // 4
        column = at_quarter(lax.axis_index("narrow"), width)
        chosen = jnp.broadcast_to(ids_row[...], (128, rows)).astype(jnp.float32).T[:, :1]
        weight = jnp.broadcast_to(prob_row[...], (128, rows)).T[:, :1]
        here = jnp.where(chosen == mine.astype(jnp.float32), 1.0, 0.0)
        for i in range(2):
            factor = weight if i else jnp.ones_like(weight)
            own[i] = (held[i].astype(jnp.float32) * (factor * here)).astype(jnp.bfloat16)
            part = held[i, :, column].astype(jnp.float32)
            same[i] = (part * (factor * here)).astype(jnp.bfloat16)
            other[i] = (part * (factor * (1.0 - here))).astype(jnp.bfloat16)
    for copy in copies[len(copies) - 6 :]:
        copy.wait()


def prologue(weights, token_args, width):
    hidden, quarter = weights[0].shape
    half = jax.ShapeDtypeStruct((3, hidden // 2, quarter), jnp.bfloat16)
    outs, scratch = (half, half), []
    if token_args:
        rows, features = token_args[0].shape
        part = jax.ShapeDtypeStruct((2, rows, width), jnp.bfloat16)
        outs += (jax.ShapeDtypeStruct((2, rows, features), jnp.bfloat16), part, part)
        scratch = [
            pltpu.VMEM((2, rows, features), jnp.bfloat16),
            pltpu.VMEM((1, rows), jnp.int32),
            pltpu.VMEM((1, rows), jnp.float32),
        ]
    return pl.pallas_call(
        functools.partial(prologue_kernel, bool(token_args)),
        out_shape=outs,
        in_specs=[HBM] * (3 + len(token_args)),
        out_specs=[VMEM] * len(outs),
        scratch_shapes=scratch + [pltpu.SemaphoreType.DMA((10,))],
        compiler_params=PARAMS,
    )(*[pltpu.with_memory_space_constraint(x, pltpu.HBM) for x in (*weights, *token_args)])


def gather_kernel(has_own, *refs):
    own = refs[0] if has_own else None
    pieces, weights = refs[has_own : has_own + 4], refs[has_own + 4 : has_own + 7]
    x_all, s_all, w_all, part = refs[has_own + 7 :]
    blocks, _, slots, width = pieces[0].shape
    member = lax.axis_index("wide") % 4
    place = lax.axis_index("narrow")
    for k, ref in enumerate(weights):
        column = at_quarter(member ^ k, width)
        for i in range(3):
            w_all[i, :, column] = ref[i]
    first = 0
    if has_own:
        x_all[:slots, :] = own[0]
        s_all[:slots, :] = own[1]
        first = slots
    for mask, ref in enumerate(pieces):
        column = at_quarter(place ^ mask, width)
        for block in range(blocks):
            rows = slice(first + block * slots, first + (block + 1) * slots)
            x_all[rows, column] = ref[block, 0]
            s_all[rows, column] = ref[block, 1]
    total = x_all.shape[0]
    tile = min(256, total)

    @pl.loop(0, total // tile)
    def _(step):
        rows = pl.ds(pl.multiple_of(step * tile, tile), tile)
        for i in range(3):
            held = s_all if i == 2 else x_all
            sums = None
            for k in range(3):
                column = at_quarter(member ^ k, width)
                term = dot_nt(w_all[i, :, column], held[rows, column])
                sums = term if sums is None else sums + term
            part[i, :, rows] = sums


def gather_parts(own, pieces, weights):
    blocks, _, slots, width = pieces[0].shape
    half = weights[0].shape[1]
    has_own = own is not None
    total = (blocks + has_own) * slots
    features = 4 * width
    return pl.pallas_call(
        functools.partial(gather_kernel, int(has_own)),
        out_shape=(
            jax.ShapeDtypeStruct((total, features), jnp.bfloat16),
            jax.ShapeDtypeStruct((total, features), jnp.bfloat16),
            jax.ShapeDtypeStruct((3, half, features), jnp.bfloat16),
            jax.ShapeDtypeStruct((3, half, total), jnp.float32),
        ),
        in_specs=[VMEM] * (7 + has_own),
        out_specs=[VMEM] * 4,
        compiler_params=PARAMS,
        cost_estimate=pl.CostEstimate(flops=1, bytes_accessed=1, transcendentals=0),
    )(*([own] if has_own else []), *pieces, *weights)


def grad_parts(units, x_all, s_all, column, outs):
    half, total = units.shape[1:]
    both = dot_nn(units[0:2].reshape(2 * half, total), x_all[:, column])
    down = dot_nn(units[2], s_all[:, column])
    for i, value in enumerate((both[:half], both[half:], down)):
        out = outs[0] if i < 2 else outs[-1]
        out[i if len(outs) == 1 else i % 2] = value.astype(out.dtype)


def outer_kernel(x_all, s_all, w_part, part, last, units, kept, sent, *refs):
    to_d, w_all = refs[:2], refs[2]
    width = last.shape[2]
    place = lax.axis_index("narrow")
    last_column = at_quarter(lax.axis_index("wide") % 4 ^ 3, width)
    w_all[...] = w_part[...]
    for i in range(3):
        w_all[i, :, last_column] = last[i]
    total = x_all.shape[0]
    tile = min(width, total)
    for ref in (kept, sent):
        ref[:, 2 * total :, :] = jnp.zeros_like(ref[:, 2 * total :, :])
    routers = []
    for step in range(total // tile):
        rows = slice(step * tile, (step + 1) * tile)
        lower = slice(total + step * tile, total + (step + 1) * tile)
        x_tile, s_tile = x_all[rows, last_column], s_all[rows, last_column]
        gate = part[0, :, rows] + dot_nt(last[0], x_tile)
        up = part[1, :, rows] + dot_nt(last[1], x_tile)
        d_hidden = part[2, :, rows] + dot_nt(last[2], s_tile)
        sigma = 0.5 + 0.5 * jnp.tanh(0.5 * gate)
        active = gate * sigma
        hidden = (active * up).astype(jnp.bfloat16)
        slope = sigma + active * (1.0 - sigma)
        d_gate = (d_hidden * up * slope).astype(jnp.bfloat16)
        d_up = (d_hidden * active).astype(jnp.bfloat16)
        units[0, :, rows] = d_gate
        units[1, :, rows] = d_up
        units[2, :, rows] = hidden
        router = jnp.sum(hidden.astype(jnp.float32) * d_hidden, axis=0, keepdims=True)
        kept[0, 2 * total + step : 2 * total + step + 1, :tile] = router
        routers.append(router)
        hidden_t, d_both = hidden.T, jnp.concatenate([d_gate, d_up], 0).T
        for mask in range(4):
            column = at_quarter(place ^ mask, width)
            target = sent if mask % 2 else kept
            out_part = dot_nn(hidden_t, w_all[2, :, column])
            in_part = dot_nn(d_both, w_all[0:2, :, column].reshape(2 * hidden.shape[0], width))
            target[mask // 2, rows, :] = out_part.astype(target.dtype)
            target[mask // 2, lower, :] = in_part.astype(target.dtype)
    put_pair(sent.at[0], 2 * total, jnp.concatenate(routers, 0))
    grad_parts(units, x_all, s_all, last_column, to_d)


def outer(x_all, s_all, w_part, part, last):
    total, features = x_all.shape
    _, half, width = last.shape
    return pl.pallas_call(
        outer_kernel,
        out_shape=(
            jax.ShapeDtypeStruct((3, half, total), jnp.bfloat16),
            jax.ShapeDtypeStruct((2, packet_rows(total), width), jnp.float32),
            jax.ShapeDtypeStruct((2, packet_rows(total), width), jnp.bfloat16),
            jax.ShapeDtypeStruct((2, half, width), jnp.bfloat16),
            jax.ShapeDtypeStruct((1, half, width), jnp.bfloat16),
        ),
        in_specs=[VMEM] * 5,
        out_specs=[VMEM] * 5,
        scratch_shapes=[pltpu.VMEM((3, half, features), jnp.bfloat16)],
        compiler_params=PARAMS,
        cost_estimate=pl.CostEstimate(
            flops=8 * half * features * total, bytes_accessed=0, transcendentals=0
        ),
    )(x_all, s_all, w_part, part, last)


def grads_kernel(units, x_all, s_all, own, to_x, to_x_down, to_z):
    width = own.shape[2]
    member = lax.axis_index("wide") % 4
    for k, outs in enumerate(((own,), (to_x, to_x_down), (to_z,))):
        grad_parts(units, x_all, s_all, at_quarter(member ^ k, width), outs)


def weight_grads(units, x_all, s_all):
    half, total = units.shape[1:]
    features = x_all.shape[1]
    shapes = ((3, jnp.float32), (2, jnp.float32), (1, jnp.float32), (3, jnp.bfloat16))
    return pl.pallas_call(
        grads_kernel,
        out_shape=tuple(
            jax.ShapeDtypeStruct((count, half, features // 4), kind) for count, kind in shapes
        ),
        in_specs=[VMEM] * 3,
        out_specs=[VMEM] * 4,
        compiler_params=PARAMS,
        cost_estimate=pl.CostEstimate(flops=5 * half * features * total, bytes_accessed=0, transcendentals=0),
    )(units, x_all, s_all)


def join_kernel(own, got_x, got_x_down, out_0, out_1, out_2, held, sems):
    half = held.shape[1]
    x_bit = lax.axis_index("wide") % 2
    copies = []
    for part, held_part in enumerate((own, held)):
        first = (part * (1 - x_bit) + (1 - part) * x_bit) * half
        rows = pl.ds(pl.multiple_of(first, 16), half)
        for i, out in enumerate((out_0, out_1, out_2)):
            if part:
                got = got_x.at[i] if i < 2 else got_x_down.at[0]
                held[i] = got[...].astype(jnp.float32)
            place = sems.at[3 * part + i]
            copies.append(pltpu.make_async_copy(held_part.at[i], out.at[rows, :], place))
            copies[-1].start()
    for copy in copies:
        copy.wait()


def join_grads(own, got_x, got_x_down):
    _, half, width = own.shape
    shape = jax.ShapeDtypeStruct((2 * half, width), jnp.float32)
    return pl.pallas_call(
        join_kernel,
        out_shape=(shape,) * 3,
        in_specs=[VMEM] * 3,
        out_specs=[HBM] * 3,
        scratch_shapes=[
            pltpu.VMEM(own.shape, jnp.float32),
            pltpu.SemaphoreType.DMA((6,)),
        ],
        compiler_params=PARAMS,
        cost_estimate=pl.CostEstimate(flops=1, bytes_accessed=0, transcendentals=0),
    )(own, got_x, got_x_down)


def cross_kernel(kept, got, sent):
    total = (kept.shape[1] - EXTRA) // 2
    tile = min(kept.shape[2], total)
    count = total // tile
    body = slice(0, 2 * total)
    sent[body, :] = (kept[1, body, :] + got[1, body, :].astype(jnp.float32)).astype(sent.dtype)
    sent[2 * total :, :] = jnp.zeros_like(sent[2 * total :, :])
    router = kept[0, 2 * total : 2 * total + count, :] + get_pair(got.at[0], 2 * total, count)
    put_pair(sent, 2 * total, router)


def cross_part(kept, got):
    return pl.pallas_call(
        cross_kernel,
        out_shape=jax.ShapeDtypeStruct(got.shape[1:], got.dtype),
        in_specs=[VMEM] * 2,
        out_specs=VMEM,
        compiler_params=PARAMS,
    )(kept, got)


def result_kernel(kept, got, across, out):
    total = (kept.shape[1] - EXTRA) // 2
    count = total // min(kept.shape[2], total)
    body, tail = slice(0, 2 * total), slice(2 * total, 2 * total + count)
    value = kept[0, body, :] + got[0, body, :].astype(jnp.float32)
    out[body, :] = value + across[body, :].astype(jnp.float32)
    out[2 * total :, :] = jnp.zeros_like(out[2 * total :, :])
    router = kept[0, tail, :] + get_pair(got.at[0], 2 * total, count)
    out[tail, :] = router + get_pair(across, 2 * total, count)


def result_parts(kept, got, across):
    return pl.pallas_call(
        result_kernel,
        out_shape=jax.ShapeDtypeStruct(kept.shape[1:], jnp.float32),
        in_specs=[VMEM] * 3,
        out_specs=VMEM,
        compiler_params=PARAMS,
    )(kept, got, across)


def first_kernel(kept, got, to_y, to_x):
    total = (kept.shape[1] - EXTRA) // 2
    slots = total // 4
    count = total // min(kept.shape[2], total)
    body = slice(0, total)
    to_y[body, :] = (kept[1, body, :] + got[1, body, :].astype(jnp.float32)).astype(to_y.dtype)
    put_pair(
        to_y,
        total,
        kept[0, 2 * total : 2 * total + count, :] + get_pair(got.at[0], 2 * total, count),
    )
    for part in range(2):
        for block in range(2):
            rows = slice(total + (2 * block + 1) * slots, total + (2 * block + 2) * slots)
            value = kept[part, rows, :] + got[part, rows, :].astype(jnp.float32)
            to_x[part, block * slots : (block + 1) * slots, :] = value.astype(to_x.dtype)


def first_parts(kept, got):
    total, width = (kept.shape[1] - EXTRA) // 2, kept.shape[2]
    return pl.pallas_call(
        first_kernel,
        out_shape=(
            jax.ShapeDtypeStruct((total + EXTRA, width), jnp.bfloat16),
            jax.ShapeDtypeStruct((2, total // 2, width), jnp.bfloat16),
        ),
        in_specs=[VMEM] * 2,
        out_specs=[VMEM] * 2,
        compiler_params=PARAMS,
    )(kept, got)


def ffn_kernel(kept, got, from_y, held, to_x):
    total = (kept.shape[1] - EXTRA) // 2
    slots, width = total // 4, kept.shape[2]
    count = total // min(width, total)
    router = kept[0, 2 * total : 2 * total + count, :] + get_pair(got.at[0], 2 * total, count)
    router = router + get_pair(from_y, total, count)
    pairs = []
    for block in range(4):
        rows = slice(block * slots, (block + 1) * slots)
        value = kept[0, rows, :] + got[0, rows, :].astype(jnp.float32)
        value = value + from_y[rows, :].astype(jnp.float32)
        out = to_x if block % 2 else held
        place = block // 2
        out[place * slots : (place + 1) * slots, :] = value.astype(out.dtype)
        lane = block * slots % width
        pairs.append(router[block * slots // width :, lane : lane + slots][:1])
    held[2 * slots :, :] = jnp.zeros_like(held[2 * slots :, :])
    to_x[2 * slots :, :] = jnp.zeros_like(to_x[2 * slots :, :])
    held[2 * slots : 2 * slots + 1, :slots] = pairs[0]
    held[2 * slots + 1 : 2 * slots + 2, :slots] = pairs[2]
    put_pair(to_x, 2 * slots, jnp.concatenate([pairs[1], pairs[3]], 0))


def ffn_parts(kept, got, from_y):
    total, width = (kept.shape[1] - EXTRA) // 2, kept.shape[2]
    shape = (total // 2 + EXTRA, width)
    return pl.pallas_call(
        ffn_kernel,
        out_shape=(
            jax.ShapeDtypeStruct(shape, jnp.float32),
            jax.ShapeDtypeStruct(shape, jnp.bfloat16),
        ),
        in_specs=[VMEM] * 3,
        out_specs=[VMEM] * 2,
        compiler_params=PARAMS,
    )(kept, got, from_y)


def input_kernel(kept, got, from_x, held, to_y):
    total = (kept.shape[1] - EXTRA) // 2
    slots = total // 4
    for part, out in enumerate((held, to_y)):
        for block in range(2):
            rows = slice(total + 2 * block * slots, total + (2 * block + 1) * slots)
            here = slice(block * slots, (block + 1) * slots)
            value = kept[part, rows, :] + got[part, rows, :].astype(jnp.float32)
            out[here, :] = (value + from_x[part, here, :].astype(jnp.float32)).astype(out.dtype)


def input_parts(kept, got, from_x):
    shape = from_x.shape[1:]
    return pl.pallas_call(
        input_kernel,
        out_shape=(
            jax.ShapeDtypeStruct(shape, jnp.float32),
            jax.ShapeDtypeStruct(shape, jnp.bfloat16),
        ),
        in_specs=[VMEM] * 3,
        out_specs=[VMEM] * 2,
        compiler_params=PARAMS,
    )(kept, got, from_x)


def last_kernel(ffn, from_x, grad, from_y, held, to_z):
    slots = grad.shape[0] // 2
    router = ffn[2 * slots : 2 * slots + 2, :] + get_pair(from_x, 2 * slots, 2)
    for block, out in enumerate((held, to_z)):
        rows = slice(block * slots, (block + 1) * slots)
        out[:slots, :] = (ffn[rows, :] + from_x[rows, :].astype(jnp.float32)).astype(out.dtype)
        out[slots : 2 * slots, :] = (grad[rows, :] + from_y[rows, :].astype(jnp.float32)).astype(
            out.dtype
        )
    held[2 * slots :, :] = jnp.broadcast_to(router[:1], (EXTRA, router.shape[1]))
    put_pair(to_z, 2 * slots, router[1:])


def last_parts(ffn, from_x, grad, from_y):
    return pl.pallas_call(
        last_kernel,
        out_shape=(
            jax.ShapeDtypeStruct(ffn.shape, jnp.float32),
            jax.ShapeDtypeStruct(ffn.shape, jnp.bfloat16),
        ),
        in_specs=[VMEM] * 4,
        out_specs=[VMEM] * 2,
        compiler_params=PARAMS,
        cost_estimate=pl.CostEstimate(flops=2 * 10**9, bytes_accessed=0, transcendentals=0),
    )(ffn, from_x, grad, from_y)


def finish_kernel(prob, own, *refs):
    got, (output, tokens_grad, prob_grad) = refs[:-3], refs[-3:]
    slots, width = output.shape
    ffn, grad = own[:slots, :], own[slots : 2 * slots, :]
    router = own[2 * slots : 2 * slots + 1, :]
    for ref in got:
        ffn = ffn + ref[:slots, :].astype(jnp.float32)
        grad = grad + ref[slots : 2 * slots, :].astype(jnp.float32)
        router = router + get_pair(ref, 2 * slots, 1)
    weight = jnp.broadcast_to(prob[...], (128, slots)).T[:, :1]
    output[...] = (ffn.astype(jnp.bfloat16).astype(jnp.float32) * weight).astype(jnp.bfloat16)
    tokens_grad[...] = grad.astype(jnp.bfloat16)
    prob_grad[...] = router[:, :slots] / prob[...]


def finish(prob, own, got):
    slots, width = (own.shape[0] - EXTRA) // 2, own.shape[1]
    part = jax.ShapeDtypeStruct((slots, width), jnp.bfloat16)
    return pl.pallas_call(
        finish_kernel,
        out_shape=(part, part, jax.ShapeDtypeStruct((1, slots), jnp.float32)),
        in_specs=[VMEM] * (2 + len(got)),
        out_specs=[VMEM] * 3,
        compiler_params=PARAMS,
    )(prob, own, *got)


def shards(tokens, cotangent, expert_ids, route_prob, gate_weight, up_weight, down_weight):
    wide_count = lax.axis_size("wide")
    narrow_count = lax.axis_size("narrow")
    expert_count = wide_count // 4
    tok_rows, features = tokens.shape
    width = features // narrow_count
    slots = min(4 * tok_rows // expert_count, tok_rows)
    direct = expert_count == 2 and slots == tok_rows
    place = lax.axis_index("narrow")
    masks = (1, 4, 5)
    groups = [
        [4 * e + 2 * b + a for e in range(expert_count) for a in range(2)] for b in range(2)
    ]

    weights = (gate_weight.T, up_weight.T, down_weight.T)
    if direct:
        keep, give, own, same, other = prologue(
            weights, (tokens, cotangent, expert_ids.T, route_prob[None, :]), width
        )
        mine = jnp.stack(
            [partner(part, "wide", mask) for mask, part in zip(masks, (same, other, other))]
        )
    else:
        own = None
        keep, give = prologue(weights, (), width)
        chosen = expert_ids[:, 0]
        onehot = (chosen[:, None] == jnp.arange(expert_count, dtype=jnp.int32)[None, :]).astype(
            jnp.int32
        )
        rank = jnp.sum((jnp.cumsum(onehot, axis=0) - onehot) * onehot, axis=1)
        slot_place = chosen * slots + rank
        source = (
            jnp.full((expert_count * slots,), tok_rows, jnp.int32)
            .at[slot_place]
            .set(jnp.arange(tok_rows, dtype=jnp.int32))
        )
        scaled = (route_prob[:, None] * cotangent.astype(jnp.float32)).astype(jnp.bfloat16)
        both = jnp.stack([tokens, scaled])
        both = lax.dynamic_slice_in_dim(both, place * width, width, 2)
        both = jnp.concatenate([both, jnp.zeros((2, 1, width), jnp.bfloat16)], 1)
        routed = both[:, source].reshape(2, expert_count, slots, width).transpose(1, 0, 2, 3)
        routed = jnp.repeat(routed, 2, axis=0)
        mine = lax.all_to_all(
            routed, "wide", split_axis=0, concat_axis=0, axis_index_groups=groups, tiled=True
        )

    from_x, from_z = lax.optimization_barrier(
        (partner(give, "wide", 1), partner(keep, "wide", 2))
    )
    from_d = partner(from_x, "wide", 2)
    across = partner(mine, "narrow", 2)
    pieces = (mine, partner(mine, "narrow", 1), across, partner(across, "narrow", 1))
    x_all, s_all, w_part, part = gather_parts(own, pieces, (keep, from_x, from_z))
    units, kept, sent, grad_d, grad_d_down = outer(x_all, s_all, w_part, part, from_d)
    got = partner(sent, "narrow", 1)
    got_d_down = partner(grad_d_down, "wide", 2)
    got_d = partner(grad_d, "wide", 2)
    if direct:
        to_y, to_x = first_parts(kept, got)
        units, _ = lax.optimization_barrier((units, to_y))
        ffn_held, ffn_x = ffn_parts(kept, got, partner(to_y, "narrow", 2))
        grad_own, grad_x, grad_x_down, grad_z = weight_grads(units, x_all, s_all)
        from_x = partner(to_x, "wide", 1)
        grad_held, grad_y = input_parts(kept, got, from_x)
        grad_z, _ = lax.optimization_barrier((grad_z, from_x))
        grad_x, _, _ = lax.optimization_barrier((grad_x, ffn_x, grad_y))
        grad_x_down = (grad_x_down + got_d_down.astype(jnp.float32)).astype(jnp.bfloat16)
        got_x_down = partner(grad_x_down, "wide", 1)
        grad_held, got_x_down = lax.optimization_barrier((grad_held, got_x_down))
        held, to_z = last_parts(
            ffn_held, partner(ffn_x, "wide", 1), grad_held, partner(grad_y, "narrow", 2)
        )
        grad_x = (grad_x + got_d.astype(jnp.float32)).astype(jnp.bfloat16)
        got_x = partner(grad_x, "wide", 1)
        held, got_x = lax.optimization_barrier((held, got_x))
        output, tokens_grad, prob_grad = finish(
            route_prob[None, :], held, [partner(to_z, "wide", 4)]
        )
        prob_grad = prob_grad[0]
    else:
        grad_own, grad_x, grad_x_down, grad_z = weight_grads(units, x_all, s_all)
        grad_x_down = (grad_x_down + got_d_down.astype(jnp.float32)).astype(jnp.bfloat16)
        got_x_down = partner(grad_x_down, "wide", 1)
        grad_x = (grad_x + got_d.astype(jnp.float32)).astype(jnp.bfloat16)
        got_x = partner(grad_x, "wide", 1)
        across = partner(cross_part(kept, got), "narrow", 2)
        result = result_parts(kept, got, across)
        total = (result.shape[0] - EXTRA) // 2
        parts = result[: 2 * total].astype(jnp.bfloat16)
        parts = parts.reshape(2, 2 * expert_count, slots, width)
        back = lax.all_to_all(
            parts, "wide", split_axis=1, concat_axis=1, axis_index_groups=groups, tiled=True
        )
        back = back.reshape(2, expert_count, 2, slots, width).astype(jnp.float32).sum(2)
        back = back.reshape(2, expert_count * slots, width)[:, slot_place]
        router = result[2 * total : 2 * total + total // min(width, total), : min(width, total)]
        router = router.reshape(2 * expert_count, slots)
        high = lax.reduce_precision(router, 8, 7)
        pair = jnp.stack([high, router - high], 1).astype(jnp.bfloat16)
        pair = lax.all_to_all(
            pair, "wide", split_axis=0, concat_axis=0, axis_index_groups=groups, tiled=True
        )
        router = pair.reshape(expert_count, 4, slots).astype(jnp.float32).sum(1)
        prob_grad = router.reshape(expert_count * slots)[slot_place] / route_prob
        ffn = back[0].astype(jnp.bfloat16).astype(jnp.float32)
        output = (route_prob[:, None] * ffn).astype(jnp.bfloat16)
        tokens_grad = back[1].astype(jnp.bfloat16)
    got_z = partner(grad_z, "wide", 2)
    gate_grad, up_grad, down_grad = join_grads(
        grad_own + got_z.astype(jnp.float32), got_x, got_x_down
    )
    return (output, tokens_grad, prob_grad, gate_grad.T, up_grad.T, down_grad.T)


def solution(mesh):
    in_specs = (
        P("wide", None),
        P("wide", None),
        P("wide", None),
        P("wide"),
        P("wide", "narrow"),
        P("wide", "narrow"),
        P("wide", "narrow"),
    )
    out_specs = (
        P("wide", "narrow"),
        P("wide", "narrow"),
        P("wide"),
        P("wide", "narrow"),
        P("wide", "narrow"),
        P("wide", "narrow"),
    )
    return jax.shard_map(shards, mesh=mesh, in_specs=in_specs, out_specs=out_specs, check_vma=False)
```

```python
import functools

import jax
import jax.numpy as jnp
from jax import lax
from jax.experimental import pallas as pl
from jax.experimental.pallas import tpu as pltpu
from jax.sharding import PartitionSpec as P

VMEM = pl.BlockSpec(memory_space=pltpu.VMEM)
HBM = pl.BlockSpec(memory_space=pltpu.HBM)
EXTRA = 16
PARAMS = pltpu.CompilerParams(vmem_limit_bytes=32 * 1024 * 1024)


def partner(x, axis, mask):
    return lax.ppermute(x, axis, [(i, i ^ mask) for i in range(lax.axis_size(axis))])


def dot_nn(left, right):
    return lax.dot_general(
        left, right, (((1,), (0,)), ((), ())), preferred_element_type=jnp.float32
    )


def dot_nt(left, right):
    return lax.dot_general(
        left, right, (((1,), (1,)), ((), ())), preferred_element_type=jnp.float32
    )


def at_quarter(index, width):
    return pl.ds(pl.multiple_of(index * width, width), width)


def packet_rows(rows):
    return 2 * rows + EXTRA


def put_pair(ref, first, value):
    count, lanes = value.shape
    high = value.astype(jnp.bfloat16).astype(jnp.float32)
    both = jnp.concatenate([high, value - high], 0)
    both = jnp.concatenate([both, jnp.zeros((EXTRA - 2 * count, lanes), jnp.float32)], 0)
    ref[first : first + EXTRA, :lanes] = both.astype(ref.dtype)


def get_pair(ref, first, count):
    both = ref[first : first + EXTRA, :].astype(jnp.float32)
    return both[:count] + both[count : 2 * count]


def prologue_kernel(routed, gate, up, down, *refs):
    if routed:
        tokens, cotangent, ids, prob, keep, give, own, same, other = refs[:9]
        held, ids_row, prob_row, sems = refs[9:]
        parts = ((tokens, held.at[0]), (cotangent, held.at[1]), (ids, ids_row), (prob, prob_row))
    else:
        keep, give, sems = refs
        parts = ()
    half = keep.shape[1]
    x_bit = lax.axis_index("wide") % 2
    keep_rows = pl.ds(pl.multiple_of(x_bit * half, 16), half)
    give_rows = pl.ds(pl.multiple_of((1 - x_bit) * half, 16), half)
    for i, ref in enumerate((gate, up, down)):
        parts += ((ref.at[keep_rows, :], keep.at[i]), (ref.at[give_rows, :], give.at[i]))
    copies = [pltpu.make_async_copy(src, dst, sems.at[i]) for i, (src, dst) in enumerate(parts)]
    for copy in copies:
        copy.start()
    if routed:
        for copy in copies[:4]:
            copy.wait()
        rows = held.shape[1]
        width = same.shape[2]
        mine = lax.axis_index("wide") // 4
        column = at_quarter(lax.axis_index("narrow"), width)
        chosen = jnp.broadcast_to(ids_row[...], (128, rows)).astype(jnp.float32).T[:, :1]
        weight = jnp.broadcast_to(prob_row[...], (128, rows)).T[:, :1]
        here = jnp.where(chosen == mine.astype(jnp.float32), 1.0, 0.0)
        for i in range(2):
            factor = weight if i else jnp.ones_like(weight)
            own[i] = (held[i].astype(jnp.float32) * (factor * here)).astype(jnp.bfloat16)
            part = held[i, :, column].astype(jnp.float32)
            same[i] = (part * (factor * here)).astype(jnp.bfloat16)
            other[i] = (part * (factor * (1.0 - here))).astype(jnp.bfloat16)
    for copy in copies[len(copies) - 6 :]:
        copy.wait()


def prologue(weights, token_args, width):
    hidden, quarter = weights[0].shape
    half = jax.ShapeDtypeStruct((3, hidden // 2, quarter), jnp.bfloat16)
    outs, scratch = (half, half), []
    if token_args:
        rows, features = token_args[0].shape
        part = jax.ShapeDtypeStruct((2, rows, width), jnp.bfloat16)
        outs += (jax.ShapeDtypeStruct((2, rows, features), jnp.bfloat16), part, part)
        scratch = [
            pltpu.VMEM((2, rows, features), jnp.bfloat16),
            pltpu.VMEM((1, rows), jnp.int32),
            pltpu.VMEM((1, rows), jnp.float32),
        ]
    return pl.pallas_call(
        functools.partial(prologue_kernel, bool(token_args)),
        out_shape=outs,
        in_specs=[HBM] * (3 + len(token_args)),
        out_specs=[VMEM] * len(outs),
        scratch_shapes=scratch + [pltpu.SemaphoreType.DMA((10,))],
        compiler_params=PARAMS,
    )(*[pltpu.with_memory_space_constraint(x, pltpu.HBM) for x in (*weights, *token_args)])


def gather_kernel(has_own, *refs):
    own = refs[0] if has_own else None
    pieces, weights = refs[has_own : has_own + 4], refs[has_own + 4 : has_own + 7]
    x_all, s_all, w_all, part = refs[has_own + 7 :]
    blocks, _, slots, width = pieces[0].shape
    member = lax.axis_index("wide") % 4
    place = lax.axis_index("narrow")
    for k, ref in enumerate(weights):
        column = at_quarter(member ^ k, width)
        for i in range(3):
            w_all[i, :, column] = ref[i]
    first = 0
    if has_own:
        x_all[:slots, :] = own[0]
        s_all[:slots, :] = own[1]
        first = slots
    for mask, ref in enumerate(pieces):
        column = at_quarter(place ^ mask, width)
        for block in range(blocks):
            rows = slice(first + block * slots, first + (block + 1) * slots)
            x_all[rows, column] = ref[block, 0]
            s_all[rows, column] = ref[block, 1]
    total = x_all.shape[0]
    tile = min(256, total)

    @pl.loop(0, total // tile)
    def _(step):
        rows = pl.ds(pl.multiple_of(step * tile, tile), tile)
        for i in range(3):
            held = s_all if i == 2 else x_all
            sums = None
            for k in range(3):
                column = at_quarter(member ^ k, width)
                term = dot_nt(w_all[i, :, column], held[rows, column])
                sums = term if sums is None else sums + term
            part[i, :, rows] = sums


def gather_parts(own, pieces, weights):
    blocks, _, slots, width = pieces[0].shape
    half = weights[0].shape[1]
    has_own = own is not None
    total = (blocks + has_own) * slots
    features = 4 * width
    return pl.pallas_call(
        functools.partial(gather_kernel, int(has_own)),
        out_shape=(
            jax.ShapeDtypeStruct((total, features), jnp.bfloat16),
            jax.ShapeDtypeStruct((total, features), jnp.bfloat16),
            jax.ShapeDtypeStruct((3, half, features), jnp.bfloat16),
            jax.ShapeDtypeStruct((3, half, total), jnp.float32),
        ),
        in_specs=[VMEM] * (7 + has_own),
        out_specs=[VMEM] * 4,
        compiler_params=PARAMS,
        cost_estimate=pl.CostEstimate(flops=1, bytes_accessed=1, transcendentals=0),
    )(*([own] if has_own else []), *pieces, *weights)


def grad_parts(units, x_all, s_all, column, outs):
    half, total = units.shape[1:]
    both = dot_nn(units[0:2].reshape(2 * half, total), x_all[:, column])
    down = dot_nn(units[2], s_all[:, column])
    for i, value in enumerate((both[:half], both[half:], down)):
        out = outs[0] if i < 2 else outs[-1]
        out[i if len(outs) == 1 else i % 2] = value.astype(out.dtype)


def outer_kernel(x_all, s_all, w_part, part, last, units, kept, sent, *refs):
    to_d, w_all, sums = refs[:2], refs[2], refs[3]
    half, width = last.shape[1:]
    chunk = 32 if half % 32 == 0 else 16
    place = lax.axis_index("narrow")
    last_column = at_quarter(lax.axis_index("wide") % 4 ^ 3, width)
    w_all[...] = w_part[...]
    for i in range(3):
        w_all[i, :, last_column] = last[i]
    total = x_all.shape[0]
    tile = min(width, total)
    for ref in (kept, sent):
        ref[:, 2 * total :, :] = jnp.zeros_like(ref[:, 2 * total :, :])
    routers = []
    for step in range(total // tile):
        rows = slice(step * tile, (step + 1) * tile)
        lower = slice(total + step * tile, total + (step + 1) * tile)
        x_tile, s_tile = x_all[rows, last_column], s_all[rows, last_column]
        for i, held in enumerate((x_tile, x_tile, s_tile)):
            sums[i] = part[i, :, rows] + dot_nt(last[i], held)
        products = jnp.zeros((chunk, tile), jnp.float32)
        for low in range(0, half, chunk):
            piece = slice(low, low + chunk)
            gate, up, d_hidden = sums[0, piece, :], sums[1, piece, :], sums[2, piece, :]
            sigma = 0.5 + 0.5 * jnp.tanh(0.5 * gate)
            active = gate * sigma
            hidden = (active * up).astype(jnp.bfloat16)
            slope = sigma + active * (1.0 - sigma)
            units[0, piece, rows] = (d_hidden * up * slope).astype(jnp.bfloat16)
            units[1, piece, rows] = (d_hidden * active).astype(jnp.bfloat16)
            units[2, piece, rows] = hidden
            products = products + hidden.astype(jnp.float32) * d_hidden
        router = jnp.sum(products, axis=0, keepdims=True)
        kept[0, 2 * total + step : 2 * total + step + 1, :tile] = router
        routers.append(router)
        hidden_t, d_both = units[2, :, rows].T, units[0:2, :, rows].reshape(2 * half, tile).T
        for mask in range(4):
            column = at_quarter(place ^ mask, width)
            target = sent if mask % 2 else kept
            out_part = dot_nn(hidden_t, w_all[2, :, column])
            in_part = dot_nn(d_both, w_all[0:2, :, column].reshape(2 * half, width))
            target[mask // 2, rows, :] = out_part.astype(target.dtype)
            target[mask // 2, lower, :] = in_part.astype(target.dtype)
    put_pair(sent.at[0], 2 * total, jnp.concatenate(routers, 0))
    grad_parts(units, x_all, s_all, last_column, to_d)


def outer(x_all, s_all, w_part, part, last):
    total, features = x_all.shape
    _, half, width = last.shape
    return pl.pallas_call(
        outer_kernel,
        out_shape=(
            jax.ShapeDtypeStruct((3, half, total), jnp.bfloat16),
            jax.ShapeDtypeStruct((2, packet_rows(total), width), jnp.float32),
            jax.ShapeDtypeStruct((2, packet_rows(total), width), jnp.bfloat16),
            jax.ShapeDtypeStruct((2, half, width), jnp.bfloat16),
            jax.ShapeDtypeStruct((1, half, width), jnp.bfloat16),
        ),
        in_specs=[VMEM] * 5,
        out_specs=[VMEM] * 5,
        scratch_shapes=[
            pltpu.VMEM((3, half, features), jnp.bfloat16),
            pltpu.VMEM((3, half, min(width, total)), jnp.float32),
        ],
        compiler_params=PARAMS,
        cost_estimate=pl.CostEstimate(
            flops=8 * half * features * total, bytes_accessed=0, transcendentals=0
        ),
    )(x_all, s_all, w_part, part, last)


def grads_kernel(units, x_all, s_all, own, to_x, to_x_down, to_z):
    width = own.shape[2]
    member = lax.axis_index("wide") % 4
    for k, outs in enumerate(((own,), (to_x, to_x_down), (to_z,))):
        grad_parts(units, x_all, s_all, at_quarter(member ^ k, width), outs)


def weight_grads(units, x_all, s_all):
    half, total = units.shape[1:]
    features = x_all.shape[1]
    shapes = ((3, jnp.float32), (2, jnp.float32), (1, jnp.float32), (3, jnp.bfloat16))
    return pl.pallas_call(
        grads_kernel,
        out_shape=tuple(
            jax.ShapeDtypeStruct((count, half, features // 4), kind) for count, kind in shapes
        ),
        in_specs=[VMEM] * 3,
        out_specs=[VMEM] * 4,
        compiler_params=PARAMS,
        cost_estimate=pl.CostEstimate(flops=5 * half * features * total, bytes_accessed=0, transcendentals=0),
    )(units, x_all, s_all)


def join_kernel(own, got_x, got_x_down, out_0, out_1, out_2, held, sems):
    half = held.shape[1]
    x_bit = lax.axis_index("wide") % 2
    copies = []
    for part, held_part in enumerate((own, held)):
        first = (part * (1 - x_bit) + (1 - part) * x_bit) * half
        rows = pl.ds(pl.multiple_of(first, 16), half)
        for i, out in enumerate((out_0, out_1, out_2)):
            if part:
                got = got_x.at[i] if i < 2 else got_x_down.at[0]
                held[i] = got[...].astype(jnp.float32)
            place = sems.at[3 * part + i]
            copies.append(pltpu.make_async_copy(held_part.at[i], out.at[rows, :], place))
            copies[-1].start()
    for copy in copies:
        copy.wait()


def join_grads(own, got_x, got_x_down):
    _, half, width = own.shape
    shape = jax.ShapeDtypeStruct((2 * half, width), jnp.float32)
    return pl.pallas_call(
        join_kernel,
        out_shape=(shape,) * 3,
        in_specs=[VMEM] * 3,
        out_specs=[HBM] * 3,
        scratch_shapes=[
            pltpu.VMEM(own.shape, jnp.float32),
            pltpu.SemaphoreType.DMA((6,)),
        ],
        compiler_params=PARAMS,
        cost_estimate=pl.CostEstimate(flops=1, bytes_accessed=0, transcendentals=0),
    )(own, got_x, got_x_down)


def cross_kernel(kept, got, sent):
    total = (kept.shape[1] - EXTRA) // 2
    tile = min(kept.shape[2], total)
    count = total // tile
    body = slice(0, 2 * total)
    sent[body, :] = (kept[1, body, :] + got[1, body, :].astype(jnp.float32)).astype(sent.dtype)
    sent[2 * total :, :] = jnp.zeros_like(sent[2 * total :, :])
    router = kept[0, 2 * total : 2 * total + count, :] + get_pair(got.at[0], 2 * total, count)
    put_pair(sent, 2 * total, router)


def cross_part(kept, got):
    return pl.pallas_call(
        cross_kernel,
        out_shape=jax.ShapeDtypeStruct(got.shape[1:], got.dtype),
        in_specs=[VMEM] * 2,
        out_specs=VMEM,
        compiler_params=PARAMS,
    )(kept, got)


def result_kernel(kept, got, across, out):
    total = (kept.shape[1] - EXTRA) // 2
    count = total // min(kept.shape[2], total)
    body, tail = slice(0, 2 * total), slice(2 * total, 2 * total + count)
    value = kept[0, body, :] + got[0, body, :].astype(jnp.float32)
    out[body, :] = value + across[body, :].astype(jnp.float32)
    out[2 * total :, :] = jnp.zeros_like(out[2 * total :, :])
    router = kept[0, tail, :] + get_pair(got.at[0], 2 * total, count)
    out[tail, :] = router + get_pair(across, 2 * total, count)


def result_parts(kept, got, across):
    return pl.pallas_call(
        result_kernel,
        out_shape=jax.ShapeDtypeStruct(kept.shape[1:], jnp.float32),
        in_specs=[VMEM] * 3,
        out_specs=VMEM,
        compiler_params=PARAMS,
    )(kept, got, across)


def first_kernel(kept, got, to_y, to_x):
    total = (kept.shape[1] - EXTRA) // 2
    slots = total // 4
    count = total // min(kept.shape[2], total)
    body = slice(0, total)
    to_y[body, :] = (kept[1, body, :] + got[1, body, :].astype(jnp.float32)).astype(to_y.dtype)
    put_pair(
        to_y,
        total,
        kept[0, 2 * total : 2 * total + count, :] + get_pair(got.at[0], 2 * total, count),
    )
    for part in range(2):
        for block in range(2):
            rows = slice(total + (2 * block + 1) * slots, total + (2 * block + 2) * slots)
            value = kept[part, rows, :] + got[part, rows, :].astype(jnp.float32)
            to_x[part, block * slots : (block + 1) * slots, :] = value.astype(to_x.dtype)


def first_parts(kept, got):
    total, width = (kept.shape[1] - EXTRA) // 2, kept.shape[2]
    return pl.pallas_call(
        first_kernel,
        out_shape=(
            jax.ShapeDtypeStruct((total + EXTRA, width), jnp.bfloat16),
            jax.ShapeDtypeStruct((2, total // 2, width), jnp.bfloat16),
        ),
        in_specs=[VMEM] * 2,
        out_specs=[VMEM] * 2,
        compiler_params=PARAMS,
    )(kept, got)


def ffn_kernel(kept, got, from_y, held, to_x):
    total = (kept.shape[1] - EXTRA) // 2
    slots, width = total // 4, kept.shape[2]
    count = total // min(width, total)
    router = kept[0, 2 * total : 2 * total + count, :] + get_pair(got.at[0], 2 * total, count)
    router = router + get_pair(from_y, total, count)
    pairs = []
    for block in range(4):
        rows = slice(block * slots, (block + 1) * slots)
        value = kept[0, rows, :] + got[0, rows, :].astype(jnp.float32)
        value = value + from_y[rows, :].astype(jnp.float32)
        out = to_x if block % 2 else held
        place = block // 2
        out[place * slots : (place + 1) * slots, :] = value.astype(out.dtype)
        lane = block * slots % width
        pairs.append(router[block * slots // width :, lane : lane + slots][:1])
    held[2 * slots :, :] = jnp.zeros_like(held[2 * slots :, :])
    to_x[2 * slots :, :] = jnp.zeros_like(to_x[2 * slots :, :])
    held[2 * slots : 2 * slots + 1, :slots] = pairs[0]
    held[2 * slots + 1 : 2 * slots + 2, :slots] = pairs[2]
    put_pair(to_x, 2 * slots, jnp.concatenate([pairs[1], pairs[3]], 0))


def ffn_parts(kept, got, from_y):
    total, width = (kept.shape[1] - EXTRA) // 2, kept.shape[2]
    shape = (total // 2 + EXTRA, width)
    return pl.pallas_call(
        ffn_kernel,
        out_shape=(
            jax.ShapeDtypeStruct(shape, jnp.float32),
            jax.ShapeDtypeStruct(shape, jnp.bfloat16),
        ),
        in_specs=[VMEM] * 3,
        out_specs=[VMEM] * 2,
        compiler_params=PARAMS,
    )(kept, got, from_y)


def input_kernel(kept, got, from_x, held, to_y):
    total = (kept.shape[1] - EXTRA) // 2
    slots = total // 4
    for part, out in enumerate((held, to_y)):
        for block in range(2):
            rows = slice(total + 2 * block * slots, total + (2 * block + 1) * slots)
            here = slice(block * slots, (block + 1) * slots)
            value = kept[part, rows, :] + got[part, rows, :].astype(jnp.float32)
            out[here, :] = (value + from_x[part, here, :].astype(jnp.float32)).astype(out.dtype)


def input_parts(kept, got, from_x):
    shape = from_x.shape[1:]
    return pl.pallas_call(
        input_kernel,
        out_shape=(
            jax.ShapeDtypeStruct(shape, jnp.float32),
            jax.ShapeDtypeStruct(shape, jnp.bfloat16),
        ),
        in_specs=[VMEM] * 3,
        out_specs=[VMEM] * 2,
        compiler_params=PARAMS,
    )(kept, got, from_x)


def last_kernel(ffn, from_x, grad, from_y, held, to_z):
    slots = grad.shape[0] // 2
    router = ffn[2 * slots : 2 * slots + 2, :] + get_pair(from_x, 2 * slots, 2)
    for block, out in enumerate((held, to_z)):
        rows = slice(block * slots, (block + 1) * slots)
        out[:slots, :] = (ffn[rows, :] + from_x[rows, :].astype(jnp.float32)).astype(out.dtype)
        out[slots : 2 * slots, :] = (grad[rows, :] + from_y[rows, :].astype(jnp.float32)).astype(
            out.dtype
        )
    held[2 * slots :, :] = jnp.broadcast_to(router[:1], (EXTRA, router.shape[1]))
    put_pair(to_z, 2 * slots, router[1:])


def last_parts(ffn, from_x, grad, from_y):
    return pl.pallas_call(
        last_kernel,
        out_shape=(
            jax.ShapeDtypeStruct(ffn.shape, jnp.float32),
            jax.ShapeDtypeStruct(ffn.shape, jnp.bfloat16),
        ),
        in_specs=[VMEM] * 4,
        out_specs=[VMEM] * 2,
        compiler_params=PARAMS,
        cost_estimate=pl.CostEstimate(flops=2 * 10**9, bytes_accessed=0, transcendentals=0),
    )(ffn, from_x, grad, from_y)


def finish_kernel(prob, own, *refs):
    got, (output, tokens_grad, prob_grad) = refs[:-3], refs[-3:]
    slots, width = output.shape
    ffn, grad = own[:slots, :], own[slots : 2 * slots, :]
    router = own[2 * slots : 2 * slots + 1, :]
    for ref in got:
        ffn = ffn + ref[:slots, :].astype(jnp.float32)
        grad = grad + ref[slots : 2 * slots, :].astype(jnp.float32)
        router = router + get_pair(ref, 2 * slots, 1)
    weight = jnp.broadcast_to(prob[...], (128, slots)).T[:, :1]
    output[...] = (ffn.astype(jnp.bfloat16).astype(jnp.float32) * weight).astype(jnp.bfloat16)
    tokens_grad[...] = grad.astype(jnp.bfloat16)
    prob_grad[...] = router[:, :slots] / prob[...]


def finish(prob, own, got):
    slots, width = (own.shape[0] - EXTRA) // 2, own.shape[1]
    part = jax.ShapeDtypeStruct((slots, width), jnp.bfloat16)
    return pl.pallas_call(
        finish_kernel,
        out_shape=(part, part, jax.ShapeDtypeStruct((1, slots), jnp.float32)),
        in_specs=[VMEM] * (2 + len(got)),
        out_specs=[VMEM] * 3,
        compiler_params=PARAMS,
    )(prob, own, *got)


def shards(tokens, cotangent, expert_ids, route_prob, gate_weight, up_weight, down_weight):
    wide_count = lax.axis_size("wide")
    narrow_count = lax.axis_size("narrow")
    expert_count = wide_count // 4
    tok_rows, features = tokens.shape
    width = features // narrow_count
    slots = min(4 * tok_rows // expert_count, tok_rows)
    direct = expert_count == 2 and slots == tok_rows
    place = lax.axis_index("narrow")
    masks = (1, 4, 5)
    groups = [
        [4 * e + 2 * b + a for e in range(expert_count) for a in range(2)] for b in range(2)
    ]

    weights = (gate_weight.T, up_weight.T, down_weight.T)
    if direct:
        keep, give, own, same, other = prologue(
            weights, (tokens, cotangent, expert_ids.T, route_prob[None, :]), width
        )
        mine = jnp.stack(
            [partner(part, "wide", mask) for mask, part in zip(masks, (same, other, other))]
        )
    else:
        own = None
        keep, give = prologue(weights, (), width)
        chosen = expert_ids[:, 0]
        onehot = (chosen[:, None] == jnp.arange(expert_count, dtype=jnp.int32)[None, :]).astype(
            jnp.int32
        )
        rank = jnp.sum((jnp.cumsum(onehot, axis=0) - onehot) * onehot, axis=1)
        slot_place = chosen * slots + rank
        source = (
            jnp.full((expert_count * slots,), tok_rows, jnp.int32)
            .at[slot_place]
            .set(jnp.arange(tok_rows, dtype=jnp.int32))
        )
        scaled = (route_prob[:, None] * cotangent.astype(jnp.float32)).astype(jnp.bfloat16)
        both = jnp.stack([tokens, scaled])
        both = lax.dynamic_slice_in_dim(both, place * width, width, 2)
        both = jnp.concatenate([both, jnp.zeros((2, 1, width), jnp.bfloat16)], 1)
        routed = both[:, source].reshape(2, expert_count, slots, width).transpose(1, 0, 2, 3)
        routed = jnp.repeat(routed, 2, axis=0)
        mine = lax.all_to_all(
            routed, "wide", split_axis=0, concat_axis=0, axis_index_groups=groups, tiled=True
        )

    from_x, from_z = lax.optimization_barrier(
        (partner(give, "wide", 1), partner(keep, "wide", 2))
    )
    from_d = partner(from_x, "wide", 2)
    across = partner(mine, "narrow", 2)
    pieces = (mine, partner(mine, "narrow", 1), across, partner(across, "narrow", 1))
    x_all, s_all, w_part, part = gather_parts(own, pieces, (keep, from_x, from_z))
    units, kept, sent, grad_d, grad_d_down = outer(x_all, s_all, w_part, part, from_d)
    got = partner(sent, "narrow", 1)
    got_d_down = partner(grad_d_down, "wide", 2)
    got_d = partner(grad_d, "wide", 2)
    if direct:
        to_y, to_x = first_parts(kept, got)
        units, _ = lax.optimization_barrier((units, to_y))
        ffn_held, ffn_x = ffn_parts(kept, got, partner(to_y, "narrow", 2))
        grad_own, grad_x, grad_x_down, grad_z = weight_grads(units, x_all, s_all)
        from_x = partner(to_x, "wide", 1)
        from_x, _ = lax.optimization_barrier((from_x, ffn_x))
        grad_held, grad_y = input_parts(kept, got, from_x)
        grad_z, _ = lax.optimization_barrier((grad_z, from_x))
        grad_x, _, _ = lax.optimization_barrier((grad_x, ffn_x, grad_y))
        grad_x_down = (grad_x_down + got_d_down.astype(jnp.float32)).astype(jnp.bfloat16)
        got_x_down = partner(grad_x_down, "wide", 1)
        grad_held, got_x_down = lax.optimization_barrier((grad_held, got_x_down))
        held, to_z = last_parts(
            ffn_held, partner(ffn_x, "wide", 1), grad_held, partner(grad_y, "narrow", 2)
        )
        grad_x = (grad_x + got_d.astype(jnp.float32)).astype(jnp.bfloat16)
        got_x = partner(grad_x, "wide", 1)
        held, got_x = lax.optimization_barrier((held, got_x))
        output, tokens_grad, prob_grad = finish(
            route_prob[None, :], held, [partner(to_z, "wide", 4)]
        )
        prob_grad = prob_grad[0]
    else:
        grad_own, grad_x, grad_x_down, grad_z = weight_grads(units, x_all, s_all)
        grad_x_down = (grad_x_down + got_d_down.astype(jnp.float32)).astype(jnp.bfloat16)
        got_x_down = partner(grad_x_down, "wide", 1)
        grad_x = (grad_x + got_d.astype(jnp.float32)).astype(jnp.bfloat16)
        got_x = partner(grad_x, "wide", 1)
        across = partner(cross_part(kept, got), "narrow", 2)
        result = result_parts(kept, got, across)
        total = (result.shape[0] - EXTRA) // 2
        parts = result[: 2 * total].astype(jnp.bfloat16)
        parts = parts.reshape(2, 2 * expert_count, slots, width)
        back = lax.all_to_all(
            parts, "wide", split_axis=1, concat_axis=1, axis_index_groups=groups, tiled=True
        )
        back = back.reshape(2, expert_count, 2, slots, width).astype(jnp.float32).sum(2)
        back = back.reshape(2, expert_count * slots, width)[:, slot_place]
        router = result[2 * total : 2 * total + total // min(width, total), : min(width, total)]
        router = router.reshape(2 * expert_count, slots)
        high = lax.reduce_precision(router, 8, 7)
        pair = jnp.stack([high, router - high], 1).astype(jnp.bfloat16)
        pair = lax.all_to_all(
            pair, "wide", split_axis=0, concat_axis=0, axis_index_groups=groups, tiled=True
        )
        router = pair.reshape(expert_count, 4, slots).astype(jnp.float32).sum(1)
        prob_grad = router.reshape(expert_count * slots)[slot_place] / route_prob
        ffn = back[0].astype(jnp.bfloat16).astype(jnp.float32)
        output = (route_prob[:, None] * ffn).astype(jnp.bfloat16)
        tokens_grad = back[1].astype(jnp.bfloat16)
    got_z = partner(grad_z, "wide", 2)
    gate_grad, up_grad, down_grad = join_grads(
        grad_own + got_z.astype(jnp.float32), got_x, got_x_down
    )
    return (output, tokens_grad, prob_grad, gate_grad.T, up_grad.T, down_grad.T)


def solution(mesh):
    in_specs = (
        P("wide", None),
        P("wide", None),
        P("wide", None),
        P("wide"),
        P("wide", "narrow"),
        P("wide", "narrow"),
        P("wide", "narrow"),
    )
    out_specs = (
        P("wide", "narrow"),
        P("wide", "narrow"),
        P("wide"),
        P("wide", "narrow"),
        P("wide", "narrow"),
        P("wide", "narrow"),
    )
    return jax.shard_map(shards, mesh=mesh, in_specs=in_specs, out_specs=out_specs, check_vma=False)
```

```python
import functools

import jax
import jax.numpy as jnp
from jax import lax
from jax.experimental import pallas as pl
from jax.experimental.pallas import tpu as pltpu
from jax.sharding import PartitionSpec as P

VMEM = pl.BlockSpec(memory_space=pltpu.VMEM)
HBM = pl.BlockSpec(memory_space=pltpu.HBM)
EXTRA = 16
PARAMS = pltpu.CompilerParams(vmem_limit_bytes=32 * 1024 * 1024)


def partner(x, axis, mask):
    return lax.ppermute(x, axis, [(i, i ^ mask) for i in range(lax.axis_size(axis))])


def dot_nn(left, right):
    return lax.dot_general(
        left, right, (((1,), (0,)), ((), ())), preferred_element_type=jnp.float32
    )


def dot_nt(left, right):
    return lax.dot_general(
        left, right, (((1,), (1,)), ((), ())), preferred_element_type=jnp.float32
    )


def at_quarter(index, width):
    return pl.ds(pl.multiple_of(index * width, width), width)


def packet_rows(rows):
    return 2 * rows + EXTRA


def put_pair(ref, first, value):
    count, lanes = value.shape
    high = value.astype(jnp.bfloat16).astype(jnp.float32)
    both = jnp.concatenate([high, value - high], 0)
    both = jnp.concatenate([both, jnp.zeros((EXTRA - 2 * count, lanes), jnp.float32)], 0)
    ref[first : first + EXTRA, :lanes] = both.astype(ref.dtype)


def get_pair(ref, first, count):
    both = ref[first : first + EXTRA, :].astype(jnp.float32)
    return both[:count] + both[count : 2 * count]


def prologue_kernel(routed, gate, up, down, *refs):
    if routed:
        tokens, cotangent, ids, prob, keep, give, own, same, other = refs[:9]
        held, ids_row, prob_row, sems = refs[9:]
        parts = ((tokens, held.at[0]), (cotangent, held.at[1]), (ids, ids_row), (prob, prob_row))
    else:
        keep, give, sems = refs
        parts = ()
    half = keep.shape[1]
    x_bit = lax.axis_index("wide") % 2
    keep_rows = pl.ds(pl.multiple_of(x_bit * half, 16), half)
    give_rows = pl.ds(pl.multiple_of((1 - x_bit) * half, 16), half)
    for i, ref in enumerate((gate, up, down)):
        parts += ((ref.at[keep_rows, :], keep.at[i]), (ref.at[give_rows, :], give.at[i]))
    copies = [pltpu.make_async_copy(src, dst, sems.at[i]) for i, (src, dst) in enumerate(parts)]
    for copy in copies:
        copy.start()
    if routed:
        for copy in copies[:4]:
            copy.wait()
        rows = held.shape[1]
        width = same.shape[2]
        mine = lax.axis_index("wide") // 4
        column = at_quarter(lax.axis_index("narrow"), width)
        chosen = jnp.broadcast_to(ids_row[...], (128, rows)).astype(jnp.float32).T[:, :1]
        weight = jnp.broadcast_to(prob_row[...], (128, rows)).T[:, :1]
        here = jnp.where(chosen == mine.astype(jnp.float32), 1.0, 0.0)
        for i in range(2):
            factor = weight if i else jnp.ones_like(weight)
            own[i] = (held[i].astype(jnp.float32) * (factor * here)).astype(jnp.bfloat16)
            part = held[i, :, column].astype(jnp.float32)
            same[i] = (part * (factor * here)).astype(jnp.bfloat16)
            other[i] = (part * (factor * (1.0 - here))).astype(jnp.bfloat16)
    for copy in copies[len(copies) - 6 :]:
        copy.wait()


def prologue(weights, token_args, width):
    hidden, quarter = weights[0].shape
    half = jax.ShapeDtypeStruct((3, hidden // 2, quarter), jnp.bfloat16)
    outs, scratch = (half, half), []
    if token_args:
        rows, features = token_args[0].shape
        part = jax.ShapeDtypeStruct((2, rows, width), jnp.bfloat16)
        outs += (jax.ShapeDtypeStruct((2, rows, features), jnp.bfloat16), part, part)
        scratch = [
            pltpu.VMEM((2, rows, features), jnp.bfloat16),
            pltpu.VMEM((1, rows), jnp.int32),
            pltpu.VMEM((1, rows), jnp.float32),
        ]
    return pl.pallas_call(
        functools.partial(prologue_kernel, bool(token_args)),
        out_shape=outs,
        in_specs=[HBM] * (3 + len(token_args)),
        out_specs=[VMEM] * len(outs),
        scratch_shapes=scratch + [pltpu.SemaphoreType.DMA((10,))],
        compiler_params=PARAMS,
    )(*[pltpu.with_memory_space_constraint(x, pltpu.HBM) for x in (*weights, *token_args)])


def gather_kernel(has_own, *refs):
    own = refs[0] if has_own else None
    pieces, weights = refs[has_own : has_own + 4], refs[has_own + 4 : has_own + 7]
    x_all, s_all, w_all, part = refs[has_own + 7 :]
    blocks, _, slots, width = pieces[0].shape
    half, reach = w_all.shape[1:]
    member = lax.axis_index("wide") % 4
    place = lax.axis_index("narrow")
    for k, ref in enumerate(weights):
        for i in range(3):
            w_all[i, :, k * width : (k + 1) * width] = ref[i]
    first = 0
    if has_own:
        for k in range(4):
            column = at_quarter(member ^ k, width)
            x_all[:slots, k * width : (k + 1) * width] = own[0, :, column]
            s_all[:slots, k * width : (k + 1) * width] = own[1, :, column]
        first = slots
    for mask, ref in enumerate(pieces):
        column = at_quarter(place ^ member ^ mask, width)
        for block in range(blocks):
            rows = slice(first + block * slots, first + (block + 1) * slots)
            x_all[rows, column] = ref[block, 0]
            s_all[rows, column] = ref[block, 1]
    total = x_all.shape[0]
    tile = min(2 * width, total)
    for step in range(total // tile):
        rows = slice(step * tile, (step + 1) * tile)
        both = dot_nt(w_all[0:2].reshape(2 * half, reach), x_all[rows, :reach])
        part[0:2, :, rows] = both.reshape(2, half, tile)
        part[2, :, rows] = dot_nt(w_all[2], s_all[rows, :reach])


def gather_parts(own, pieces, weights):
    blocks, _, slots, width = pieces[0].shape
    half = weights[0].shape[1]
    has_own = own is not None
    total = (blocks + has_own) * slots
    features = 4 * width
    return pl.pallas_call(
        functools.partial(gather_kernel, int(has_own)),
        out_shape=(
            jax.ShapeDtypeStruct((total, features), jnp.bfloat16),
            jax.ShapeDtypeStruct((total, features), jnp.bfloat16),
            jax.ShapeDtypeStruct((3, half, 3 * width), jnp.bfloat16),
            jax.ShapeDtypeStruct((3, half, total), jnp.float32),
        ),
        in_specs=[VMEM] * (7 + has_own),
        out_specs=[VMEM] * 4,
        compiler_params=PARAMS,
        cost_estimate=pl.CostEstimate(flops=1, bytes_accessed=1, transcendentals=0),
    )(*([own] if has_own else []), *pieces, *weights)


def grad_parts(units, x_all, s_all, column, outs):
    half, total = units.shape[1:]
    both = dot_nn(units[0:2].reshape(2 * half, total), x_all[:, column])
    down = dot_nn(units[2], s_all[:, column])
    for i, value in enumerate((both[:half], both[half:], down)):
        out = outs[0] if i < 2 else outs[-1]
        out[i if len(outs) == 1 else i % 2] = value.astype(out.dtype)


def outer_kernel(x_all, s_all, w_part, part, last, units, kept, sent, *refs):
    to_d, w_all, sums = refs[:2], refs[2], refs[3]
    half, width = last.shape[1:]
    offset = lax.axis_index("narrow") ^ lax.axis_index("wide") % 4
    last_column = slice(3 * width, 4 * width)
    for k in range(4):
        column = at_quarter(offset ^ k, width)
        for i in range(3):
            w_all[i, :, column] = last[i] if k == 3 else w_part[i, :, k * width : (k + 1) * width]
    total, tile = x_all.shape[0], sums.shape[2]
    lanes = min(width, total)
    for ref in (kept, sent):
        ref[:, 2 * total :, :] = jnp.zeros_like(ref[:, 2 * total :, :])
    routers = []
    for step in range(total // tile):
        rows = slice(step * tile, (step + 1) * tile)
        both = dot_nt(last[0:2].reshape(2 * half, width), x_all[rows, last_column])
        sums[0:2] = part[0:2, :, rows] + both.reshape(2, half, tile)
        sums[2] = part[2, :, rows] + dot_nt(last[2], s_all[rows, last_column])
        products = jnp.zeros((16, tile), jnp.float32)
        for low in range(0, half, 16):
            piece = slice(low, low + 16)
            gate, up, d_hidden = sums[0, piece, :], sums[1, piece, :], sums[2, piece, :]
            sigma = 0.5 + 0.5 * jnp.tanh(0.5 * gate)
            active = gate * sigma
            hidden = (active * up).astype(jnp.bfloat16)
            slope = sigma + active * (1.0 - sigma)
            units[0, piece, rows] = (d_hidden * up * slope).astype(jnp.bfloat16)
            units[1, piece, rows] = (d_hidden * active).astype(jnp.bfloat16)
            units[2, piece, rows] = hidden
            products = products + hidden.astype(jnp.float32) * d_hidden
        router = jnp.sum(products, axis=0, keepdims=True)
        routers += [router[:, low : low + lanes] for low in range(0, tile, lanes)]
        for low in range(step * tile, (step + 1) * tile, lanes):
            here = slice(low, low + lanes)
            lower = slice(total + low, total + low + lanes)
            out_part = dot_nn(units[2, :, here].T, w_all[2])
            left = units[0:2, :, here].reshape(2 * half, lanes).T
            in_part = dot_nn(left, w_all[0:2].reshape(2 * half, 4 * width))
            for mask in range(4):
                target = sent if mask % 2 else kept
                column = slice(mask * width, (mask + 1) * width)
                target[mask // 2, here, :] = out_part[:, column].astype(target.dtype)
                target[mask // 2, lower, :] = in_part[:, column].astype(target.dtype)
    router = jnp.concatenate(routers, 0)
    kept[0, 2 * total : 2 * total + len(routers), :lanes] = router
    put_pair(sent.at[0], 2 * total, router)
    grad_parts(units, x_all, s_all, last_column, to_d)


def outer(x_all, s_all, w_part, part, last):
    total, features = x_all.shape
    _, half, width = last.shape
    return pl.pallas_call(
        outer_kernel,
        out_shape=(
            jax.ShapeDtypeStruct((3, half, total), jnp.bfloat16),
            jax.ShapeDtypeStruct((2, packet_rows(total), width), jnp.float32),
            jax.ShapeDtypeStruct((2, packet_rows(total), width), jnp.bfloat16),
            jax.ShapeDtypeStruct((2, half, width), jnp.bfloat16),
            jax.ShapeDtypeStruct((1, half, width), jnp.bfloat16),
        ),
        in_specs=[VMEM] * 5,
        out_specs=[VMEM] * 5,
        scratch_shapes=[
            pltpu.VMEM((3, half, features), jnp.bfloat16),
            pltpu.VMEM((3, half, min(2 * width, total)), jnp.float32),
        ],
        compiler_params=PARAMS,
        cost_estimate=pl.CostEstimate(
            flops=8 * half * features * total, bytes_accessed=0, transcendentals=0
        ),
    )(x_all, s_all, w_part, part, last)


def grads_kernel(units, x_all, s_all, own, to_x, to_x_down, to_z):
    width = own.shape[2]
    for k, outs in enumerate(((own,), (to_x, to_x_down), (to_z,))):
        grad_parts(units, x_all, s_all, slice(k * width, (k + 1) * width), outs)


def weight_grads(units, x_all, s_all):
    half, total = units.shape[1:]
    features = x_all.shape[1]
    shapes = ((3, jnp.float32), (2, jnp.float32), (1, jnp.float32), (3, jnp.bfloat16))
    return pl.pallas_call(
        grads_kernel,
        out_shape=tuple(
            jax.ShapeDtypeStruct((count, half, features // 4), kind) for count, kind in shapes
        ),
        in_specs=[VMEM] * 3,
        out_specs=[VMEM] * 4,
        compiler_params=PARAMS,
        cost_estimate=pl.CostEstimate(flops=5 * half * features * total, bytes_accessed=0, transcendentals=0),
    )(units, x_all, s_all)


def join_kernel(own, got_x, got_x_down, out_0, out_1, out_2, held, sems):
    half = held.shape[1]
    x_bit = lax.axis_index("wide") % 2
    copies = []
    for part, held_part in enumerate((own, held)):
        first = (part * (1 - x_bit) + (1 - part) * x_bit) * half
        rows = pl.ds(pl.multiple_of(first, 16), half)
        for i, out in enumerate((out_0, out_1, out_2)):
            if part:
                got = got_x.at[i] if i < 2 else got_x_down.at[0]
                held[i] = got[...].astype(jnp.float32)
            place = sems.at[3 * part + i]
            copies.append(pltpu.make_async_copy(held_part.at[i], out.at[rows, :], place))
            copies[-1].start()
    for copy in copies:
        copy.wait()


def join_grads(own, got_x, got_x_down):
    _, half, width = own.shape
    shape = jax.ShapeDtypeStruct((2 * half, width), jnp.float32)
    return pl.pallas_call(
        join_kernel,
        out_shape=(shape,) * 3,
        in_specs=[VMEM] * 3,
        out_specs=[HBM] * 3,
        scratch_shapes=[
            pltpu.VMEM(own.shape, jnp.float32),
            pltpu.SemaphoreType.DMA((6,)),
        ],
        compiler_params=PARAMS,
        cost_estimate=pl.CostEstimate(flops=1, bytes_accessed=0, transcendentals=0),
    )(own, got_x, got_x_down)


def cross_kernel(kept, got, sent):
    total = (kept.shape[1] - EXTRA) // 2
    tile = min(kept.shape[2], total)
    count = total // tile
    body = slice(0, 2 * total)
    sent[body, :] = (kept[1, body, :] + got[1, body, :].astype(jnp.float32)).astype(sent.dtype)
    sent[2 * total :, :] = jnp.zeros_like(sent[2 * total :, :])
    router = kept[0, 2 * total : 2 * total + count, :] + get_pair(got.at[0], 2 * total, count)
    put_pair(sent, 2 * total, router)


def cross_part(kept, got):
    return pl.pallas_call(
        cross_kernel,
        out_shape=jax.ShapeDtypeStruct(got.shape[1:], got.dtype),
        in_specs=[VMEM] * 2,
        out_specs=VMEM,
        compiler_params=PARAMS,
    )(kept, got)


def result_kernel(kept, got, across, out):
    total = (kept.shape[1] - EXTRA) // 2
    count = total // min(kept.shape[2], total)
    body, tail = slice(0, 2 * total), slice(2 * total, 2 * total + count)
    value = kept[0, body, :] + got[0, body, :].astype(jnp.float32)
    out[body, :] = value + across[body, :].astype(jnp.float32)
    out[2 * total :, :] = jnp.zeros_like(out[2 * total :, :])
    router = kept[0, tail, :] + get_pair(got.at[0], 2 * total, count)
    out[tail, :] = router + get_pair(across, 2 * total, count)


def result_parts(kept, got, across):
    return pl.pallas_call(
        result_kernel,
        out_shape=jax.ShapeDtypeStruct(kept.shape[1:], jnp.float32),
        in_specs=[VMEM] * 3,
        out_specs=VMEM,
        compiler_params=PARAMS,
    )(kept, got, across)


def first_kernel(kept, got, to_y, to_x):
    total = (kept.shape[1] - EXTRA) // 2
    slots = total // 4
    count = total // min(kept.shape[2], total)
    body = slice(0, total)
    to_y[body, :] = (kept[1, body, :] + got[1, body, :].astype(jnp.float32)).astype(to_y.dtype)
    put_pair(
        to_y,
        total,
        kept[0, 2 * total : 2 * total + count, :] + get_pair(got.at[0], 2 * total, count),
    )
    for part in range(2):
        for block in range(2):
            rows = slice(total + (2 * block + 1) * slots, total + (2 * block + 2) * slots)
            value = kept[part, rows, :] + got[part, rows, :].astype(jnp.float32)
            to_x[part, block * slots : (block + 1) * slots, :] = value.astype(to_x.dtype)


def first_parts(kept, got):
    total, width = (kept.shape[1] - EXTRA) // 2, kept.shape[2]
    return pl.pallas_call(
        first_kernel,
        out_shape=(
            jax.ShapeDtypeStruct((total + EXTRA, width), jnp.bfloat16),
            jax.ShapeDtypeStruct((2, total // 2, width), jnp.bfloat16),
        ),
        in_specs=[VMEM] * 2,
        out_specs=[VMEM] * 2,
        compiler_params=PARAMS,
    )(kept, got)


def ffn_kernel(kept, got, from_y, held, to_x):
    total = (kept.shape[1] - EXTRA) // 2
    slots, width = total // 4, kept.shape[2]
    count = total // min(width, total)
    router = kept[0, 2 * total : 2 * total + count, :] + get_pair(got.at[0], 2 * total, count)
    router = router + get_pair(from_y, total, count)
    pairs = []
    for block in range(4):
        rows = slice(block * slots, (block + 1) * slots)
        value = kept[0, rows, :] + got[0, rows, :].astype(jnp.float32)
        value = value + from_y[rows, :].astype(jnp.float32)
        out = to_x if block % 2 else held
        place = block // 2
        out[place * slots : (place + 1) * slots, :] = value.astype(out.dtype)
        lane = block * slots % width
        pairs.append(router[block * slots // width :, lane : lane + slots][:1])
    held[2 * slots :, :] = jnp.zeros_like(held[2 * slots :, :])
    to_x[2 * slots :, :] = jnp.zeros_like(to_x[2 * slots :, :])
    held[2 * slots : 2 * slots + 1, :slots] = pairs[0]
    held[2 * slots + 1 : 2 * slots + 2, :slots] = pairs[2]
    put_pair(to_x, 2 * slots, jnp.concatenate([pairs[1], pairs[3]], 0))


def ffn_parts(kept, got, from_y):
    total, width = (kept.shape[1] - EXTRA) // 2, kept.shape[2]
    shape = (total // 2 + EXTRA, width)
    return pl.pallas_call(
        ffn_kernel,
        out_shape=(
            jax.ShapeDtypeStruct(shape, jnp.float32),
            jax.ShapeDtypeStruct(shape, jnp.bfloat16),
        ),
        in_specs=[VMEM] * 3,
        out_specs=[VMEM] * 2,
        compiler_params=PARAMS,
    )(kept, got, from_y)


def input_kernel(kept, got, from_x, held, to_y):
    total = (kept.shape[1] - EXTRA) // 2
    slots = total // 4
    for part, out in enumerate((held, to_y)):
        for block in range(2):
            rows = slice(total + 2 * block * slots, total + (2 * block + 1) * slots)
            here = slice(block * slots, (block + 1) * slots)
            value = kept[part, rows, :] + got[part, rows, :].astype(jnp.float32)
            out[here, :] = (value + from_x[part, here, :].astype(jnp.float32)).astype(out.dtype)


def input_parts(kept, got, from_x):
    shape = from_x.shape[1:]
    return pl.pallas_call(
        input_kernel,
        out_shape=(
            jax.ShapeDtypeStruct(shape, jnp.float32),
            jax.ShapeDtypeStruct(shape, jnp.bfloat16),
        ),
        in_specs=[VMEM] * 3,
        out_specs=[VMEM] * 2,
        compiler_params=PARAMS,
    )(kept, got, from_x)


def last_kernel(ffn, from_x, grad, from_y, held, to_z):
    slots = grad.shape[0] // 2
    router = ffn[2 * slots : 2 * slots + 2, :] + get_pair(from_x, 2 * slots, 2)
    for block, out in enumerate((held, to_z)):
        rows = slice(block * slots, (block + 1) * slots)
        out[:slots, :] = (ffn[rows, :] + from_x[rows, :].astype(jnp.float32)).astype(out.dtype)
        out[slots : 2 * slots, :] = (grad[rows, :] + from_y[rows, :].astype(jnp.float32)).astype(
            out.dtype
        )
    held[2 * slots :, :] = jnp.broadcast_to(router[:1], (EXTRA, router.shape[1]))
    put_pair(to_z, 2 * slots, router[1:])


def last_parts(ffn, from_x, grad, from_y):
    return pl.pallas_call(
        last_kernel,
        out_shape=(
            jax.ShapeDtypeStruct(ffn.shape, jnp.float32),
            jax.ShapeDtypeStruct(ffn.shape, jnp.bfloat16),
        ),
        in_specs=[VMEM] * 4,
        out_specs=[VMEM] * 2,
        compiler_params=PARAMS,
        cost_estimate=pl.CostEstimate(flops=2 * 10**9, bytes_accessed=0, transcendentals=0),
    )(ffn, from_x, grad, from_y)


def finish_kernel(prob, own, *refs):
    got, (output, tokens_grad, prob_grad) = refs[:-3], refs[-3:]
    slots, width = output.shape
    ffn, grad = own[:slots, :], own[slots : 2 * slots, :]
    router = own[2 * slots : 2 * slots + 1, :]
    for ref in got:
        ffn = ffn + ref[:slots, :].astype(jnp.float32)
        grad = grad + ref[slots : 2 * slots, :].astype(jnp.float32)
        router = router + get_pair(ref, 2 * slots, 1)
    weight = jnp.broadcast_to(prob[...], (128, slots)).T[:, :1]
    output[...] = (ffn.astype(jnp.bfloat16).astype(jnp.float32) * weight).astype(jnp.bfloat16)
    tokens_grad[...] = grad.astype(jnp.bfloat16)
    prob_grad[...] = router[:, :slots] / prob[...]


def finish(prob, own, got):
    slots, width = (own.shape[0] - EXTRA) // 2, own.shape[1]
    part = jax.ShapeDtypeStruct((slots, width), jnp.bfloat16)
    return pl.pallas_call(
        finish_kernel,
        out_shape=(part, part, jax.ShapeDtypeStruct((1, slots), jnp.float32)),
        in_specs=[VMEM] * (2 + len(got)),
        out_specs=[VMEM] * 3,
        compiler_params=PARAMS,
    )(prob, own, *got)


def shards(tokens, cotangent, expert_ids, route_prob, gate_weight, up_weight, down_weight):
    wide_count = lax.axis_size("wide")
    narrow_count = lax.axis_size("narrow")
    expert_count = wide_count // 4
    tok_rows, features = tokens.shape
    width = features // narrow_count
    slots = min(4 * tok_rows // expert_count, tok_rows)
    direct = expert_count == 2 and slots == tok_rows
    place = lax.axis_index("narrow")
    masks = (1, 4, 5)
    groups = [
        [4 * e + 2 * b + a for e in range(expert_count) for a in range(2)] for b in range(2)
    ]

    weights = (gate_weight.T, up_weight.T, down_weight.T)
    if direct:
        keep, give, own, same, other = prologue(
            weights, (tokens, cotangent, expert_ids.T, route_prob[None, :]), width
        )
        mine = jnp.stack(
            [partner(part, "wide", mask) for mask, part in zip(masks, (same, other, other))]
        )
    else:
        own = None
        keep, give = prologue(weights, (), width)
        chosen = expert_ids[:, 0]
        onehot = (chosen[:, None] == jnp.arange(expert_count, dtype=jnp.int32)[None, :]).astype(
            jnp.int32
        )
        rank = jnp.sum((jnp.cumsum(onehot, axis=0) - onehot) * onehot, axis=1)
        slot_place = chosen * slots + rank
        source = (
            jnp.full((expert_count * slots,), tok_rows, jnp.int32)
            .at[slot_place]
            .set(jnp.arange(tok_rows, dtype=jnp.int32))
        )
        scaled = (route_prob[:, None] * cotangent.astype(jnp.float32)).astype(jnp.bfloat16)
        both = jnp.stack([tokens, scaled])
        both = lax.dynamic_slice_in_dim(both, place * width, width, 2)
        both = jnp.concatenate([both, jnp.zeros((2, 1, width), jnp.bfloat16)], 1)
        routed = both[:, source].reshape(2, expert_count, slots, width).transpose(1, 0, 2, 3)
        routed = jnp.repeat(routed, 2, axis=0)
        mine = lax.all_to_all(
            routed, "wide", split_axis=0, concat_axis=0, axis_index_groups=groups, tiled=True
        )

    from_x, from_z = lax.optimization_barrier(
        (partner(give, "wide", 1), partner(keep, "wide", 2))
    )
    from_d = partner(from_x, "wide", 2)
    across = partner(mine, "narrow", 2)
    pieces = (mine, partner(mine, "narrow", 1), across, partner(across, "narrow", 1))
    x_all, s_all, w_part, part = gather_parts(own, pieces, (keep, from_x, from_z))
    units, kept, sent, grad_d, grad_d_down = outer(x_all, s_all, w_part, part, from_d)
    got = partner(sent, "narrow", 1)
    got_d_down = partner(grad_d_down, "wide", 2)
    got_d = partner(grad_d, "wide", 2)
    if direct:
        to_y, to_x = first_parts(kept, got)
        units, _ = lax.optimization_barrier((units, to_y))
        ffn_held, ffn_x = ffn_parts(kept, got, partner(to_y, "narrow", 2))
        grad_own, grad_x, grad_x_down, grad_z = weight_grads(units, x_all, s_all)
        from_x = partner(to_x, "wide", 1)
        from_x, _ = lax.optimization_barrier((from_x, ffn_x))
        grad_held, grad_y = input_parts(kept, got, from_x)
        grad_z, _ = lax.optimization_barrier((grad_z, from_x))
        grad_x, _, _ = lax.optimization_barrier((grad_x, ffn_x, grad_y))
        grad_x_down = (grad_x_down + got_d_down.astype(jnp.float32)).astype(jnp.bfloat16)
        got_x_down = partner(grad_x_down, "wide", 1)
        grad_held, got_x_down = lax.optimization_barrier((grad_held, got_x_down))
        held, to_z = last_parts(
            ffn_held, partner(ffn_x, "wide", 1), grad_held, partner(grad_y, "narrow", 2)
        )
        grad_x = (grad_x + got_d.astype(jnp.float32)).astype(jnp.bfloat16)
        got_x = partner(grad_x, "wide", 1)
        held, got_x = lax.optimization_barrier((held, got_x))
        output, tokens_grad, prob_grad = finish(
            route_prob[None, :], held, [partner(to_z, "wide", 4)]
        )
        prob_grad = prob_grad[0]
    else:
        grad_own, grad_x, grad_x_down, grad_z = weight_grads(units, x_all, s_all)
        grad_x_down = (grad_x_down + got_d_down.astype(jnp.float32)).astype(jnp.bfloat16)
        got_x_down = partner(grad_x_down, "wide", 1)
        grad_x = (grad_x + got_d.astype(jnp.float32)).astype(jnp.bfloat16)
        got_x = partner(grad_x, "wide", 1)
        across = partner(cross_part(kept, got), "narrow", 2)
        result = result_parts(kept, got, across)
        total = (result.shape[0] - EXTRA) // 2
        parts = result[: 2 * total].astype(jnp.bfloat16)
        parts = parts.reshape(2, 2 * expert_count, slots, width)
        back = lax.all_to_all(
            parts, "wide", split_axis=1, concat_axis=1, axis_index_groups=groups, tiled=True
        )
        back = back.reshape(2, expert_count, 2, slots, width).astype(jnp.float32).sum(2)
        back = back.reshape(2, expert_count * slots, width)[:, slot_place]
        router = result[2 * total : 2 * total + total // min(width, total), : min(width, total)]
        router = router.reshape(2 * expert_count, slots)
        high = lax.reduce_precision(router, 8, 7)
        pair = jnp.stack([high, router - high], 1).astype(jnp.bfloat16)
        pair = lax.all_to_all(
            pair, "wide", split_axis=0, concat_axis=0, axis_index_groups=groups, tiled=True
        )
        router = pair.reshape(expert_count, 4, slots).astype(jnp.float32).sum(1)
        prob_grad = router.reshape(expert_count * slots)[slot_place] / route_prob
        ffn = back[0].astype(jnp.bfloat16).astype(jnp.float32)
        output = (route_prob[:, None] * ffn).astype(jnp.bfloat16)
        tokens_grad = back[1].astype(jnp.bfloat16)
    got_z = partner(grad_z, "wide", 2)
    gate_grad, up_grad, down_grad = join_grads(
        grad_own + got_z.astype(jnp.float32), got_x, got_x_down
    )
    return (output, tokens_grad, prob_grad, gate_grad.T, up_grad.T, down_grad.T)


def solution(mesh):
    in_specs = (
        P("wide", None),
        P("wide", None),
        P("wide", None),
        P("wide"),
        P("wide", "narrow"),
        P("wide", "narrow"),
        P("wide", "narrow"),
    )
    out_specs = (
        P("wide", "narrow"),
        P("wide", "narrow"),
        P("wide"),
        P("wide", "narrow"),
        P("wide", "narrow"),
        P("wide", "narrow"),
    )
    return jax.shard_map(shards, mesh=mesh, in_specs=in_specs, out_specs=out_specs, check_vma=False)
```

```python
import functools

import jax
import jax.numpy as jnp
from jax import lax
from jax.experimental import pallas as pl
from jax.experimental.pallas import tpu as pltpu
from jax.sharding import PartitionSpec as P

VMEM = pl.BlockSpec(memory_space=pltpu.VMEM)
HBM = pl.BlockSpec(memory_space=pltpu.HBM)
EXTRA = 16
PARAMS = pltpu.CompilerParams(vmem_limit_bytes=32 * 1024 * 1024)


def partner(x, axis, mask):
    return lax.ppermute(x, axis, [(i, i ^ mask) for i in range(lax.axis_size(axis))])


def dot_nn(left, right):
    return lax.dot_general(
        left, right, (((1,), (0,)), ((), ())), preferred_element_type=jnp.float32
    )


def dot_nt(left, right):
    return lax.dot_general(
        left, right, (((1,), (1,)), ((), ())), preferred_element_type=jnp.float32
    )


def at_quarter(index, width):
    return pl.ds(pl.multiple_of(index * width, width), width)


def packet_rows(rows):
    return 2 * rows + EXTRA


def put_pair(ref, first, value):
    count, lanes = value.shape
    high = value.astype(jnp.bfloat16).astype(jnp.float32)
    both = jnp.concatenate([high, value - high], 0)
    both = jnp.concatenate([both, jnp.zeros((EXTRA - 2 * count, lanes), jnp.float32)], 0)
    ref[first : first + EXTRA, :lanes] = both.astype(ref.dtype)


def get_pair(ref, first, count):
    both = ref[first : first + EXTRA, :].astype(jnp.float32)
    return both[:count] + both[count : 2 * count]


def prologue_kernel(routed, gate, up, down, *refs):
    if routed:
        tokens, cotangent, ids, prob, keep, give, own, same, other = refs[:9]
        held, ids_row, prob_row, sems = refs[9:]
        parts = ((tokens, held.at[0]), (cotangent, held.at[1]), (ids, ids_row), (prob, prob_row))
    else:
        keep, give, sems = refs
        parts = ()
    half = keep.shape[1]
    x_bit = lax.axis_index("wide") % 2
    keep_rows = pl.ds(pl.multiple_of(x_bit * half, 16), half)
    give_rows = pl.ds(pl.multiple_of((1 - x_bit) * half, 16), half)
    for i, ref in enumerate((gate, up, down)):
        parts += ((ref.at[keep_rows, :], keep.at[i]), (ref.at[give_rows, :], give.at[i]))
    copies = [pltpu.make_async_copy(src, dst, sems.at[i]) for i, (src, dst) in enumerate(parts)]
    for copy in copies:
        copy.start()
    if routed:
        for copy in copies[:4]:
            copy.wait()
        rows = held.shape[1]
        width = same.shape[2]
        mine = lax.axis_index("wide") // 4
        column = at_quarter(lax.axis_index("narrow"), width)
        chosen = jnp.broadcast_to(ids_row[...], (128, rows)).astype(jnp.float32).T[:, :1]
        weight = jnp.broadcast_to(prob_row[...], (128, rows)).T[:, :1]
        here = jnp.where(chosen == mine.astype(jnp.float32), 1.0, 0.0)
        for i in range(2):
            factor = weight if i else jnp.ones_like(weight)
            own[i] = (held[i].astype(jnp.float32) * (factor * here)).astype(jnp.bfloat16)
            part = held[i, :, column].astype(jnp.float32)
            same[i] = (part * (factor * here)).astype(jnp.bfloat16)
            other[i] = (part * (factor * (1.0 - here))).astype(jnp.bfloat16)
    for copy in copies[len(copies) - 6 :]:
        copy.wait()


def prologue(weights, token_args, width):
    hidden, quarter = weights[0].shape
    half = jax.ShapeDtypeStruct((3, hidden // 2, quarter), jnp.bfloat16)
    outs, scratch = (half, half), []
    if token_args:
        rows, features = token_args[0].shape
        part = jax.ShapeDtypeStruct((2, rows, width), jnp.bfloat16)
        outs += (jax.ShapeDtypeStruct((2, rows, features), jnp.bfloat16), part, part)
        scratch = [
            pltpu.VMEM((2, rows, features), jnp.bfloat16),
            pltpu.VMEM((1, rows), jnp.int32),
            pltpu.VMEM((1, rows), jnp.float32),
        ]
    return pl.pallas_call(
        functools.partial(prologue_kernel, bool(token_args)),
        out_shape=outs,
        in_specs=[HBM] * (3 + len(token_args)),
        out_specs=[VMEM] * len(outs),
        scratch_shapes=scratch + [pltpu.SemaphoreType.DMA((10,))],
        compiler_params=PARAMS,
    )(*[pltpu.with_memory_space_constraint(x, pltpu.HBM) for x in (*weights, *token_args)])


def gather_kernel(has_own, *refs):
    own = refs[0] if has_own else None
    pieces, weights = refs[has_own : has_own + 4], refs[has_own + 4 : has_own + 7]
    x_all, s_all, w_all, part = refs[has_own + 7 :]
    blocks, _, slots, width = pieces[0].shape
    half, reach = w_all.shape[1:]
    member = lax.axis_index("wide") % 4
    place = lax.axis_index("narrow")
    for k, ref in enumerate(weights):
        for i in range(3):
            w_all[i, :, k * width : (k + 1) * width] = ref[i]
    first = 0
    if has_own:
        for k in range(4):
            column = at_quarter(member ^ k, width)
            x_all[:slots, k * width : (k + 1) * width] = own[0, :, column]
            s_all[:slots, k * width : (k + 1) * width] = own[1, :, column]
        first = slots
    for mask, ref in enumerate(pieces):
        column = at_quarter(place ^ member ^ mask, width)
        for block in range(blocks):
            rows = slice(first + block * slots, first + (block + 1) * slots)
            x_all[rows, column] = ref[block, 0]
            s_all[rows, column] = ref[block, 1]
    total = x_all.shape[0]
    tile = min(2 * width, total)
    for step in range(total // tile):
        rows = slice(step * tile, (step + 1) * tile)
        both = dot_nt(w_all[0:2].reshape(2 * half, reach), x_all[rows, :reach])
        part[0:2, :, rows] = both.reshape(2, half, tile)
        part[2, :, rows] = dot_nt(w_all[2], s_all[rows, :reach])


def gather_parts(own, pieces, weights):
    blocks, _, slots, width = pieces[0].shape
    half = weights[0].shape[1]
    has_own = own is not None
    total = (blocks + has_own) * slots
    features = 4 * width
    return pl.pallas_call(
        functools.partial(gather_kernel, int(has_own)),
        out_shape=(
            jax.ShapeDtypeStruct((total, features), jnp.bfloat16),
            jax.ShapeDtypeStruct((total, features), jnp.bfloat16),
            jax.ShapeDtypeStruct((3, half, 3 * width), jnp.bfloat16),
            jax.ShapeDtypeStruct((3, half, total), jnp.float32),
        ),
        in_specs=[VMEM] * (7 + has_own),
        out_specs=[VMEM] * 4,
        compiler_params=PARAMS,
        cost_estimate=pl.CostEstimate(flops=1, bytes_accessed=1, transcendentals=0),
    )(*([own] if has_own else []), *pieces, *weights)


def grad_parts(units, x_all, s_all, column, outs):
    half, total = units.shape[1:]
    both = dot_nn(units[0:2].reshape(2 * half, total), x_all[:, column])
    down = dot_nn(units[2], s_all[:, column])
    for i, value in enumerate((both[:half], both[half:], down)):
        out = outs[0] if i < 2 else outs[-1]
        out[i if len(outs) == 1 else i % 2] = value.astype(out.dtype)


def outer_kernel(x_all, s_all, w_part, part, last, units, kept, sent, *refs):
    to_d, w_all, sums = refs[:2], refs[2], refs[3]
    half, width = last.shape[1:]
    offset = lax.axis_index("narrow") ^ lax.axis_index("wide") % 4
    last_column = slice(3 * width, 4 * width)
    for k in range(4):
        column = at_quarter(offset ^ k, width)
        for i in range(3):
            w_all[i, :, column] = last[i] if k == 3 else w_part[i, :, k * width : (k + 1) * width]
    total, tile = x_all.shape[0], sums.shape[2]
    lanes = min(width, total)
    for ref in (kept, sent):
        ref[:, 2 * total :, :] = jnp.zeros_like(ref[:, 2 * total :, :])
    routers = []
    for step in range(total // tile):
        rows = slice(step * tile, (step + 1) * tile)
        both = dot_nt(last[0:2].reshape(2 * half, width), x_all[rows, last_column])
        sums[0:2] = part[0:2, :, rows] + both.reshape(2, half, tile)
        sums[2] = part[2, :, rows] + dot_nt(last[2], s_all[rows, last_column])
        products = jnp.zeros((16, tile), jnp.float32)
        for low in range(0, half, 16):
            piece = slice(low, low + 16)
            gate, up, d_hidden = sums[0, piece, :], sums[1, piece, :], sums[2, piece, :]
            sigma = 0.5 + 0.5 * jnp.tanh(0.5 * gate)
            active = gate * sigma
            hidden = (active * up).astype(jnp.bfloat16)
            slope = sigma + active * (1.0 - sigma)
            units[0, piece, rows] = (d_hidden * up * slope).astype(jnp.bfloat16)
            units[1, piece, rows] = (d_hidden * active).astype(jnp.bfloat16)
            units[2, piece, rows] = hidden
            products = products + hidden.astype(jnp.float32) * d_hidden
        router = jnp.sum(products, axis=0, keepdims=True)
        routers += [router[:, low : low + lanes] for low in range(0, tile, lanes)]
        for low in range(step * tile, (step + 1) * tile, lanes):
            here = slice(low, low + lanes)
            lower = slice(total + low, total + low + lanes)
            out_part = dot_nn(units[2, :, here].T, w_all[2])
            left = units[0:2, :, here].reshape(2 * half, lanes).T
            in_part = dot_nn(left, w_all[0:2].reshape(2 * half, 4 * width))
            for mask in range(4):
                target = sent if mask % 2 else kept
                column = slice(mask * width, (mask + 1) * width)
                target[mask // 2, here, :] = out_part[:, column].astype(target.dtype)
                target[mask // 2, lower, :] = in_part[:, column].astype(target.dtype)
    router = jnp.concatenate(routers, 0)
    kept[0, 2 * total : 2 * total + len(routers), :lanes] = router
    put_pair(sent.at[0], 2 * total, router)
    grad_parts(units, x_all, s_all, last_column, to_d)


def outer(x_all, s_all, w_part, part, last):
    total, features = x_all.shape
    _, half, width = last.shape
    return pl.pallas_call(
        outer_kernel,
        out_shape=(
            jax.ShapeDtypeStruct((3, half, total), jnp.bfloat16),
            jax.ShapeDtypeStruct((2, packet_rows(total), width), jnp.float32),
            jax.ShapeDtypeStruct((2, packet_rows(total), width), jnp.bfloat16),
            jax.ShapeDtypeStruct((2, half, width), jnp.bfloat16),
            jax.ShapeDtypeStruct((1, half, width), jnp.bfloat16),
        ),
        in_specs=[VMEM] * 5,
        out_specs=[VMEM] * 5,
        scratch_shapes=[
            pltpu.VMEM((3, half, features), jnp.bfloat16),
            pltpu.VMEM((3, half, min(2 * width, total)), jnp.float32),
        ],
        compiler_params=PARAMS,
        cost_estimate=pl.CostEstimate(
            flops=8 * half * features * total, bytes_accessed=0, transcendentals=0
        ),
    )(x_all, s_all, w_part, part, last)


def grads_kernel(units, x_all, s_all, own, to_x, to_x_down, to_z):
    width = own.shape[2]
    for k, outs in enumerate(((own,), (to_x, to_x_down), (to_z,))):
        grad_parts(units, x_all, s_all, slice(k * width, (k + 1) * width), outs)


def weight_grads(units, x_all, s_all):
    half, total = units.shape[1:]
    features = x_all.shape[1]
    shapes = ((3, jnp.float32), (2, jnp.float32), (1, jnp.float32), (3, jnp.bfloat16))
    return pl.pallas_call(
        grads_kernel,
        out_shape=tuple(
            jax.ShapeDtypeStruct((count, half, features // 4), kind) for count, kind in shapes
        ),
        in_specs=[VMEM] * 3,
        out_specs=[VMEM] * 4,
        compiler_params=PARAMS,
        cost_estimate=pl.CostEstimate(flops=5 * half * features * total, bytes_accessed=0, transcendentals=0),
    )(units, x_all, s_all)


def write_rows(values, outs, held, sems, first):
    rows = pl.ds(pl.multiple_of(first, 16), held.shape[1])
    copies = []
    for i, out in enumerate(outs):
        held[i] = values(i)
        copies.append(pltpu.make_async_copy(held.at[i], out.at[rows, :], sems.at[i]))
        copies[-1].start()
    for copy in copies:
        copy.wait()


def give_kernel(got, got_down, out_0, out_1, out_2, held, sems):
    def values(i):
        return (got[i] if i < 2 else got_down[0]).astype(jnp.float32)

    first = (1 - lax.axis_index("wide") % 2) * held.shape[1]
    write_rows(values, (out_0, out_1, out_2), held, sems, first)


def keep_kernel(in_0, in_1, in_2, own, got, out_0, out_1, out_2, held, sems):
    def values(i):
        return own[i] + got[i].astype(jnp.float32)

    first = lax.axis_index("wide") % 2 * held.shape[1]
    write_rows(values, (out_0, out_1, out_2), held, sems, first)


def write_half(kernel, shape, held, values):
    held_in = [pltpu.with_memory_space_constraint(x, pltpu.HBM) for x in held]
    return pl.pallas_call(
        kernel,
        out_shape=(jax.ShapeDtypeStruct((2 * shape[1], shape[2]), jnp.float32),) * 3,
        in_specs=[HBM] * len(held) + [VMEM] * len(values),
        out_specs=[HBM] * 3,
        scratch_shapes=[pltpu.VMEM(shape, jnp.float32), pltpu.SemaphoreType.DMA((3,))],
        input_output_aliases={i: i for i in range(len(held))},
        compiler_params=PARAMS,
        cost_estimate=pl.CostEstimate(flops=1, bytes_accessed=0, transcendentals=0),
    )(*held_in, *values)


def cross_kernel(kept, got, sent):
    total = (kept.shape[1] - EXTRA) // 2
    tile = min(kept.shape[2], total)
    count = total // tile
    body = slice(0, 2 * total)
    sent[body, :] = (kept[1, body, :] + got[1, body, :].astype(jnp.float32)).astype(sent.dtype)
    sent[2 * total :, :] = jnp.zeros_like(sent[2 * total :, :])
    router = kept[0, 2 * total : 2 * total + count, :] + get_pair(got.at[0], 2 * total, count)
    put_pair(sent, 2 * total, router)


def cross_part(kept, got):
    return pl.pallas_call(
        cross_kernel,
        out_shape=jax.ShapeDtypeStruct(got.shape[1:], got.dtype),
        in_specs=[VMEM] * 2,
        out_specs=VMEM,
        compiler_params=PARAMS,
    )(kept, got)


def result_kernel(kept, got, across, out):
    total = (kept.shape[1] - EXTRA) // 2
    count = total // min(kept.shape[2], total)
    body, tail = slice(0, 2 * total), slice(2 * total, 2 * total + count)
    value = kept[0, body, :] + got[0, body, :].astype(jnp.float32)
    out[body, :] = value + across[body, :].astype(jnp.float32)
    out[2 * total :, :] = jnp.zeros_like(out[2 * total :, :])
    router = kept[0, tail, :] + get_pair(got.at[0], 2 * total, count)
    out[tail, :] = router + get_pair(across, 2 * total, count)


def result_parts(kept, got, across):
    return pl.pallas_call(
        result_kernel,
        out_shape=jax.ShapeDtypeStruct(kept.shape[1:], jnp.float32),
        in_specs=[VMEM] * 3,
        out_specs=VMEM,
        compiler_params=PARAMS,
    )(kept, got, across)


def first_kernel(kept, got, to_y, to_x):
    total = (kept.shape[1] - EXTRA) // 2
    slots = total // 4
    count = total // min(kept.shape[2], total)
    body = slice(0, total)
    to_y[body, :] = (kept[1, body, :] + got[1, body, :].astype(jnp.float32)).astype(to_y.dtype)
    put_pair(
        to_y,
        total,
        kept[0, 2 * total : 2 * total + count, :] + get_pair(got.at[0], 2 * total, count),
    )
    for part in range(2):
        for block in range(2):
            rows = slice(total + (2 * block + 1) * slots, total + (2 * block + 2) * slots)
            value = kept[part, rows, :] + got[part, rows, :].astype(jnp.float32)
            to_x[part, block * slots : (block + 1) * slots, :] = value.astype(to_x.dtype)


def first_parts(kept, got):
    total, width = (kept.shape[1] - EXTRA) // 2, kept.shape[2]
    return pl.pallas_call(
        first_kernel,
        out_shape=(
            jax.ShapeDtypeStruct((total + EXTRA, width), jnp.bfloat16),
            jax.ShapeDtypeStruct((2, total // 2, width), jnp.bfloat16),
        ),
        in_specs=[VMEM] * 2,
        out_specs=[VMEM] * 2,
        compiler_params=PARAMS,
    )(kept, got)


def ffn_kernel(kept, got, from_y, held, to_x):
    total = (kept.shape[1] - EXTRA) // 2
    slots, width = total // 4, kept.shape[2]
    count = total // min(width, total)
    router = kept[0, 2 * total : 2 * total + count, :] + get_pair(got.at[0], 2 * total, count)
    router = router + get_pair(from_y, total, count)
    pairs = []
    for block in range(4):
        rows = slice(block * slots, (block + 1) * slots)
        value = kept[0, rows, :] + got[0, rows, :].astype(jnp.float32)
        value = value + from_y[rows, :].astype(jnp.float32)
        out = to_x if block % 2 else held
        place = block // 2
        out[place * slots : (place + 1) * slots, :] = value.astype(out.dtype)
        lane = block * slots % width
        pairs.append(router[block * slots // width :, lane : lane + slots][:1])
    held[2 * slots :, :] = jnp.zeros_like(held[2 * slots :, :])
    to_x[2 * slots :, :] = jnp.zeros_like(to_x[2 * slots :, :])
    held[2 * slots : 2 * slots + 1, :slots] = pairs[0]
    held[2 * slots + 1 : 2 * slots + 2, :slots] = pairs[2]
    put_pair(to_x, 2 * slots, jnp.concatenate([pairs[1], pairs[3]], 0))


def ffn_parts(kept, got, from_y):
    total, width = (kept.shape[1] - EXTRA) // 2, kept.shape[2]
    shape = (total // 2 + EXTRA, width)
    return pl.pallas_call(
        ffn_kernel,
        out_shape=(
            jax.ShapeDtypeStruct(shape, jnp.float32),
            jax.ShapeDtypeStruct(shape, jnp.bfloat16),
        ),
        in_specs=[VMEM] * 3,
        out_specs=[VMEM] * 2,
        compiler_params=PARAMS,
    )(kept, got, from_y)


def input_kernel(kept, got, from_x, held, to_y):
    total = (kept.shape[1] - EXTRA) // 2
    slots = total // 4
    for part, out in enumerate((held, to_y)):
        for block in range(2):
            rows = slice(total + 2 * block * slots, total + (2 * block + 1) * slots)
            here = slice(block * slots, (block + 1) * slots)
            value = kept[part, rows, :] + got[part, rows, :].astype(jnp.float32)
            out[here, :] = (value + from_x[part, here, :].astype(jnp.float32)).astype(out.dtype)


def input_parts(kept, got, from_x):
    shape = from_x.shape[1:]
    return pl.pallas_call(
        input_kernel,
        out_shape=(
            jax.ShapeDtypeStruct(shape, jnp.float32),
            jax.ShapeDtypeStruct(shape, jnp.bfloat16),
        ),
        in_specs=[VMEM] * 3,
        out_specs=[VMEM] * 2,
        compiler_params=PARAMS,
    )(kept, got, from_x)


def last_kernel(ffn, from_x, grad, from_y, held, to_z):
    slots = grad.shape[0] // 2
    router = ffn[2 * slots : 2 * slots + 2, :] + get_pair(from_x, 2 * slots, 2)
    for block, out in enumerate((held, to_z)):
        rows = slice(block * slots, (block + 1) * slots)
        out[:slots, :] = (ffn[rows, :] + from_x[rows, :].astype(jnp.float32)).astype(out.dtype)
        out[slots : 2 * slots, :] = (grad[rows, :] + from_y[rows, :].astype(jnp.float32)).astype(
            out.dtype
        )
    held[2 * slots :, :] = jnp.broadcast_to(router[:1], (EXTRA, router.shape[1]))
    put_pair(to_z, 2 * slots, router[1:])


def last_parts(ffn, from_x, grad, from_y):
    return pl.pallas_call(
        last_kernel,
        out_shape=(
            jax.ShapeDtypeStruct(ffn.shape, jnp.float32),
            jax.ShapeDtypeStruct(ffn.shape, jnp.bfloat16),
        ),
        in_specs=[VMEM] * 4,
        out_specs=[VMEM] * 2,
        compiler_params=PARAMS,
        cost_estimate=pl.CostEstimate(flops=2 * 10**9, bytes_accessed=0, transcendentals=0),
    )(ffn, from_x, grad, from_y)


def finish_kernel(prob, own, *refs):
    got, (output, tokens_grad, prob_grad) = refs[:-3], refs[-3:]
    slots, width = output.shape
    ffn, grad = own[:slots, :], own[slots : 2 * slots, :]
    router = own[2 * slots : 2 * slots + 1, :]
    for ref in got:
        ffn = ffn + ref[:slots, :].astype(jnp.float32)
        grad = grad + ref[slots : 2 * slots, :].astype(jnp.float32)
        router = router + get_pair(ref, 2 * slots, 1)
    weight = jnp.broadcast_to(prob[...], (128, slots)).T[:, :1]
    output[...] = (ffn.astype(jnp.bfloat16).astype(jnp.float32) * weight).astype(jnp.bfloat16)
    tokens_grad[...] = grad.astype(jnp.bfloat16)
    prob_grad[...] = router[:, :slots] / prob[...]


def finish(prob, own, got):
    slots, width = (own.shape[0] - EXTRA) // 2, own.shape[1]
    part = jax.ShapeDtypeStruct((slots, width), jnp.bfloat16)
    return pl.pallas_call(
        finish_kernel,
        out_shape=(part, part, jax.ShapeDtypeStruct((1, slots), jnp.float32)),
        in_specs=[VMEM] * (2 + len(got)),
        out_specs=[VMEM] * 3,
        compiler_params=PARAMS,
    )(prob, own, *got)


def shards(tokens, cotangent, expert_ids, route_prob, gate_weight, up_weight, down_weight):
    wide_count = lax.axis_size("wide")
    narrow_count = lax.axis_size("narrow")
    expert_count = wide_count // 4
    tok_rows, features = tokens.shape
    width = features // narrow_count
    slots = min(4 * tok_rows // expert_count, tok_rows)
    direct = expert_count == 2 and slots == tok_rows
    place = lax.axis_index("narrow")
    masks = (1, 4, 5)
    groups = [
        [4 * e + 2 * b + a for e in range(expert_count) for a in range(2)] for b in range(2)
    ]

    weights = (gate_weight.T, up_weight.T, down_weight.T)
    if direct:
        keep, give, own, same, other = prologue(
            weights, (tokens, cotangent, expert_ids.T, route_prob[None, :]), width
        )
        mine = jnp.stack(
            [partner(part, "wide", mask) for mask, part in zip(masks, (same, other, other))]
        )
    else:
        own = None
        keep, give = prologue(weights, (), width)
        chosen = expert_ids[:, 0]
        onehot = (chosen[:, None] == jnp.arange(expert_count, dtype=jnp.int32)[None, :]).astype(
            jnp.int32
        )
        rank = jnp.sum((jnp.cumsum(onehot, axis=0) - onehot) * onehot, axis=1)
        slot_place = chosen * slots + rank
        source = (
            jnp.full((expert_count * slots,), tok_rows, jnp.int32)
            .at[slot_place]
            .set(jnp.arange(tok_rows, dtype=jnp.int32))
        )
        scaled = (route_prob[:, None] * cotangent.astype(jnp.float32)).astype(jnp.bfloat16)
        both = jnp.stack([tokens, scaled])
        both = lax.dynamic_slice_in_dim(both, place * width, width, 2)
        both = jnp.concatenate([both, jnp.zeros((2, 1, width), jnp.bfloat16)], 1)
        routed = both[:, source].reshape(2, expert_count, slots, width).transpose(1, 0, 2, 3)
        routed = jnp.repeat(routed, 2, axis=0)
        mine = lax.all_to_all(
            routed, "wide", split_axis=0, concat_axis=0, axis_index_groups=groups, tiled=True
        )

    from_x, from_z = lax.optimization_barrier(
        (partner(give, "wide", 1), partner(keep, "wide", 2))
    )
    from_d = partner(from_x, "wide", 2)
    across = partner(mine, "narrow", 2)
    pieces = (mine, partner(mine, "narrow", 1), across, partner(across, "narrow", 1))
    x_all, s_all, w_part, part = gather_parts(own, pieces, (keep, from_x, from_z))
    units, kept, sent, grad_d, grad_d_down = outer(x_all, s_all, w_part, part, from_d)
    got = partner(sent, "narrow", 1)
    got_d_down = partner(grad_d_down, "wide", 2)
    got_d = partner(grad_d, "wide", 2)
    if direct:
        to_y, to_x = first_parts(kept, got)
        units, _ = lax.optimization_barrier((units, to_y))
        ffn_held, ffn_x = ffn_parts(kept, got, partner(to_y, "narrow", 2))
        grad_own, grad_x, grad_x_down, grad_z = weight_grads(units, x_all, s_all)
        from_x = partner(to_x, "wide", 1)
        from_x, _ = lax.optimization_barrier((from_x, ffn_x))
        grad_held, grad_y = input_parts(kept, got, from_x)
        grad_z, _ = lax.optimization_barrier((grad_z, from_x))
        grad_x, _, _ = lax.optimization_barrier((grad_x, ffn_x, grad_y))
        grad_x_down = (grad_x_down + got_d_down.astype(jnp.float32)).astype(jnp.bfloat16)
        got_x_down = partner(grad_x_down, "wide", 1)
        grad_held, got_x_down = lax.optimization_barrier((grad_held, got_x_down))
        held, to_z = last_parts(
            ffn_held, partner(ffn_x, "wide", 1), grad_held, partner(grad_y, "narrow", 2)
        )
        grad_x = (grad_x + got_d.astype(jnp.float32)).astype(jnp.bfloat16)
        got_x = partner(grad_x, "wide", 1)
        given = write_half(give_kernel, grad_own.shape, (), (got_x, got_x_down))
        held, _ = lax.optimization_barrier((held, given[0]))
        output, tokens_grad, prob_grad = finish(
            route_prob[None, :], held, [partner(to_z, "wide", 4)]
        )
        prob_grad = prob_grad[0]
    else:
        grad_own, grad_x, grad_x_down, grad_z = weight_grads(units, x_all, s_all)
        grad_x_down = (grad_x_down + got_d_down.astype(jnp.float32)).astype(jnp.bfloat16)
        got_x_down = partner(grad_x_down, "wide", 1)
        grad_x = (grad_x + got_d.astype(jnp.float32)).astype(jnp.bfloat16)
        got_x = partner(grad_x, "wide", 1)
        across = partner(cross_part(kept, got), "narrow", 2)
        result = result_parts(kept, got, across)
        total = (result.shape[0] - EXTRA) // 2
        parts = result[: 2 * total].astype(jnp.bfloat16)
        parts = parts.reshape(2, 2 * expert_count, slots, width)
        back = lax.all_to_all(
            parts, "wide", split_axis=1, concat_axis=1, axis_index_groups=groups, tiled=True
        )
        back = back.reshape(2, expert_count, 2, slots, width).astype(jnp.float32).sum(2)
        back = back.reshape(2, expert_count * slots, width)[:, slot_place]
        router = result[2 * total : 2 * total + total // min(width, total), : min(width, total)]
        router = router.reshape(2 * expert_count, slots)
        high = lax.reduce_precision(router, 8, 7)
        pair = jnp.stack([high, router - high], 1).astype(jnp.bfloat16)
        pair = lax.all_to_all(
            pair, "wide", split_axis=0, concat_axis=0, axis_index_groups=groups, tiled=True
        )
        router = pair.reshape(expert_count, 4, slots).astype(jnp.float32).sum(1)
        prob_grad = router.reshape(expert_count * slots)[slot_place] / route_prob
        ffn = back[0].astype(jnp.bfloat16).astype(jnp.float32)
        output = (route_prob[:, None] * ffn).astype(jnp.bfloat16)
        tokens_grad = back[1].astype(jnp.bfloat16)
        given = write_half(give_kernel, grad_own.shape, (), (got_x, got_x_down))
    got_z = partner(grad_z, "wide", 2)
    gate_grad, up_grad, down_grad = write_half(
        keep_kernel, grad_own.shape, given, (grad_own, got_z)
    )
    return (output, tokens_grad, prob_grad, gate_grad.T, up_grad.T, down_grad.T)


def solution(mesh):
    in_specs = (
        P("wide", None),
        P("wide", None),
        P("wide", None),
        P("wide"),
        P("wide", "narrow"),
        P("wide", "narrow"),
        P("wide", "narrow"),
    )
    out_specs = (
        P("wide", "narrow"),
        P("wide", "narrow"),
        P("wide"),
        P("wide", "narrow"),
        P("wide", "narrow"),
        P("wide", "narrow"),
    )
    return jax.shard_map(shards, mesh=mesh, in_specs=in_specs, out_specs=out_specs, check_vma=False)
```

```python
import functools

import jax
import jax.numpy as jnp
from jax import lax
from jax.experimental import pallas as pl
from jax.experimental.pallas import tpu as pltpu
from jax.sharding import PartitionSpec as P

VMEM = pl.BlockSpec(memory_space=pltpu.VMEM)
HBM = pl.BlockSpec(memory_space=pltpu.HBM)
EXTRA = 16
PARAMS = pltpu.CompilerParams(vmem_limit_bytes=32 * 1024 * 1024)


def partner(x, axis, mask):
    return lax.ppermute(x, axis, [(i, i ^ mask) for i in range(lax.axis_size(axis))])


def dot_nn(left, right):
    return lax.dot_general(
        left, right, (((1,), (0,)), ((), ())), preferred_element_type=jnp.float32
    )


def dot_nt(left, right):
    return lax.dot_general(
        left, right, (((1,), (1,)), ((), ())), preferred_element_type=jnp.float32
    )


def at_quarter(index, width):
    return pl.ds(pl.multiple_of(index * width, width), width)


def packet_rows(rows):
    return 2 * rows + EXTRA


def put_pair(ref, first, value):
    count, lanes = value.shape
    high = value.astype(jnp.bfloat16).astype(jnp.float32)
    both = jnp.concatenate([high, value - high], 0)
    both = jnp.concatenate([both, jnp.zeros((EXTRA - 2 * count, lanes), jnp.float32)], 0)
    ref[first : first + EXTRA, :lanes] = both.astype(ref.dtype)


def get_pair(ref, first, count):
    both = ref[first : first + EXTRA, :].astype(jnp.float32)
    return both[:count] + both[count : 2 * count]


def prologue_kernel(routed, gate, up, down, *refs):
    if routed:
        tokens, cotangent, ids, prob, keep, give, own, same, other = refs[:9]
        held, ids_row, prob_row, sems = refs[9:]
        parts = ((tokens, held.at[0]), (cotangent, held.at[1]), (ids, ids_row), (prob, prob_row))
    else:
        keep, give, sems = refs
        parts = ()
    half = keep.shape[1]
    x_bit = lax.axis_index("wide") % 2
    keep_rows = pl.ds(pl.multiple_of(x_bit * half, 16), half)
    give_rows = pl.ds(pl.multiple_of((1 - x_bit) * half, 16), half)
    for i, ref in enumerate((gate, up, down)):
        parts += ((ref.at[keep_rows, :], keep.at[i]), (ref.at[give_rows, :], give.at[i]))
    copies = [pltpu.make_async_copy(src, dst, sems.at[i]) for i, (src, dst) in enumerate(parts)]
    for copy in copies:
        copy.start()
    if routed:
        for copy in copies[:4]:
            copy.wait()
        rows = held.shape[1]
        width = same.shape[2]
        mine = lax.axis_index("wide") // 4
        column = at_quarter(lax.axis_index("narrow"), width)
        chosen = jnp.broadcast_to(ids_row[...], (128, rows)).astype(jnp.float32).T[:, :1]
        weight = jnp.broadcast_to(prob_row[...], (128, rows)).T[:, :1]
        here = jnp.where(chosen == mine.astype(jnp.float32), 1.0, 0.0)
        for i in range(2):
            factor = weight if i else jnp.ones_like(weight)
            own[i] = (held[i].astype(jnp.float32) * (factor * here)).astype(jnp.bfloat16)
            part = held[i, :, column].astype(jnp.float32)
            same[i] = (part * (factor * here)).astype(jnp.bfloat16)
            other[i] = (part * (factor * (1.0 - here))).astype(jnp.bfloat16)
    for copy in copies[len(copies) - 6 :]:
        copy.wait()


def prologue(weights, token_args, width):
    hidden, quarter = weights[0].shape
    half = jax.ShapeDtypeStruct((3, hidden // 2, quarter), jnp.bfloat16)
    outs, scratch = (half, half), []
    if token_args:
        rows, features = token_args[0].shape
        part = jax.ShapeDtypeStruct((2, rows, width), jnp.bfloat16)
        outs += (jax.ShapeDtypeStruct((2, rows, features), jnp.bfloat16), part, part)
        scratch = [
            pltpu.VMEM((2, rows, features), jnp.bfloat16),
            pltpu.VMEM((1, rows), jnp.int32),
            pltpu.VMEM((1, rows), jnp.float32),
        ]
    return pl.pallas_call(
        functools.partial(prologue_kernel, bool(token_args)),
        out_shape=outs,
        in_specs=[HBM] * (3 + len(token_args)),
        out_specs=[VMEM] * len(outs),
        scratch_shapes=scratch + [pltpu.SemaphoreType.DMA((10,))],
        compiler_params=PARAMS,
    )(*[pltpu.with_memory_space_constraint(x, pltpu.HBM) for x in (*weights, *token_args)])


def stack_kernel(*refs):
    for i, ref in enumerate(refs[:-1]):
        refs[-1][i] = ref[...]


def stack_parts(parts):
    return pl.pallas_call(
        stack_kernel,
        out_shape=jax.ShapeDtypeStruct((len(parts), *parts[0].shape), parts[0].dtype),
        in_specs=[VMEM] * len(parts),
        out_specs=VMEM,
        compiler_params=PARAMS,
        cost_estimate=pl.CostEstimate(flops=2 * 10**9, bytes_accessed=0, transcendentals=0),
    )(*parts)


def gather_kernel(has_own, *refs):
    own = refs[0] if has_own else None
    pieces, weights = refs[has_own : has_own + 4], refs[has_own + 4 : has_own + 7]
    x_all, s_all, w_all, part = refs[has_own + 7 :]
    blocks, _, slots, width = pieces[0].shape
    half, reach = w_all.shape[1:]
    member = lax.axis_index("wide") % 4
    place = lax.axis_index("narrow")
    for k, ref in enumerate(weights):
        for i in range(3):
            w_all[i, :, k * width : (k + 1) * width] = ref[i]
    first = 0
    if has_own:
        for k in range(4):
            column = at_quarter(member ^ k, width)
            x_all[:slots, k * width : (k + 1) * width] = own[0, :, column]
            s_all[:slots, k * width : (k + 1) * width] = own[1, :, column]
        first = slots
    for mask, ref in enumerate(pieces):
        column = at_quarter(place ^ member ^ mask, width)
        for block in range(blocks):
            rows = slice(first + block * slots, first + (block + 1) * slots)
            x_all[rows, column] = ref[block, 0]
            s_all[rows, column] = ref[block, 1]
    total = x_all.shape[0]
    tile = min(2 * width, total)
    for step in range(total // tile):
        rows = slice(step * tile, (step + 1) * tile)
        both = dot_nt(w_all[0:2].reshape(2 * half, reach), x_all[rows, :reach])
        part[0:2, :, rows] = both.reshape(2, half, tile)
        part[2, :, rows] = dot_nt(w_all[2], s_all[rows, :reach])


def gather_parts(own, pieces, weights):
    blocks, _, slots, width = pieces[0].shape
    half = weights[0].shape[1]
    has_own = own is not None
    total = (blocks + has_own) * slots
    features = 4 * width
    return pl.pallas_call(
        functools.partial(gather_kernel, int(has_own)),
        out_shape=(
            jax.ShapeDtypeStruct((total, features), jnp.bfloat16),
            jax.ShapeDtypeStruct((total, features), jnp.bfloat16),
            jax.ShapeDtypeStruct((3, half, 3 * width), jnp.bfloat16),
            jax.ShapeDtypeStruct((3, half, total), jnp.float32),
        ),
        in_specs=[VMEM] * (7 + has_own),
        out_specs=[VMEM] * 4,
        compiler_params=PARAMS,
        cost_estimate=pl.CostEstimate(flops=1, bytes_accessed=1, transcendentals=0),
    )(*([own] if has_own else []), *pieces, *weights)


def grad_parts(units, x_all, s_all, column, outs):
    half, total = units.shape[1:]
    both = dot_nn(units[0:2].reshape(2 * half, total), x_all[:, column])
    down = dot_nn(units[2], s_all[:, column])
    for i, value in enumerate((both[:half], both[half:], down)):
        out = outs[0] if i < 2 else outs[-1]
        out[i if len(outs) == 1 else i % 2] = value.astype(out.dtype)


def outer_kernel(x_all, s_all, w_part, part, last, units, kept, sent, *refs):
    to_d, w_all, sums = refs[:2], refs[2], refs[3]
    half, width = last.shape[1:]
    offset = lax.axis_index("narrow") ^ lax.axis_index("wide") % 4
    last_column = slice(3 * width, 4 * width)
    for k in range(4):
        column = at_quarter(offset ^ k, width)
        for i in range(3):
            w_all[i, :, column] = last[i] if k == 3 else w_part[i, :, k * width : (k + 1) * width]
    total, tile = x_all.shape[0], sums.shape[2]
    lanes = min(width, total)
    for ref in (kept, sent):
        ref[:, 2 * total :, :] = jnp.zeros_like(ref[:, 2 * total :, :])
    routers = []
    for step in range(total // tile):
        rows = slice(step * tile, (step + 1) * tile)
        both = dot_nt(last[0:2].reshape(2 * half, width), x_all[rows, last_column])
        sums[0:2] = part[0:2, :, rows] + both.reshape(2, half, tile)
        sums[2] = part[2, :, rows] + dot_nt(last[2], s_all[rows, last_column])
        products = jnp.zeros((16, tile), jnp.float32)
        for low in range(0, half, 16):
            piece = slice(low, low + 16)
            gate, up, d_hidden = sums[0, piece, :], sums[1, piece, :], sums[2, piece, :]
            sigma = 0.5 + 0.5 * jnp.tanh(0.5 * gate)
            active = gate * sigma
            hidden = (active * up).astype(jnp.bfloat16)
            slope = sigma + active * (1.0 - sigma)
            units[0, piece, rows] = (d_hidden * up * slope).astype(jnp.bfloat16)
            units[1, piece, rows] = (d_hidden * active).astype(jnp.bfloat16)
            units[2, piece, rows] = hidden
            products = products + hidden.astype(jnp.float32) * d_hidden
        router = jnp.sum(products, axis=0, keepdims=True)
        routers += [router[:, low : low + lanes] for low in range(0, tile, lanes)]
        for low in range(step * tile, (step + 1) * tile, lanes):
            here = slice(low, low + lanes)
            lower = slice(total + low, total + low + lanes)
            out_part = dot_nn(units[2, :, here].T, w_all[2])
            left = units[0:2, :, here].reshape(2 * half, lanes).T
            in_part = dot_nn(left, w_all[0:2].reshape(2 * half, 4 * width))
            for mask in range(4):
                target = sent if mask % 2 else kept
                column = slice(mask * width, (mask + 1) * width)
                target[mask // 2, here, :] = out_part[:, column].astype(target.dtype)
                target[mask // 2, lower, :] = in_part[:, column].astype(target.dtype)
    router = jnp.concatenate(routers, 0)
    kept[0, 2 * total : 2 * total + len(routers), :lanes] = router
    put_pair(sent.at[0], 2 * total, router)
    grad_parts(units, x_all, s_all, last_column, to_d)


def outer(x_all, s_all, w_part, part, last):
    total, features = x_all.shape
    _, half, width = last.shape
    return pl.pallas_call(
        outer_kernel,
        out_shape=(
            jax.ShapeDtypeStruct((3, half, total), jnp.bfloat16),
            jax.ShapeDtypeStruct((2, packet_rows(total), width), jnp.float32),
            jax.ShapeDtypeStruct((2, packet_rows(total), width), jnp.bfloat16),
            jax.ShapeDtypeStruct((2, half, width), jnp.bfloat16),
            jax.ShapeDtypeStruct((1, half, width), jnp.bfloat16),
        ),
        in_specs=[VMEM] * 5,
        out_specs=[VMEM] * 5,
        scratch_shapes=[
            pltpu.VMEM((3, half, features), jnp.bfloat16),
            pltpu.VMEM((3, half, min(2 * width, total)), jnp.float32),
        ],
        compiler_params=PARAMS,
        cost_estimate=pl.CostEstimate(
            flops=8 * half * features * total, bytes_accessed=0, transcendentals=0
        ),
    )(x_all, s_all, w_part, part, last)


def grads_kernel(units, x_all, s_all, own, to_x, to_x_down, to_z):
    width = own.shape[2]
    for k, outs in enumerate(((own,), (to_x, to_x_down), (to_z,))):
        grad_parts(units, x_all, s_all, slice(k * width, (k + 1) * width), outs)


def weight_grads(units, x_all, s_all):
    half, total = units.shape[1:]
    features = x_all.shape[1]
    shapes = ((3, jnp.float32), (2, jnp.float32), (1, jnp.float32), (3, jnp.bfloat16))
    return pl.pallas_call(
        grads_kernel,
        out_shape=tuple(
            jax.ShapeDtypeStruct((count, half, features // 4), kind) for count, kind in shapes
        ),
        in_specs=[VMEM] * 3,
        out_specs=[VMEM] * 4,
        compiler_params=PARAMS,
        cost_estimate=pl.CostEstimate(flops=5 * half * features * total, bytes_accessed=0, transcendentals=0),
    )(units, x_all, s_all)


def write_rows(values, outs, held, sems, first):
    rows = pl.ds(pl.multiple_of(first, 16), held.shape[1])
    copies = []
    for i, out in enumerate(outs):
        held[i] = values(i)
        copies.append(pltpu.make_async_copy(held.at[i], out.at[rows, :], sems.at[i]))
        copies[-1].start()
    for copy in copies:
        copy.wait()


def give_kernel(got, got_down, out_0, out_1, out_2, held, sems):
    def values(i):
        return (got[i] if i < 2 else got_down[0]).astype(jnp.float32)

    first = (1 - lax.axis_index("wide") % 2) * held.shape[1]
    write_rows(values, (out_0, out_1, out_2), held, sems, first)


def keep_kernel(in_0, in_1, in_2, own, got, out_0, out_1, out_2, held, sems):
    def values(i):
        return own[i] + got[i].astype(jnp.float32)

    first = lax.axis_index("wide") % 2 * held.shape[1]
    write_rows(values, (out_0, out_1, out_2), held, sems, first)


def write_half(kernel, shape, held, values):
    held_in = [pltpu.with_memory_space_constraint(x, pltpu.HBM) for x in held]
    return pl.pallas_call(
        kernel,
        out_shape=(jax.ShapeDtypeStruct((2 * shape[1], shape[2]), jnp.float32),) * 3,
        in_specs=[HBM] * len(held) + [VMEM] * len(values),
        out_specs=[HBM] * 3,
        scratch_shapes=[pltpu.VMEM(shape, jnp.float32), pltpu.SemaphoreType.DMA((3,))],
        input_output_aliases={i: i for i in range(len(held))},
        compiler_params=PARAMS,
        cost_estimate=pl.CostEstimate(flops=1, bytes_accessed=0, transcendentals=0),
    )(*held_in, *values)


def cross_kernel(kept, got, sent):
    total = (kept.shape[1] - EXTRA) // 2
    tile = min(kept.shape[2], total)
    count = total // tile
    body = slice(0, 2 * total)
    sent[body, :] = (kept[1, body, :] + got[1, body, :].astype(jnp.float32)).astype(sent.dtype)
    sent[2 * total :, :] = jnp.zeros_like(sent[2 * total :, :])
    router = kept[0, 2 * total : 2 * total + count, :] + get_pair(got.at[0], 2 * total, count)
    put_pair(sent, 2 * total, router)


def cross_part(kept, got):
    return pl.pallas_call(
        cross_kernel,
        out_shape=jax.ShapeDtypeStruct(got.shape[1:], got.dtype),
        in_specs=[VMEM] * 2,
        out_specs=VMEM,
        compiler_params=PARAMS,
    )(kept, got)


def result_kernel(kept, got, across, out):
    total = (kept.shape[1] - EXTRA) // 2
    count = total // min(kept.shape[2], total)
    body, tail = slice(0, 2 * total), slice(2 * total, 2 * total + count)
    value = kept[0, body, :] + got[0, body, :].astype(jnp.float32)
    out[body, :] = value + across[body, :].astype(jnp.float32)
    out[2 * total :, :] = jnp.zeros_like(out[2 * total :, :])
    router = kept[0, tail, :] + get_pair(got.at[0], 2 * total, count)
    out[tail, :] = router + get_pair(across, 2 * total, count)


def result_parts(kept, got, across):
    return pl.pallas_call(
        result_kernel,
        out_shape=jax.ShapeDtypeStruct(kept.shape[1:], jnp.float32),
        in_specs=[VMEM] * 3,
        out_specs=VMEM,
        compiler_params=PARAMS,
    )(kept, got, across)


def first_kernel(kept, got, to_y, to_x):
    total = (kept.shape[1] - EXTRA) // 2
    slots = total // 4
    count = total // min(kept.shape[2], total)
    body = slice(0, total)
    to_y[body, :] = (kept[1, body, :] + got[1, body, :].astype(jnp.float32)).astype(to_y.dtype)
    put_pair(
        to_y,
        total,
        kept[0, 2 * total : 2 * total + count, :] + get_pair(got.at[0], 2 * total, count),
    )
    for part in range(2):
        for block in range(2):
            rows = slice(total + (2 * block + 1) * slots, total + (2 * block + 2) * slots)
            value = kept[part, rows, :] + got[part, rows, :].astype(jnp.float32)
            to_x[part, block * slots : (block + 1) * slots, :] = value.astype(to_x.dtype)


def first_parts(kept, got):
    total, width = (kept.shape[1] - EXTRA) // 2, kept.shape[2]
    return pl.pallas_call(
        first_kernel,
        out_shape=(
            jax.ShapeDtypeStruct((total + EXTRA, width), jnp.bfloat16),
            jax.ShapeDtypeStruct((2, total // 2, width), jnp.bfloat16),
        ),
        in_specs=[VMEM] * 2,
        out_specs=[VMEM] * 2,
        compiler_params=PARAMS,
    )(kept, got)


def ffn_kernel(kept, got, from_y, held, to_x):
    total = (kept.shape[1] - EXTRA) // 2
    slots, width = total // 4, kept.shape[2]
    count = total // min(width, total)
    router = kept[0, 2 * total : 2 * total + count, :] + get_pair(got.at[0], 2 * total, count)
    router = router + get_pair(from_y, total, count)
    pairs = []
    for block in range(4):
        rows = slice(block * slots, (block + 1) * slots)
        value = kept[0, rows, :] + got[0, rows, :].astype(jnp.float32)
        value = value + from_y[rows, :].astype(jnp.float32)
        out = to_x if block % 2 else held
        place = block // 2
        out[place * slots : (place + 1) * slots, :] = value.astype(out.dtype)
        lane = block * slots % width
        pairs.append(router[block * slots // width :, lane : lane + slots][:1])
    held[2 * slots :, :] = jnp.zeros_like(held[2 * slots :, :])
    to_x[2 * slots :, :] = jnp.zeros_like(to_x[2 * slots :, :])
    held[2 * slots : 2 * slots + 1, :slots] = pairs[0]
    held[2 * slots + 1 : 2 * slots + 2, :slots] = pairs[2]
    put_pair(to_x, 2 * slots, jnp.concatenate([pairs[1], pairs[3]], 0))


def ffn_parts(kept, got, from_y):
    total, width = (kept.shape[1] - EXTRA) // 2, kept.shape[2]
    shape = (total // 2 + EXTRA, width)
    return pl.pallas_call(
        ffn_kernel,
        out_shape=(
            jax.ShapeDtypeStruct(shape, jnp.float32),
            jax.ShapeDtypeStruct(shape, jnp.bfloat16),
        ),
        in_specs=[VMEM] * 3,
        out_specs=[VMEM] * 2,
        compiler_params=PARAMS,
    )(kept, got, from_y)


def input_kernel(kept, got, from_x, held, to_y):
    total = (kept.shape[1] - EXTRA) // 2
    slots = total // 4
    for part, out in enumerate((held, to_y)):
        for block in range(2):
            rows = slice(total + 2 * block * slots, total + (2 * block + 1) * slots)
            here = slice(block * slots, (block + 1) * slots)
            value = kept[part, rows, :] + got[part, rows, :].astype(jnp.float32)
            out[here, :] = (value + from_x[part, here, :].astype(jnp.float32)).astype(out.dtype)


def input_parts(kept, got, from_x):
    shape = from_x.shape[1:]
    return pl.pallas_call(
        input_kernel,
        out_shape=(
            jax.ShapeDtypeStruct(shape, jnp.float32),
            jax.ShapeDtypeStruct(shape, jnp.bfloat16),
        ),
        in_specs=[VMEM] * 3,
        out_specs=[VMEM] * 2,
        compiler_params=PARAMS,
    )(kept, got, from_x)


def last_kernel(ffn, from_x, grad, from_y, held, to_z):
    slots = grad.shape[0] // 2
    router = ffn[2 * slots : 2 * slots + 2, :] + get_pair(from_x, 2 * slots, 2)
    for block, out in enumerate((held, to_z)):
        rows = slice(block * slots, (block + 1) * slots)
        out[:slots, :] = (ffn[rows, :] + from_x[rows, :].astype(jnp.float32)).astype(out.dtype)
        out[slots : 2 * slots, :] = (grad[rows, :] + from_y[rows, :].astype(jnp.float32)).astype(
            out.dtype
        )
    held[2 * slots :, :] = jnp.broadcast_to(router[:1], (EXTRA, router.shape[1]))
    put_pair(to_z, 2 * slots, router[1:])


def last_parts(ffn, from_x, grad, from_y):
    return pl.pallas_call(
        last_kernel,
        out_shape=(
            jax.ShapeDtypeStruct(ffn.shape, jnp.float32),
            jax.ShapeDtypeStruct(ffn.shape, jnp.bfloat16),
        ),
        in_specs=[VMEM] * 4,
        out_specs=[VMEM] * 2,
        compiler_params=PARAMS,
        cost_estimate=pl.CostEstimate(flops=2 * 10**9, bytes_accessed=0, transcendentals=0),
    )(ffn, from_x, grad, from_y)


def finish_kernel(prob, own, *refs):
    got, (output, tokens_grad, prob_grad) = refs[:-3], refs[-3:]
    slots, width = output.shape
    ffn, grad = own[:slots, :], own[slots : 2 * slots, :]
    router = own[2 * slots : 2 * slots + 1, :]
    for ref in got:
        ffn = ffn + ref[:slots, :].astype(jnp.float32)
        grad = grad + ref[slots : 2 * slots, :].astype(jnp.float32)
        router = router + get_pair(ref, 2 * slots, 1)
    weight = jnp.broadcast_to(prob[...], (128, slots)).T[:, :1]
    output[...] = (ffn.astype(jnp.bfloat16).astype(jnp.float32) * weight).astype(jnp.bfloat16)
    tokens_grad[...] = grad.astype(jnp.bfloat16)
    prob_grad[...] = router[:, :slots] / prob[...]


def finish(prob, own, got):
    slots, width = (own.shape[0] - EXTRA) // 2, own.shape[1]
    part = jax.ShapeDtypeStruct((slots, width), jnp.bfloat16)
    return pl.pallas_call(
        finish_kernel,
        out_shape=(part, part, jax.ShapeDtypeStruct((1, slots), jnp.float32)),
        in_specs=[VMEM] * (2 + len(got)),
        out_specs=[VMEM] * 3,
        compiler_params=PARAMS,
    )(prob, own, *got)


def shards(tokens, cotangent, expert_ids, route_prob, gate_weight, up_weight, down_weight):
    wide_count = lax.axis_size("wide")
    narrow_count = lax.axis_size("narrow")
    expert_count = wide_count // 4
    tok_rows, features = tokens.shape
    width = features // narrow_count
    slots = min(4 * tok_rows // expert_count, tok_rows)
    direct = expert_count == 2 and slots == tok_rows
    place = lax.axis_index("narrow")
    masks = (1, 4, 5)
    groups = [
        [4 * e + 2 * b + a for e in range(expert_count) for a in range(2)] for b in range(2)
    ]

    weights = (gate_weight.T, up_weight.T, down_weight.T)
    if direct:
        keep, give, own, same, other = prologue(
            weights, (tokens, cotangent, expert_ids.T, route_prob[None, :]), width
        )
        mine = stack_parts(
            [partner(part, "wide", mask) for mask, part in zip(masks, (same, other, other))]
        )
    else:
        own = None
        keep, give = prologue(weights, (), width)
        chosen = expert_ids[:, 0]
        onehot = (chosen[:, None] == jnp.arange(expert_count, dtype=jnp.int32)[None, :]).astype(
            jnp.int32
        )
        rank = jnp.sum((jnp.cumsum(onehot, axis=0) - onehot) * onehot, axis=1)
        slot_place = chosen * slots + rank
        source = (
            jnp.full((expert_count * slots,), tok_rows, jnp.int32)
            .at[slot_place]
            .set(jnp.arange(tok_rows, dtype=jnp.int32))
        )
        scaled = (route_prob[:, None] * cotangent.astype(jnp.float32)).astype(jnp.bfloat16)
        both = jnp.stack([tokens, scaled])
        both = lax.dynamic_slice_in_dim(both, place * width, width, 2)
        both = jnp.concatenate([both, jnp.zeros((2, 1, width), jnp.bfloat16)], 1)
        routed = both[:, source].reshape(2, expert_count, slots, width).transpose(1, 0, 2, 3)
        routed = jnp.repeat(routed, 2, axis=0)
        mine = lax.all_to_all(
            routed, "wide", split_axis=0, concat_axis=0, axis_index_groups=groups, tiled=True
        )

    from_x, from_z = lax.optimization_barrier(
        (partner(give, "wide", 1), partner(keep, "wide", 2))
    )
    from_d = partner(from_x, "wide", 2)
    across = partner(mine, "narrow", 2)
    pieces = (mine, partner(mine, "narrow", 1), across, partner(across, "narrow", 1))
    x_all, s_all, w_part, part = gather_parts(own, pieces, (keep, from_x, from_z))
    units, kept, sent, grad_d, grad_d_down = outer(x_all, s_all, w_part, part, from_d)
    got = partner(sent, "narrow", 1)
    got_d_down = partner(grad_d_down, "wide", 2)
    got_d = partner(grad_d, "wide", 2)
    if direct:
        to_y, to_x = first_parts(kept, got)
        units, _ = lax.optimization_barrier((units, to_y))
        ffn_held, ffn_x = ffn_parts(kept, got, partner(to_y, "narrow", 2))
        grad_own, grad_x, grad_x_down, grad_z = weight_grads(units, x_all, s_all)
        from_x = partner(to_x, "wide", 1)
        from_x, _ = lax.optimization_barrier((from_x, ffn_x))
        grad_held, grad_y = input_parts(kept, got, from_x)
        grad_z, _ = lax.optimization_barrier((grad_z, from_x))
        grad_x, _, _ = lax.optimization_barrier((grad_x, ffn_x, grad_y))
        grad_x_down = (grad_x_down + got_d_down.astype(jnp.float32)).astype(jnp.bfloat16)
        got_x_down = partner(grad_x_down, "wide", 1)
        grad_held, got_x_down = lax.optimization_barrier((grad_held, got_x_down))
        held, to_z = last_parts(
            ffn_held, partner(ffn_x, "wide", 1), grad_held, partner(grad_y, "narrow", 2)
        )
        grad_x = (grad_x + got_d.astype(jnp.float32)).astype(jnp.bfloat16)
        got_x = partner(grad_x, "wide", 1)
        given = write_half(give_kernel, grad_own.shape, (), (got_x, got_x_down))
        held, _ = lax.optimization_barrier((held, given[0]))
        output, tokens_grad, prob_grad = finish(
            route_prob[None, :], held, [partner(to_z, "wide", 4)]
        )
        prob_grad = prob_grad[0]
    else:
        grad_own, grad_x, grad_x_down, grad_z = weight_grads(units, x_all, s_all)
        grad_x_down = (grad_x_down + got_d_down.astype(jnp.float32)).astype(jnp.bfloat16)
        got_x_down = partner(grad_x_down, "wide", 1)
        grad_x = (grad_x + got_d.astype(jnp.float32)).astype(jnp.bfloat16)
        got_x = partner(grad_x, "wide", 1)
        across = partner(cross_part(kept, got), "narrow", 2)
        result = result_parts(kept, got, across)
        total = (result.shape[0] - EXTRA) // 2
        parts = result[: 2 * total].astype(jnp.bfloat16)
        parts = parts.reshape(2, 2 * expert_count, slots, width)
        back = lax.all_to_all(
            parts, "wide", split_axis=1, concat_axis=1, axis_index_groups=groups, tiled=True
        )
        back = back.reshape(2, expert_count, 2, slots, width).astype(jnp.float32).sum(2)
        back = back.reshape(2, expert_count * slots, width)[:, slot_place]
        router = result[2 * total : 2 * total + total // min(width, total), : min(width, total)]
        router = router.reshape(2 * expert_count, slots)
        high = lax.reduce_precision(router, 8, 7)
        pair = jnp.stack([high, router - high], 1).astype(jnp.bfloat16)
        pair = lax.all_to_all(
            pair, "wide", split_axis=0, concat_axis=0, axis_index_groups=groups, tiled=True
        )
        router = pair.reshape(expert_count, 4, slots).astype(jnp.float32).sum(1)
        prob_grad = router.reshape(expert_count * slots)[slot_place] / route_prob
        ffn = back[0].astype(jnp.bfloat16).astype(jnp.float32)
        output = (route_prob[:, None] * ffn).astype(jnp.bfloat16)
        tokens_grad = back[1].astype(jnp.bfloat16)
        given = write_half(give_kernel, grad_own.shape, (), (got_x, got_x_down))
    got_z = partner(grad_z, "wide", 2)
    gate_grad, up_grad, down_grad = write_half(
        keep_kernel, grad_own.shape, given, (grad_own, got_z)
    )
    return (output, tokens_grad, prob_grad, gate_grad.T, up_grad.T, down_grad.T)


def solution(mesh):
    in_specs = (
        P("wide", None),
        P("wide", None),
        P("wide", None),
        P("wide"),
        P("wide", "narrow"),
        P("wide", "narrow"),
        P("wide", "narrow"),
    )
    out_specs = (
        P("wide", "narrow"),
        P("wide", "narrow"),
        P("wide"),
        P("wide", "narrow"),
        P("wide", "narrow"),
        P("wide", "narrow"),
    )
    return jax.shard_map(shards, mesh=mesh, in_specs=in_specs, out_specs=out_specs, check_vma=False)
```

```python
import functools

import jax
import jax.numpy as jnp
from jax import lax
from jax.experimental import pallas as pl
from jax.experimental.pallas import tpu as pltpu
from jax.sharding import PartitionSpec as P

VMEM = pl.BlockSpec(memory_space=pltpu.VMEM)
HBM = pl.BlockSpec(memory_space=pltpu.HBM)
EXTRA = 16
PARAMS = pltpu.CompilerParams(vmem_limit_bytes=32 * 1024 * 1024)


def partner(x, axis, mask):
    return lax.ppermute(x, axis, [(i, i ^ mask) for i in range(lax.axis_size(axis))])


def dot_nn(left, right):
    return lax.dot_general(
        left, right, (((1,), (0,)), ((), ())), preferred_element_type=jnp.float32
    )


def dot_nt(left, right):
    return lax.dot_general(
        left, right, (((1,), (1,)), ((), ())), preferred_element_type=jnp.float32
    )


def at_quarter(index, width):
    return pl.ds(pl.multiple_of(index * width, width), width)


def packet_rows(rows):
    return 2 * rows + EXTRA


def put_pair(ref, first, value):
    count, lanes = value.shape
    high = value.astype(jnp.bfloat16).astype(jnp.float32)
    both = jnp.concatenate([high, value - high], 0)
    both = jnp.concatenate([both, jnp.zeros((EXTRA - 2 * count, lanes), jnp.float32)], 0)
    ref[first : first + EXTRA, :lanes] = both.astype(ref.dtype)


def get_pair(ref, first, count):
    both = ref[first : first + EXTRA, :].astype(jnp.float32)
    return both[:count] + both[count : 2 * count]


def prologue_kernel(routed, gate, up, down, *refs):
    if routed:
        tokens, cotangent, ids, prob, keep, give, own, same, other = refs[:9]
        held, ids_row, prob_row, sems = refs[9:]
        parts = ((tokens, held.at[0]), (cotangent, held.at[1]), (ids, ids_row), (prob, prob_row))
    else:
        keep, give, sems = refs
        parts = ()
    half = keep.shape[1]
    x_bit = lax.axis_index("wide") % 2
    keep_rows = pl.ds(pl.multiple_of(x_bit * half, 16), half)
    give_rows = pl.ds(pl.multiple_of((1 - x_bit) * half, 16), half)
    for i, ref in enumerate((gate, up, down)):
        parts += ((ref.at[keep_rows, :], keep.at[i]), (ref.at[give_rows, :], give.at[i]))
    copies = [pltpu.make_async_copy(src, dst, sems.at[i]) for i, (src, dst) in enumerate(parts)]
    for copy in copies:
        copy.start()
    if routed:
        for copy in copies[:4]:
            copy.wait()
        rows = held.shape[1]
        width = same.shape[2]
        mine = lax.axis_index("wide") // 4
        column = at_quarter(lax.axis_index("narrow"), width)
        chosen = jnp.broadcast_to(ids_row[...], (128, rows)).astype(jnp.float32).T[:, :1]
        weight = jnp.broadcast_to(prob_row[...], (128, rows)).T[:, :1]
        here = jnp.where(chosen == mine.astype(jnp.float32), 1.0, 0.0)
        for i in range(2):
            factor = weight if i else jnp.ones_like(weight)
            own[i] = (held[i].astype(jnp.float32) * (factor * here)).astype(jnp.bfloat16)
            part = held[i, :, column].astype(jnp.float32)
            same[i] = (part * (factor * here)).astype(jnp.bfloat16)
            other[i] = (part * (factor * (1.0 - here))).astype(jnp.bfloat16)
    for copy in copies[len(copies) - 6 :]:
        copy.wait()


def prologue(weights, token_args, width):
    hidden, quarter = weights[0].shape
    half = jax.ShapeDtypeStruct((3, hidden // 2, quarter), jnp.bfloat16)
    outs, scratch = (half, half), []
    if token_args:
        rows, features = token_args[0].shape
        part = jax.ShapeDtypeStruct((2, rows, width), jnp.bfloat16)
        outs += (jax.ShapeDtypeStruct((2, rows, features), jnp.bfloat16), part, part)
        scratch = [
            pltpu.VMEM((2, rows, features), jnp.bfloat16),
            pltpu.VMEM((1, rows), jnp.int32),
            pltpu.VMEM((1, rows), jnp.float32),
        ]
    return pl.pallas_call(
        functools.partial(prologue_kernel, bool(token_args)),
        out_shape=outs,
        in_specs=[HBM] * (3 + len(token_args)),
        out_specs=[VMEM] * len(outs),
        scratch_shapes=scratch + [pltpu.SemaphoreType.DMA((10,))],
        compiler_params=PARAMS,
    )(*[pltpu.with_memory_space_constraint(x, pltpu.HBM) for x in (*weights, *token_args)])


def stack_kernel(*refs):
    for i, ref in enumerate(refs[:-1]):
        refs[-1][i] = ref[...]


def stack_parts(parts):
    return pl.pallas_call(
        stack_kernel,
        out_shape=jax.ShapeDtypeStruct((len(parts), *parts[0].shape), parts[0].dtype),
        in_specs=[VMEM] * len(parts),
        out_specs=VMEM,
        compiler_params=PARAMS,
        cost_estimate=pl.CostEstimate(flops=1 * 10**9, bytes_accessed=0, transcendentals=0),
    )(*parts)


def gather_kernel(has_own, *refs):
    own = refs[0] if has_own else None
    pieces, weights = refs[has_own : has_own + 4], refs[has_own + 4 : has_own + 7]
    x_all, s_all, w_all, part = refs[has_own + 7 :]
    blocks, _, slots, width = pieces[0].shape
    half, reach = w_all.shape[1:]
    member = lax.axis_index("wide") % 4
    place = lax.axis_index("narrow")
    for k, ref in enumerate(weights):
        for i in range(3):
            w_all[i, :, k * width : (k + 1) * width] = ref[i]
    first = 0
    if has_own:
        for k in range(4):
            column = at_quarter(member ^ k, width)
            x_all[:slots, k * width : (k + 1) * width] = own[0, :, column]
            s_all[:slots, k * width : (k + 1) * width] = own[1, :, column]
        first = slots
    for mask, ref in enumerate(pieces):
        column = at_quarter(place ^ member ^ mask, width)
        for block in range(blocks):
            rows = slice(first + block * slots, first + (block + 1) * slots)
            x_all[rows, column] = ref[block, 0]
            s_all[rows, column] = ref[block, 1]
    total = x_all.shape[0]
    tile = min(2 * width, total)
    for step in range(total // tile):
        rows = slice(step * tile, (step + 1) * tile)
        both = dot_nt(w_all[0:2].reshape(2 * half, reach), x_all[rows, :reach])
        part[0:2, :, rows] = both.reshape(2, half, tile)
        part[2, :, rows] = dot_nt(w_all[2], s_all[rows, :reach])


def gather_parts(own, pieces, weights):
    blocks, _, slots, width = pieces[0].shape
    half = weights[0].shape[1]
    has_own = own is not None
    total = (blocks + has_own) * slots
    features = 4 * width
    return pl.pallas_call(
        functools.partial(gather_kernel, int(has_own)),
        out_shape=(
            jax.ShapeDtypeStruct((total, features), jnp.bfloat16),
            jax.ShapeDtypeStruct((total, features), jnp.bfloat16),
            jax.ShapeDtypeStruct((3, half, 3 * width), jnp.bfloat16),
            jax.ShapeDtypeStruct((3, half, total), jnp.float32),
        ),
        in_specs=[VMEM] * (7 + has_own),
        out_specs=[VMEM] * 4,
        compiler_params=PARAMS,
        cost_estimate=pl.CostEstimate(flops=1, bytes_accessed=1, transcendentals=0),
    )(*([own] if has_own else []), *pieces, *weights)


def grad_parts(units, x_all, s_all, column, outs):
    half, total = units.shape[1:]
    both = dot_nn(units[0:2].reshape(2 * half, total), x_all[:, column])
    down = dot_nn(units[2], s_all[:, column])
    for i, value in enumerate((both[:half], both[half:], down)):
        out = outs[0] if i < 2 else outs[-1]
        out[i if len(outs) == 1 else i % 2] = value.astype(out.dtype)


def outer_kernel(x_all, s_all, w_part, part, last, units, kept, sent, *refs):
    to_d, w_all, sums = refs[:2], refs[2], refs[3]
    half, width = last.shape[1:]
    offset = lax.axis_index("narrow") ^ lax.axis_index("wide") % 4
    last_column = slice(3 * width, 4 * width)
    for k in range(4):
        column = at_quarter(offset ^ k, width)
        for i in range(3):
            w_all[i, :, column] = last[i] if k == 3 else w_part[i, :, k * width : (k + 1) * width]
    total, tile = x_all.shape[0], sums.shape[2]
    lanes = min(width, total)
    for ref in (kept, sent):
        ref[:, 2 * total :, :] = jnp.zeros_like(ref[:, 2 * total :, :])
    routers = []
    for step in range(total // tile):
        rows = slice(step * tile, (step + 1) * tile)
        both = dot_nt(last[0:2].reshape(2 * half, width), x_all[rows, last_column])
        sums[0:2] = part[0:2, :, rows] + both.reshape(2, half, tile)
        sums[2] = part[2, :, rows] + dot_nt(last[2], s_all[rows, last_column])
        products = jnp.zeros((16, tile), jnp.float32)
        for low in range(0, half, 16):
            piece = slice(low, low + 16)
            gate, up, d_hidden = sums[0, piece, :], sums[1, piece, :], sums[2, piece, :]
            sigma = 0.5 + 0.5 * jnp.tanh(0.5 * gate)
            active = gate * sigma
            hidden = (active * up).astype(jnp.bfloat16)
            slope = sigma + active * (1.0 - sigma)
            units[0, piece, rows] = (d_hidden * up * slope).astype(jnp.bfloat16)
            units[1, piece, rows] = (d_hidden * active).astype(jnp.bfloat16)
            units[2, piece, rows] = hidden
            products = products + hidden.astype(jnp.float32) * d_hidden
        router = jnp.sum(products, axis=0, keepdims=True)
        routers += [router[:, low : low + lanes] for low in range(0, tile, lanes)]
        for low in range(step * tile, (step + 1) * tile, lanes):
            here = slice(low, low + lanes)
            lower = slice(total + low, total + low + lanes)
            out_part = dot_nn(units[2, :, here].T, w_all[2])
            left = units[0:2, :, here].reshape(2 * half, lanes).T
            in_part = dot_nn(left, w_all[0:2].reshape(2 * half, 4 * width))
            for mask in range(4):
                target = sent if mask % 2 else kept
                column = slice(mask * width, (mask + 1) * width)
                target[mask // 2, here, :] = out_part[:, column].astype(target.dtype)
                target[mask // 2, lower, :] = in_part[:, column].astype(target.dtype)
    router = jnp.concatenate(routers, 0)
    kept[0, 2 * total : 2 * total + len(routers), :lanes] = router
    put_pair(sent.at[0], 2 * total, router)
    grad_parts(units, x_all, s_all, last_column, to_d)


def outer(x_all, s_all, w_part, part, last):
    total, features = x_all.shape
    _, half, width = last.shape
    return pl.pallas_call(
        outer_kernel,
        out_shape=(
            jax.ShapeDtypeStruct((3, half, total), jnp.bfloat16),
            jax.ShapeDtypeStruct((2, packet_rows(total), width), jnp.float32),
            jax.ShapeDtypeStruct((2, packet_rows(total), width), jnp.bfloat16),
            jax.ShapeDtypeStruct((2, half, width), jnp.bfloat16),
            jax.ShapeDtypeStruct((1, half, width), jnp.bfloat16),
        ),
        in_specs=[VMEM] * 5,
        out_specs=[VMEM] * 5,
        scratch_shapes=[
            pltpu.VMEM((3, half, features), jnp.bfloat16),
            pltpu.VMEM((3, half, min(2 * width, total)), jnp.float32),
        ],
        compiler_params=PARAMS,
        cost_estimate=pl.CostEstimate(
            flops=8 * half * features * total, bytes_accessed=0, transcendentals=0
        ),
    )(x_all, s_all, w_part, part, last)


def grads_kernel(units, x_all, s_all, own, to_x, to_x_down, to_z):
    width = own.shape[2]
    for k, outs in enumerate(((own,), (to_x, to_x_down), (to_z,))):
        grad_parts(units, x_all, s_all, slice(k * width, (k + 1) * width), outs)


def weight_grads(units, x_all, s_all):
    half, total = units.shape[1:]
    features = x_all.shape[1]
    shapes = ((3, jnp.float32), (2, jnp.float32), (1, jnp.float32), (3, jnp.bfloat16))
    return pl.pallas_call(
        grads_kernel,
        out_shape=tuple(
            jax.ShapeDtypeStruct((count, half, features // 4), kind) for count, kind in shapes
        ),
        in_specs=[VMEM] * 3,
        out_specs=[VMEM] * 4,
        compiler_params=PARAMS,
        cost_estimate=pl.CostEstimate(flops=5 * half * features * total, bytes_accessed=0, transcendentals=0),
    )(units, x_all, s_all)


def write_rows(values, outs, held, sems, first):
    rows = pl.ds(pl.multiple_of(first, 16), held.shape[1])
    copies = []
    for i, out in enumerate(outs):
        held[i] = values(i)
        copies.append(pltpu.make_async_copy(held.at[i], out.at[rows, :], sems.at[i]))
        copies[-1].start()
    for copy in copies:
        copy.wait()


def give_kernel(got, got_down, out_0, out_1, out_2, held, sems):
    def values(i):
        return (got[i] if i < 2 else got_down[0]).astype(jnp.float32)

    first = (1 - lax.axis_index("wide") % 2) * held.shape[1]
    write_rows(values, (out_0, out_1, out_2), held, sems, first)


def keep_kernel(in_0, in_1, in_2, own, got, out_0, out_1, out_2, held, sems):
    def values(i):
        return own[i] + got[i].astype(jnp.float32)

    first = lax.axis_index("wide") % 2 * held.shape[1]
    write_rows(values, (out_0, out_1, out_2), held, sems, first)


def write_half(kernel, shape, held, values):
    held_in = [pltpu.with_memory_space_constraint(x, pltpu.HBM) for x in held]
    return pl.pallas_call(
        kernel,
        out_shape=(jax.ShapeDtypeStruct((2 * shape[1], shape[2]), jnp.float32),) * 3,
        in_specs=[HBM] * len(held) + [VMEM] * len(values),
        out_specs=[HBM] * 3,
        scratch_shapes=[pltpu.VMEM(shape, jnp.float32), pltpu.SemaphoreType.DMA((3,))],
        input_output_aliases={i: i for i in range(len(held))},
        compiler_params=PARAMS,
        cost_estimate=pl.CostEstimate(flops=1, bytes_accessed=0, transcendentals=0),
    )(*held_in, *values)


def cross_kernel(kept, got, sent):
    total = (kept.shape[1] - EXTRA) // 2
    tile = min(kept.shape[2], total)
    count = total // tile
    body = slice(0, 2 * total)
    sent[body, :] = (kept[1, body, :] + got[1, body, :].astype(jnp.float32)).astype(sent.dtype)
    sent[2 * total :, :] = jnp.zeros_like(sent[2 * total :, :])
    router = kept[0, 2 * total : 2 * total + count, :] + get_pair(got.at[0], 2 * total, count)
    put_pair(sent, 2 * total, router)


def cross_part(kept, got):
    return pl.pallas_call(
        cross_kernel,
        out_shape=jax.ShapeDtypeStruct(got.shape[1:], got.dtype),
        in_specs=[VMEM] * 2,
        out_specs=VMEM,
        compiler_params=PARAMS,
    )(kept, got)


def result_kernel(kept, got, across, out):
    total = (kept.shape[1] - EXTRA) // 2
    count = total // min(kept.shape[2], total)
    body, tail = slice(0, 2 * total), slice(2 * total, 2 * total + count)
    value = kept[0, body, :] + got[0, body, :].astype(jnp.float32)
    out[body, :] = value + across[body, :].astype(jnp.float32)
    out[2 * total :, :] = jnp.zeros_like(out[2 * total :, :])
    router = kept[0, tail, :] + get_pair(got.at[0], 2 * total, count)
    out[tail, :] = router + get_pair(across, 2 * total, count)


def result_parts(kept, got, across):
    return pl.pallas_call(
        result_kernel,
        out_shape=jax.ShapeDtypeStruct(kept.shape[1:], jnp.float32),
        in_specs=[VMEM] * 3,
        out_specs=VMEM,
        compiler_params=PARAMS,
    )(kept, got, across)


def first_kernel(kept, got, to_y, to_x):
    total = (kept.shape[1] - EXTRA) // 2
    slots = total // 4
    count = total // min(kept.shape[2], total)
    body = slice(0, total)
    to_y[body, :] = (kept[1, body, :] + got[1, body, :].astype(jnp.float32)).astype(to_y.dtype)
    put_pair(
        to_y,
        total,
        kept[0, 2 * total : 2 * total + count, :] + get_pair(got.at[0], 2 * total, count),
    )
    for part in range(2):
        for block in range(2):
            rows = slice(total + (2 * block + 1) * slots, total + (2 * block + 2) * slots)
            value = kept[part, rows, :] + got[part, rows, :].astype(jnp.float32)
            to_x[part, block * slots : (block + 1) * slots, :] = value.astype(to_x.dtype)


def first_parts(kept, got):
    total, width = (kept.shape[1] - EXTRA) // 2, kept.shape[2]
    return pl.pallas_call(
        first_kernel,
        out_shape=(
            jax.ShapeDtypeStruct((total + EXTRA, width), jnp.bfloat16),
            jax.ShapeDtypeStruct((2, total // 2, width), jnp.bfloat16),
        ),
        in_specs=[VMEM] * 2,
        out_specs=[VMEM] * 2,
        compiler_params=PARAMS,
    )(kept, got)


def ffn_kernel(kept, got, from_y, held, to_x):
    total = (kept.shape[1] - EXTRA) // 2
    slots, width = total // 4, kept.shape[2]
    count = total // min(width, total)
    router = kept[0, 2 * total : 2 * total + count, :] + get_pair(got.at[0], 2 * total, count)
    router = router + get_pair(from_y, total, count)
    pairs = []
    for block in range(4):
        rows = slice(block * slots, (block + 1) * slots)
        value = kept[0, rows, :] + got[0, rows, :].astype(jnp.float32)
        value = value + from_y[rows, :].astype(jnp.float32)
        out = to_x if block % 2 else held
        place = block // 2
        out[place * slots : (place + 1) * slots, :] = value.astype(out.dtype)
        lane = block * slots % width
        pairs.append(router[block * slots // width :, lane : lane + slots][:1])
    held[2 * slots :, :] = jnp.zeros_like(held[2 * slots :, :])
    to_x[2 * slots :, :] = jnp.zeros_like(to_x[2 * slots :, :])
    held[2 * slots : 2 * slots + 1, :slots] = pairs[0]
    held[2 * slots + 1 : 2 * slots + 2, :slots] = pairs[2]
    put_pair(to_x, 2 * slots, jnp.concatenate([pairs[1], pairs[3]], 0))


def ffn_parts(kept, got, from_y):
    total, width = (kept.shape[1] - EXTRA) // 2, kept.shape[2]
    shape = (total // 2 + EXTRA, width)
    return pl.pallas_call(
        ffn_kernel,
        out_shape=(
            jax.ShapeDtypeStruct(shape, jnp.float32),
            jax.ShapeDtypeStruct(shape, jnp.bfloat16),
        ),
        in_specs=[VMEM] * 3,
        out_specs=[VMEM] * 2,
        compiler_params=PARAMS,
    )(kept, got, from_y)


def input_kernel(kept, got, from_x, held, to_y):
    total = (kept.shape[1] - EXTRA) // 2
    slots = total // 4
    for part, out in enumerate((held, to_y)):
        for block in range(2):
            rows = slice(total + 2 * block * slots, total + (2 * block + 1) * slots)
            here = slice(block * slots, (block + 1) * slots)
            value = kept[part, rows, :] + got[part, rows, :].astype(jnp.float32)
            out[here, :] = (value + from_x[part, here, :].astype(jnp.float32)).astype(out.dtype)


def input_parts(kept, got, from_x):
    shape = from_x.shape[1:]
    return pl.pallas_call(
        input_kernel,
        out_shape=(
            jax.ShapeDtypeStruct(shape, jnp.float32),
            jax.ShapeDtypeStruct(shape, jnp.bfloat16),
        ),
        in_specs=[VMEM] * 3,
        out_specs=[VMEM] * 2,
        compiler_params=PARAMS,
    )(kept, got, from_x)


def last_kernel(ffn, from_x, grad, from_y, held, to_z):
    slots = grad.shape[0] // 2
    router = ffn[2 * slots : 2 * slots + 2, :] + get_pair(from_x, 2 * slots, 2)
    for block, out in enumerate((held, to_z)):
        rows = slice(block * slots, (block + 1) * slots)
        out[:slots, :] = (ffn[rows, :] + from_x[rows, :].astype(jnp.float32)).astype(out.dtype)
        out[slots : 2 * slots, :] = (grad[rows, :] + from_y[rows, :].astype(jnp.float32)).astype(
            out.dtype
        )
    held[2 * slots :, :] = jnp.broadcast_to(router[:1], (EXTRA, router.shape[1]))
    put_pair(to_z, 2 * slots, router[1:])


def last_parts(ffn, from_x, grad, from_y):
    return pl.pallas_call(
        last_kernel,
        out_shape=(
            jax.ShapeDtypeStruct(ffn.shape, jnp.float32),
            jax.ShapeDtypeStruct(ffn.shape, jnp.bfloat16),
        ),
        in_specs=[VMEM] * 4,
        out_specs=[VMEM] * 2,
        compiler_params=PARAMS,
        cost_estimate=pl.CostEstimate(flops=2 * 10**9, bytes_accessed=0, transcendentals=0),
    )(ffn, from_x, grad, from_y)


def finish_kernel(prob, own, *refs):
    got, (output, tokens_grad, prob_grad) = refs[:-3], refs[-3:]
    slots, width = output.shape
    ffn, grad = own[:slots, :], own[slots : 2 * slots, :]
    router = own[2 * slots : 2 * slots + 1, :]
    for ref in got:
        ffn = ffn + ref[:slots, :].astype(jnp.float32)
        grad = grad + ref[slots : 2 * slots, :].astype(jnp.float32)
        router = router + get_pair(ref, 2 * slots, 1)
    weight = jnp.broadcast_to(prob[...], (128, slots)).T[:, :1]
    output[...] = (ffn.astype(jnp.bfloat16).astype(jnp.float32) * weight).astype(jnp.bfloat16)
    tokens_grad[...] = grad.astype(jnp.bfloat16)
    prob_grad[...] = router[:, :slots] / prob[...]


def finish(prob, own, got):
    slots, width = (own.shape[0] - EXTRA) // 2, own.shape[1]
    part = jax.ShapeDtypeStruct((slots, width), jnp.bfloat16)
    return pl.pallas_call(
        finish_kernel,
        out_shape=(part, part, jax.ShapeDtypeStruct((1, slots), jnp.float32)),
        in_specs=[VMEM] * (2 + len(got)),
        out_specs=[VMEM] * 3,
        compiler_params=PARAMS,
    )(prob, own, *got)


def shards(tokens, cotangent, expert_ids, route_prob, gate_weight, up_weight, down_weight):
    wide_count = lax.axis_size("wide")
    narrow_count = lax.axis_size("narrow")
    expert_count = wide_count // 4
    tok_rows, features = tokens.shape
    width = features // narrow_count
    slots = min(4 * tok_rows // expert_count, tok_rows)
    direct = expert_count == 2 and slots == tok_rows
    place = lax.axis_index("narrow")
    masks = (1, 4, 5)
    groups = [
        [4 * e + 2 * b + a for e in range(expert_count) for a in range(2)] for b in range(2)
    ]

    weights = (gate_weight.T, up_weight.T, down_weight.T)
    if direct:
        keep, give, own, same, other = prologue(
            weights, (tokens, cotangent, expert_ids.T, route_prob[None, :]), width
        )
        mine = stack_parts(
            [partner(part, "wide", mask) for mask, part in zip(masks, (same, other, other))]
        )
    else:
        own = None
        keep, give = prologue(weights, (), width)
        chosen = expert_ids[:, 0]
        onehot = (chosen[:, None] == jnp.arange(expert_count, dtype=jnp.int32)[None, :]).astype(
            jnp.int32
        )
        rank = jnp.sum((jnp.cumsum(onehot, axis=0) - onehot) * onehot, axis=1)
        slot_place = chosen * slots + rank
        source = (
            jnp.full((expert_count * slots,), tok_rows, jnp.int32)
            .at[slot_place]
            .set(jnp.arange(tok_rows, dtype=jnp.int32))
        )
        scaled = (route_prob[:, None] * cotangent.astype(jnp.float32)).astype(jnp.bfloat16)
        both = jnp.stack([tokens, scaled])
        both = lax.dynamic_slice_in_dim(both, place * width, width, 2)
        both = jnp.concatenate([both, jnp.zeros((2, 1, width), jnp.bfloat16)], 1)
        routed = both[:, source].reshape(2, expert_count, slots, width).transpose(1, 0, 2, 3)
        routed = jnp.repeat(routed, 2, axis=0)
        mine = lax.all_to_all(
            routed, "wide", split_axis=0, concat_axis=0, axis_index_groups=groups, tiled=True
        )

    from_x, from_z = partner(give, "wide", 1), partner(keep, "wide", 2)
    from_d = partner(from_x, "wide", 2)
    across, from_z = lax.optimization_barrier((partner(mine, "narrow", 2), from_z))
    pieces = (mine, partner(mine, "narrow", 1), across, partner(across, "narrow", 1))
    x_all, s_all, w_part, part = gather_parts(own, pieces, (keep, from_x, from_z))
    units, kept, sent, grad_d, grad_d_down = outer(x_all, s_all, w_part, part, from_d)
    got = partner(sent, "narrow", 1)
    got_d_down = partner(grad_d_down, "wide", 2)
    got_d = partner(grad_d, "wide", 2)
    if direct:
        to_y, to_x = first_parts(kept, got)
        units, _ = lax.optimization_barrier((units, to_y))
        ffn_held, ffn_x = ffn_parts(kept, got, partner(to_y, "narrow", 2))
        grad_own, grad_x, grad_x_down, grad_z = weight_grads(units, x_all, s_all)
        from_x = partner(to_x, "wide", 1)
        from_x, _ = lax.optimization_barrier((from_x, ffn_x))
        grad_held, grad_y = input_parts(kept, got, from_x)
        grad_z, _ = lax.optimization_barrier((grad_z, from_x))
        grad_x, _, _ = lax.optimization_barrier((grad_x, ffn_x, grad_y))
        grad_x_down = (grad_x_down + got_d_down.astype(jnp.float32)).astype(jnp.bfloat16)
        got_x_down = partner(grad_x_down, "wide", 1)
        grad_held, got_x_down = lax.optimization_barrier((grad_held, got_x_down))
        held, to_z = last_parts(
            ffn_held, partner(ffn_x, "wide", 1), grad_held, partner(grad_y, "narrow", 2)
        )
        grad_x = (grad_x + got_d.astype(jnp.float32)).astype(jnp.bfloat16)
        got_x = partner(grad_x, "wide", 1)
        given = write_half(give_kernel, grad_own.shape, (), (got_x, got_x_down))
        held, _ = lax.optimization_barrier((held, given[0]))
        output, tokens_grad, prob_grad = finish(
            route_prob[None, :], held, [partner(to_z, "wide", 4)]
        )
        prob_grad = prob_grad[0]
    else:
        grad_own, grad_x, grad_x_down, grad_z = weight_grads(units, x_all, s_all)
        grad_x_down = (grad_x_down + got_d_down.astype(jnp.float32)).astype(jnp.bfloat16)
        got_x_down = partner(grad_x_down, "wide", 1)
        grad_x = (grad_x + got_d.astype(jnp.float32)).astype(jnp.bfloat16)
        got_x = partner(grad_x, "wide", 1)
        across = partner(cross_part(kept, got), "narrow", 2)
        result = result_parts(kept, got, across)
        total = (result.shape[0] - EXTRA) // 2
        parts = result[: 2 * total].astype(jnp.bfloat16)
        parts = parts.reshape(2, 2 * expert_count, slots, width)
        back = lax.all_to_all(
            parts, "wide", split_axis=1, concat_axis=1, axis_index_groups=groups, tiled=True
        )
        back = back.reshape(2, expert_count, 2, slots, width).astype(jnp.float32).sum(2)
        back = back.reshape(2, expert_count * slots, width)[:, slot_place]
        router = result[2 * total : 2 * total + total // min(width, total), : min(width, total)]
        router = router.reshape(2 * expert_count, slots)
        high = lax.reduce_precision(router, 8, 7)
        pair = jnp.stack([high, router - high], 1).astype(jnp.bfloat16)
        pair = lax.all_to_all(
            pair, "wide", split_axis=0, concat_axis=0, axis_index_groups=groups, tiled=True
        )
        router = pair.reshape(expert_count, 4, slots).astype(jnp.float32).sum(1)
        prob_grad = router.reshape(expert_count * slots)[slot_place] / route_prob
        ffn = back[0].astype(jnp.bfloat16).astype(jnp.float32)
        output = (route_prob[:, None] * ffn).astype(jnp.bfloat16)
        tokens_grad = back[1].astype(jnp.bfloat16)
        given = write_half(give_kernel, grad_own.shape, (), (got_x, got_x_down))
    got_z = partner(grad_z, "wide", 2)
    gate_grad, up_grad, down_grad = write_half(
        keep_kernel, grad_own.shape, given, (grad_own, got_z)
    )
    return (output, tokens_grad, prob_grad, gate_grad.T, up_grad.T, down_grad.T)


def solution(mesh):
    in_specs = (
        P("wide", None),
        P("wide", None),
        P("wide", None),
        P("wide"),
        P("wide", "narrow"),
        P("wide", "narrow"),
        P("wide", "narrow"),
    )
    out_specs = (
        P("wide", "narrow"),
        P("wide", "narrow"),
        P("wide"),
        P("wide", "narrow"),
        P("wide", "narrow"),
        P("wide", "narrow"),
    )
    return jax.shard_map(shards, mesh=mesh, in_specs=in_specs, out_specs=out_specs, check_vma=False)
```

```python
import functools

import jax
import jax.numpy as jnp
from jax import lax
from jax.experimental import pallas as pl
from jax.experimental.pallas import tpu as pltpu
from jax.sharding import PartitionSpec as P

VMEM = pl.BlockSpec(memory_space=pltpu.VMEM)
HBM = pl.BlockSpec(memory_space=pltpu.HBM)
EXTRA = 16
PARAMS = pltpu.CompilerParams(vmem_limit_bytes=32 * 1024 * 1024)


def partner(x, axis, mask):
    return lax.ppermute(x, axis, [(i, i ^ mask) for i in range(lax.axis_size(axis))])


def dot_nn(left, right):
    return lax.dot_general(
        left, right, (((1,), (0,)), ((), ())), preferred_element_type=jnp.float32
    )


def dot_nt(left, right):
    return lax.dot_general(
        left, right, (((1,), (1,)), ((), ())), preferred_element_type=jnp.float32
    )


def at_quarter(index, width):
    return pl.ds(pl.multiple_of(index * width, width), width)


def packet_rows(rows):
    return 2 * rows + EXTRA


def put_pair(ref, first, value):
    count, lanes = value.shape
    high = value.astype(jnp.bfloat16).astype(jnp.float32)
    both = jnp.concatenate([high, value - high], 0)
    both = jnp.concatenate([both, jnp.zeros((EXTRA - 2 * count, lanes), jnp.float32)], 0)
    ref[first : first + EXTRA, :lanes] = both.astype(ref.dtype)


def get_pair(ref, first, count):
    both = ref[first : first + EXTRA, :].astype(jnp.float32)
    return both[:count] + both[count : 2 * count]


def prologue_kernel(routed, gate, up, down, *refs):
    if routed:
        tokens, cotangent, ids, prob, keep, give, own, same, other = refs[:9]
        held, ids_row, prob_row, sems = refs[9:]
        parts = ((tokens, held.at[0]), (cotangent, held.at[1]), (ids, ids_row), (prob, prob_row))
    else:
        keep, give, sems = refs
        parts = ()
    half = keep.shape[1]
    x_bit = lax.axis_index("wide") % 2
    keep_rows = pl.ds(pl.multiple_of(x_bit * half, 16), half)
    give_rows = pl.ds(pl.multiple_of((1 - x_bit) * half, 16), half)
    for i, ref in enumerate((gate, up, down)):
        parts += ((ref.at[keep_rows, :], keep.at[i]), (ref.at[give_rows, :], give.at[i]))
    copies = [pltpu.make_async_copy(src, dst, sems.at[i]) for i, (src, dst) in enumerate(parts)]
    for copy in copies:
        copy.start()
    if routed:
        for copy in copies[:4]:
            copy.wait()
        rows = held.shape[1]
        width = same.shape[2]
        mine = lax.axis_index("wide") // 4
        column = at_quarter(lax.axis_index("narrow"), width)
        chosen = jnp.broadcast_to(ids_row[...], (128, rows)).astype(jnp.float32).T[:, :1]
        weight = jnp.broadcast_to(prob_row[...], (128, rows)).T[:, :1]
        here = jnp.where(chosen == mine.astype(jnp.float32), 1.0, 0.0)
        for i in range(2):
            factor = weight if i else jnp.ones_like(weight)
            own[i] = (held[i].astype(jnp.float32) * (factor * here)).astype(jnp.bfloat16)
            part = held[i, :, column].astype(jnp.float32)
            same[i] = (part * (factor * here)).astype(jnp.bfloat16)
            other[i] = (part * (factor * (1.0 - here))).astype(jnp.bfloat16)
    for copy in copies[len(copies) - 6 :]:
        copy.wait()


def prologue(weights, token_args, width):
    hidden, quarter = weights[0].shape
    half = jax.ShapeDtypeStruct((3, hidden // 2, quarter), jnp.bfloat16)
    outs, scratch = (half, half), []
    if token_args:
        rows, features = token_args[0].shape
        part = jax.ShapeDtypeStruct((2, rows, width), jnp.bfloat16)
        outs += (jax.ShapeDtypeStruct((2, rows, features), jnp.bfloat16), part, part)
        scratch = [
            pltpu.VMEM((2, rows, features), jnp.bfloat16),
            pltpu.VMEM((1, rows), jnp.int32),
            pltpu.VMEM((1, rows), jnp.float32),
        ]
    return pl.pallas_call(
        functools.partial(prologue_kernel, bool(token_args)),
        out_shape=outs,
        in_specs=[HBM] * (3 + len(token_args)),
        out_specs=[VMEM] * len(outs),
        scratch_shapes=scratch + [pltpu.SemaphoreType.DMA((10,))],
        compiler_params=PARAMS,
    )(*[pltpu.with_memory_space_constraint(x, pltpu.HBM) for x in (*weights, *token_args)])


def stack_kernel(*refs):
    for i, ref in enumerate(refs[:-1]):
        refs[-1][i] = ref[...]


def stack_parts(parts):
    return pl.pallas_call(
        stack_kernel,
        out_shape=jax.ShapeDtypeStruct((len(parts), *parts[0].shape), parts[0].dtype),
        in_specs=[VMEM] * len(parts),
        out_specs=VMEM,
        compiler_params=PARAMS,
        cost_estimate=pl.CostEstimate(flops=2 * 10**9, bytes_accessed=0, transcendentals=0),
    )(*parts)


def gather_kernel(has_own, *refs):
    own = refs[0] if has_own else None
    pieces, weights = refs[has_own : has_own + 4], refs[has_own + 4 : has_own + 7]
    x_all, s_all, w_all, part = refs[has_own + 7 :]
    blocks, _, slots, width = pieces[0].shape
    half, reach = w_all.shape[1:]
    member = lax.axis_index("wide") % 4
    place = lax.axis_index("narrow")
    for k, ref in enumerate(weights):
        for i in range(3):
            w_all[i, :, k * width : (k + 1) * width] = ref[i]
    first = 0
    if has_own:
        for k in range(4):
            column = at_quarter(member ^ k, width)
            x_all[:slots, k * width : (k + 1) * width] = own[0, :, column]
            s_all[:slots, k * width : (k + 1) * width] = own[1, :, column]
        first = slots
    for mask, ref in enumerate(pieces):
        column = at_quarter(place ^ member ^ mask, width)
        for block in range(blocks):
            rows = slice(first + block * slots, first + (block + 1) * slots)
            x_all[rows, column] = ref[block, 0]
            s_all[rows, column] = ref[block, 1]
    total = x_all.shape[0]
    tile = min(2 * width, total)
    for step in range(total // tile):
        rows = slice(step * tile, (step + 1) * tile)
        both = dot_nt(w_all[0:2].reshape(2 * half, reach), x_all[rows, :reach])
        part[0:2, :, rows] = both.reshape(2, half, tile)
        part[2, :, rows] = dot_nt(w_all[2], s_all[rows, :reach])


def gather_parts(own, pieces, weights):
    blocks, _, slots, width = pieces[0].shape
    half = weights[0].shape[1]
    has_own = own is not None
    total = (blocks + has_own) * slots
    features = 4 * width
    return pl.pallas_call(
        functools.partial(gather_kernel, int(has_own)),
        out_shape=(
            jax.ShapeDtypeStruct((total, features), jnp.bfloat16),
            jax.ShapeDtypeStruct((total, features), jnp.bfloat16),
            jax.ShapeDtypeStruct((3, half, 3 * width), jnp.bfloat16),
            jax.ShapeDtypeStruct((3, half, total), jnp.float32),
        ),
        in_specs=[VMEM] * (7 + has_own),
        out_specs=[VMEM] * 4,
        compiler_params=PARAMS,
        cost_estimate=pl.CostEstimate(flops=1, bytes_accessed=1, transcendentals=0),
    )(*([own] if has_own else []), *pieces, *weights)


def grad_parts(units, x_all, s_all, column, outs):
    half, total = units.shape[1:]
    both = dot_nn(units[0:2].reshape(2 * half, total), x_all[:, column])
    down = dot_nn(units[2], s_all[:, column])
    for i, value in enumerate((both[:half], both[half:], down)):
        out = outs[0] if i < 2 else outs[-1]
        out[i if len(outs) == 1 else i % 2] = value.astype(out.dtype)


def outer_kernel(x_all, s_all, w_part, part, last, units, kept, sent, *refs):
    to_d, w_all, sums = refs[:2], refs[2], refs[3]
    half, width = last.shape[1:]
    offset = lax.axis_index("narrow") ^ lax.axis_index("wide") % 4
    last_column = slice(3 * width, 4 * width)
    for k in range(4):
        column = at_quarter(offset ^ k, width)
        for i in range(3):
            w_all[i, :, column] = last[i] if k == 3 else w_part[i, :, k * width : (k + 1) * width]
    total, tile = x_all.shape[0], sums.shape[2]
    lanes = min(width, total)
    for ref in (kept, sent):
        ref[:, 2 * total :, :] = jnp.zeros_like(ref[:, 2 * total :, :])
    routers = []
    for step in range(total // tile):
        rows = slice(step * tile, (step + 1) * tile)
        both = dot_nt(last[0:2].reshape(2 * half, width), x_all[rows, last_column])
        sums[0:2] = part[0:2, :, rows] + both.reshape(2, half, tile)
        sums[2] = part[2, :, rows] + dot_nt(last[2], s_all[rows, last_column])
        products = jnp.zeros((16, tile), jnp.float32)
        for low in range(0, half, 16):
            piece = slice(low, low + 16)
            gate, up, d_hidden = sums[0, piece, :], sums[1, piece, :], sums[2, piece, :]
            sigma = 0.5 + 0.5 * jnp.tanh(0.5 * gate)
            active = gate * sigma
            hidden = (active * up).astype(jnp.bfloat16)
            slope = sigma + active * (1.0 - sigma)
            units[0, piece, rows] = (d_hidden * up * slope).astype(jnp.bfloat16)
            units[1, piece, rows] = (d_hidden * active).astype(jnp.bfloat16)
            units[2, piece, rows] = hidden
            products = products + hidden.astype(jnp.float32) * d_hidden
        router = jnp.sum(products, axis=0, keepdims=True)
        routers += [router[:, low : low + lanes] for low in range(0, tile, lanes)]
        for low in range(step * tile, (step + 1) * tile, lanes):
            here = slice(low, low + lanes)
            lower = slice(total + low, total + low + lanes)
            out_part = dot_nn(units[2, :, here].T, w_all[2])
            left = units[0:2, :, here].reshape(2 * half, lanes).T
            in_part = dot_nn(left, w_all[0:2].reshape(2 * half, 4 * width))
            for mask in range(4):
                target = sent if mask % 2 else kept
                column = slice(mask * width, (mask + 1) * width)
                target[mask // 2, here, :] = out_part[:, column].astype(target.dtype)
                target[mask // 2, lower, :] = in_part[:, column].astype(target.dtype)
    router = jnp.concatenate(routers, 0)
    kept[0, 2 * total : 2 * total + len(routers), :lanes] = router
    put_pair(sent.at[0], 2 * total, router)
    grad_parts(units, x_all, s_all, last_column, to_d)


def outer(x_all, s_all, w_part, part, last):
    total, features = x_all.shape
    _, half, width = last.shape
    return pl.pallas_call(
        outer_kernel,
        out_shape=(
            jax.ShapeDtypeStruct((3, half, total), jnp.bfloat16),
            jax.ShapeDtypeStruct((2, packet_rows(total), width), jnp.float32),
            jax.ShapeDtypeStruct((2, packet_rows(total), width), jnp.bfloat16),
            jax.ShapeDtypeStruct((2, half, width), jnp.bfloat16),
            jax.ShapeDtypeStruct((1, half, width), jnp.bfloat16),
        ),
        in_specs=[VMEM] * 5,
        out_specs=[VMEM] * 5,
        scratch_shapes=[
            pltpu.VMEM((3, half, features), jnp.bfloat16),
            pltpu.VMEM((3, half, min(2 * width, total)), jnp.float32),
        ],
        compiler_params=PARAMS,
        cost_estimate=pl.CostEstimate(
            flops=8 * half * features * total, bytes_accessed=0, transcendentals=0
        ),
    )(x_all, s_all, w_part, part, last)


def grads_kernel(units, x_all, s_all, own, to_x, to_x_down, to_z):
    width = own.shape[2]
    for k, outs in enumerate(((own,), (to_x, to_x_down), (to_z,))):
        grad_parts(units, x_all, s_all, slice(k * width, (k + 1) * width), outs)


def weight_grads(units, x_all, s_all):
    half, total = units.shape[1:]
    features = x_all.shape[1]
    shapes = ((3, jnp.float32), (2, jnp.float32), (1, jnp.float32), (3, jnp.bfloat16))
    return pl.pallas_call(
        grads_kernel,
        out_shape=tuple(
            jax.ShapeDtypeStruct((count, half, features // 4), kind) for count, kind in shapes
        ),
        in_specs=[VMEM] * 3,
        out_specs=[VMEM] * 4,
        compiler_params=PARAMS,
        cost_estimate=pl.CostEstimate(flops=5 * half * features * total, bytes_accessed=0, transcendentals=0),
    )(units, x_all, s_all)


def write_rows(values, outs, held, sems, first):
    rows = pl.ds(pl.multiple_of(first, 16), held.shape[1])
    copies = []
    for i, out in enumerate(outs):
        held[i] = values(i)
        copies.append(pltpu.make_async_copy(held.at[i], out.at[rows, :], sems.at[i]))
        copies[-1].start()
    for copy in copies:
        copy.wait()


def give_kernel(got, got_down, out_0, out_1, out_2, held, sems):
    def values(i):
        return (got[i] if i < 2 else got_down[0]).astype(jnp.float32)

    first = (1 - lax.axis_index("wide") % 2) * held.shape[1]
    write_rows(values, (out_0, out_1, out_2), held, sems, first)


def keep_kernel(in_0, in_1, in_2, own, got, out_0, out_1, out_2, held, sems):
    def values(i):
        return own[i] + got[i].astype(jnp.float32)

    first = lax.axis_index("wide") % 2 * held.shape[1]
    write_rows(values, (out_0, out_1, out_2), held, sems, first)


def write_half(kernel, shape, held, values):
    held_in = [pltpu.with_memory_space_constraint(x, pltpu.HBM) for x in held]
    return pl.pallas_call(
        kernel,
        out_shape=(jax.ShapeDtypeStruct((2 * shape[1], shape[2]), jnp.float32),) * 3,
        in_specs=[HBM] * len(held) + [VMEM] * len(values),
        out_specs=[HBM] * 3,
        scratch_shapes=[pltpu.VMEM(shape, jnp.float32), pltpu.SemaphoreType.DMA((3,))],
        input_output_aliases={i: i for i in range(len(held))},
        compiler_params=PARAMS,
        cost_estimate=pl.CostEstimate(flops=1, bytes_accessed=0, transcendentals=0),
    )(*held_in, *values)


def cross_kernel(kept, got, sent):
    total = (kept.shape[1] - EXTRA) // 2
    tile = min(kept.shape[2], total)
    count = total // tile
    body = slice(0, 2 * total)
    sent[body, :] = (kept[1, body, :] + got[1, body, :].astype(jnp.float32)).astype(sent.dtype)
    sent[2 * total :, :] = jnp.zeros_like(sent[2 * total :, :])
    router = kept[0, 2 * total : 2 * total + count, :] + get_pair(got.at[0], 2 * total, count)
    put_pair(sent, 2 * total, router)


def cross_part(kept, got):
    return pl.pallas_call(
        cross_kernel,
        out_shape=jax.ShapeDtypeStruct(got.shape[1:], got.dtype),
        in_specs=[VMEM] * 2,
        out_specs=VMEM,
        compiler_params=PARAMS,
    )(kept, got)


def result_kernel(kept, got, across, out):
    total = (kept.shape[1] - EXTRA) // 2
    count = total // min(kept.shape[2], total)
    body, tail = slice(0, 2 * total), slice(2 * total, 2 * total + count)
    value = kept[0, body, :] + got[0, body, :].astype(jnp.float32)
    out[body, :] = value + across[body, :].astype(jnp.float32)
    out[2 * total :, :] = jnp.zeros_like(out[2 * total :, :])
    router = kept[0, tail, :] + get_pair(got.at[0], 2 * total, count)
    out[tail, :] = router + get_pair(across, 2 * total, count)


def result_parts(kept, got, across):
    return pl.pallas_call(
        result_kernel,
        out_shape=jax.ShapeDtypeStruct(kept.shape[1:], jnp.float32),
        in_specs=[VMEM] * 3,
        out_specs=VMEM,
        compiler_params=PARAMS,
    )(kept, got, across)


def first_kernel(kept, got, to_y, to_x):
    total = (kept.shape[1] - EXTRA) // 2
    slots = total // 4
    count = total // min(kept.shape[2], total)
    body = slice(0, total)
    to_y[body, :] = (kept[1, body, :] + got[1, body, :].astype(jnp.float32)).astype(to_y.dtype)
    put_pair(
        to_y,
        total,
        kept[0, 2 * total : 2 * total + count, :] + get_pair(got.at[0], 2 * total, count),
    )
    for part in range(2):
        for block in range(2):
            rows = slice(total + (2 * block + 1) * slots, total + (2 * block + 2) * slots)
            value = kept[part, rows, :] + got[part, rows, :].astype(jnp.float32)
            to_x[part, block * slots : (block + 1) * slots, :] = value.astype(to_x.dtype)


def first_parts(kept, got):
    total, width = (kept.shape[1] - EXTRA) // 2, kept.shape[2]
    return pl.pallas_call(
        first_kernel,
        out_shape=(
            jax.ShapeDtypeStruct((total + EXTRA, width), jnp.bfloat16),
            jax.ShapeDtypeStruct((2, total // 2, width), jnp.bfloat16),
        ),
        in_specs=[VMEM] * 2,
        out_specs=[VMEM] * 2,
        compiler_params=PARAMS,
    )(kept, got)


def ffn_kernel(kept, got, from_y, held, to_x):
    total = (kept.shape[1] - EXTRA) // 2
    slots, width = total // 4, kept.shape[2]
    count = total // min(width, total)
    router = kept[0, 2 * total : 2 * total + count, :] + get_pair(got.at[0], 2 * total, count)
    router = router + get_pair(from_y, total, count)
    pairs = []
    for block in range(4):
        rows = slice(block * slots, (block + 1) * slots)
        value = kept[0, rows, :] + got[0, rows, :].astype(jnp.float32)
        value = value + from_y[rows, :].astype(jnp.float32)
        out = to_x if block % 2 else held
        place = block // 2
        out[place * slots : (place + 1) * slots, :] = value.astype(out.dtype)
        lane = block * slots % width
        pairs.append(router[block * slots // width :, lane : lane + slots][:1])
    held[2 * slots :, :] = jnp.zeros_like(held[2 * slots :, :])
    to_x[2 * slots :, :] = jnp.zeros_like(to_x[2 * slots :, :])
    held[2 * slots : 2 * slots + 1, :slots] = pairs[0]
    held[2 * slots + 1 : 2 * slots + 2, :slots] = pairs[2]
    put_pair(to_x, 2 * slots, jnp.concatenate([pairs[1], pairs[3]], 0))


def ffn_parts(kept, got, from_y):
    total, width = (kept.shape[1] - EXTRA) // 2, kept.shape[2]
    shape = (total // 2 + EXTRA, width)
    return pl.pallas_call(
        ffn_kernel,
        out_shape=(
            jax.ShapeDtypeStruct(shape, jnp.float32),
            jax.ShapeDtypeStruct(shape, jnp.bfloat16),
        ),
        in_specs=[VMEM] * 3,
        out_specs=[VMEM] * 2,
        compiler_params=PARAMS,
    )(kept, got, from_y)


def input_kernel(kept, got, from_x, held, to_y):
    total = (kept.shape[1] - EXTRA) // 2
    slots = total // 4
    for part, out in enumerate((held, to_y)):
        for block in range(2):
            rows = slice(total + 2 * block * slots, total + (2 * block + 1) * slots)
            here = slice(block * slots, (block + 1) * slots)
            value = kept[part, rows, :] + got[part, rows, :].astype(jnp.float32)
            out[here, :] = (value + from_x[part, here, :].astype(jnp.float32)).astype(out.dtype)


def input_parts(kept, got, from_x):
    shape = from_x.shape[1:]
    return pl.pallas_call(
        input_kernel,
        out_shape=(
            jax.ShapeDtypeStruct(shape, jnp.float32),
            jax.ShapeDtypeStruct(shape, jnp.bfloat16),
        ),
        in_specs=[VMEM] * 3,
        out_specs=[VMEM] * 2,
        compiler_params=PARAMS,
    )(kept, got, from_x)


def last_kernel(ffn, from_x, grad, from_y, held, to_z):
    slots = grad.shape[0] // 2
    router = ffn[2 * slots : 2 * slots + 2, :] + get_pair(from_x, 2 * slots, 2)
    for block, out in enumerate((held, to_z)):
        rows = slice(block * slots, (block + 1) * slots)
        out[:slots, :] = (ffn[rows, :] + from_x[rows, :].astype(jnp.float32)).astype(out.dtype)
        out[slots : 2 * slots, :] = (grad[rows, :] + from_y[rows, :].astype(jnp.float32)).astype(
            out.dtype
        )
    held[2 * slots :, :] = jnp.broadcast_to(router[:1], (EXTRA, router.shape[1]))
    put_pair(to_z, 2 * slots, router[1:])


def last_parts(ffn, from_x, grad, from_y):
    return pl.pallas_call(
        last_kernel,
        out_shape=(
            jax.ShapeDtypeStruct(ffn.shape, jnp.float32),
            jax.ShapeDtypeStruct(ffn.shape, jnp.bfloat16),
        ),
        in_specs=[VMEM] * 4,
        out_specs=[VMEM] * 2,
        compiler_params=PARAMS,
        cost_estimate=pl.CostEstimate(flops=2 * 10**9, bytes_accessed=0, transcendentals=0),
    )(ffn, from_x, grad, from_y)


def finish_kernel(prob, own, *refs):
    got, (output, tokens_grad, prob_grad) = refs[:-3], refs[-3:]
    slots, width = output.shape
    ffn, grad = own[:slots, :], own[slots : 2 * slots, :]
    router = own[2 * slots : 2 * slots + 1, :]
    for ref in got:
        ffn = ffn + ref[:slots, :].astype(jnp.float32)
        grad = grad + ref[slots : 2 * slots, :].astype(jnp.float32)
        router = router + get_pair(ref, 2 * slots, 1)
    weight = jnp.broadcast_to(prob[...], (128, slots)).T[:, :1]
    output[...] = (ffn.astype(jnp.bfloat16).astype(jnp.float32) * weight).astype(jnp.bfloat16)
    tokens_grad[...] = grad.astype(jnp.bfloat16)
    prob_grad[...] = router[:, :slots] / prob[...]


def finish(prob, own, got):
    slots, width = (own.shape[0] - EXTRA) // 2, own.shape[1]
    part = jax.ShapeDtypeStruct((slots, width), jnp.bfloat16)
    return pl.pallas_call(
        finish_kernel,
        out_shape=(part, part, jax.ShapeDtypeStruct((1, slots), jnp.float32)),
        in_specs=[VMEM] * (2 + len(got)),
        out_specs=[VMEM] * 3,
        compiler_params=PARAMS,
    )(prob, own, *got)


def shards(tokens, cotangent, expert_ids, route_prob, gate_weight, up_weight, down_weight):
    wide_count = lax.axis_size("wide")
    narrow_count = lax.axis_size("narrow")
    expert_count = wide_count // 4
    tok_rows, features = tokens.shape
    width = features // narrow_count
    slots = min(4 * tok_rows // expert_count, tok_rows)
    direct = expert_count == 2 and slots == tok_rows
    place = lax.axis_index("narrow")
    masks = (1, 4, 5)
    groups = [
        [4 * e + 2 * b + a for e in range(expert_count) for a in range(2)] for b in range(2)
    ]

    weights = (gate_weight.T, up_weight.T, down_weight.T)
    if direct:
        keep, give, own, same, other = prologue(
            weights, (tokens, cotangent, expert_ids.T, route_prob[None, :]), width
        )
        mine = stack_parts(
            [partner(part, "wide", mask) for mask, part in zip(masks, (same, other, other))]
        )
    else:
        own = None
        keep, give = prologue(weights, (), width)
        chosen = expert_ids[:, 0]
        onehot = (chosen[:, None] == jnp.arange(expert_count, dtype=jnp.int32)[None, :]).astype(
            jnp.int32
        )
        rank = jnp.sum((jnp.cumsum(onehot, axis=0) - onehot) * onehot, axis=1)
        slot_place = chosen * slots + rank
        source = (
            jnp.full((expert_count * slots,), tok_rows, jnp.int32)
            .at[slot_place]
            .set(jnp.arange(tok_rows, dtype=jnp.int32))
        )
        scaled = (route_prob[:, None] * cotangent.astype(jnp.float32)).astype(jnp.bfloat16)
        both = jnp.stack([tokens, scaled])
        both = lax.dynamic_slice_in_dim(both, place * width, width, 2)
        both = jnp.concatenate([both, jnp.zeros((2, 1, width), jnp.bfloat16)], 1)
        routed = both[:, source].reshape(2, expert_count, slots, width).transpose(1, 0, 2, 3)
        routed = jnp.repeat(routed, 2, axis=0)
        mine = lax.all_to_all(
            routed, "wide", split_axis=0, concat_axis=0, axis_index_groups=groups, tiled=True
        )

    from_x, from_z = partner(give, "wide", 1), partner(keep, "wide", 2)
    from_d = partner(from_x, "wide", 2)
    across, from_z = lax.optimization_barrier((partner(mine, "narrow", 2), from_z))
    pieces = (mine, partner(mine, "narrow", 1), across, partner(across, "narrow", 1))
    x_all, s_all, w_part, part = gather_parts(own, pieces, (keep, from_x, from_z))
    units, kept, sent, grad_d, grad_d_down = outer(x_all, s_all, w_part, part, from_d)
    got = partner(sent, "narrow", 1)
    got_d_down = partner(grad_d_down, "wide", 2)
    got_d = partner(grad_d, "wide", 2)
    if direct:
        to_y, to_x = first_parts(kept, got)
        units, _ = lax.optimization_barrier((units, to_y))
        ffn_held, ffn_x = ffn_parts(kept, got, partner(to_y, "narrow", 2))
        grad_own, grad_x, grad_x_down, grad_z = weight_grads(units, x_all, s_all)
        from_x = partner(to_x, "wide", 1)
        from_x, _ = lax.optimization_barrier((from_x, ffn_x))
        grad_held, grad_y = input_parts(kept, got, from_x)
        grad_z, _ = lax.optimization_barrier((grad_z, from_x))
        grad_x, _, _ = lax.optimization_barrier((grad_x, ffn_x, grad_y))
        grad_x_down = (grad_x_down + got_d_down.astype(jnp.float32)).astype(jnp.bfloat16)
        got_x_down = partner(grad_x_down, "wide", 1)
        grad_held, got_x_down = lax.optimization_barrier((grad_held, got_x_down))
        held, to_z = last_parts(
            ffn_held, partner(ffn_x, "wide", 1), grad_held, partner(grad_y, "narrow", 2)
        )
        grad_x = (grad_x + got_d.astype(jnp.float32)).astype(jnp.bfloat16)
        got_x = partner(grad_x, "wide", 1)
        given = write_half(give_kernel, grad_own.shape, (), (got_x, got_x_down))
        held, _ = lax.optimization_barrier((held, given[0]))
        output, tokens_grad, prob_grad = finish(
            route_prob[None, :], held, [partner(to_z, "wide", 4)]
        )
        prob_grad = prob_grad[0]
    else:
        grad_own, grad_x, grad_x_down, grad_z = weight_grads(units, x_all, s_all)
        grad_x_down = (grad_x_down + got_d_down.astype(jnp.float32)).astype(jnp.bfloat16)
        got_x_down = partner(grad_x_down, "wide", 1)
        grad_x = (grad_x + got_d.astype(jnp.float32)).astype(jnp.bfloat16)
        got_x = partner(grad_x, "wide", 1)
        across = partner(cross_part(kept, got), "narrow", 2)
        result = result_parts(kept, got, across)
        total = (result.shape[0] - EXTRA) // 2
        parts = result[: 2 * total].astype(jnp.bfloat16)
        parts = parts.reshape(2, 2 * expert_count, slots, width)
        back = lax.all_to_all(
            parts, "wide", split_axis=1, concat_axis=1, axis_index_groups=groups, tiled=True
        )
        back = back.reshape(2, expert_count, 2, slots, width).astype(jnp.float32).sum(2)
        back = back.reshape(2, expert_count * slots, width)[:, slot_place]
        router = result[2 * total : 2 * total + total // min(width, total), : min(width, total)]
        router = router.reshape(2 * expert_count, slots)
        high = lax.reduce_precision(router, 8, 7)
        pair = jnp.stack([high, router - high], 1).astype(jnp.bfloat16)
        pair = lax.all_to_all(
            pair, "wide", split_axis=0, concat_axis=0, axis_index_groups=groups, tiled=True
        )
        router = pair.reshape(expert_count, 4, slots).astype(jnp.float32).sum(1)
        prob_grad = router.reshape(expert_count * slots)[slot_place] / route_prob
        ffn = back[0].astype(jnp.bfloat16).astype(jnp.float32)
        output = (route_prob[:, None] * ffn).astype(jnp.bfloat16)
        tokens_grad = back[1].astype(jnp.bfloat16)
        given = write_half(give_kernel, grad_own.shape, (), (got_x, got_x_down))
    got_z = partner(grad_z, "wide", 2)
    gate_grad, up_grad, down_grad = write_half(
        keep_kernel, grad_own.shape, given, (grad_own, got_z)
    )
    return (output, tokens_grad, prob_grad, gate_grad.T, up_grad.T, down_grad.T)


def solution(mesh):
    in_specs = (
        P("wide", None),
        P("wide", None),
        P("wide", None),
        P("wide"),
        P("wide", "narrow"),
        P("wide", "narrow"),
        P("wide", "narrow"),
    )
    out_specs = (
        P("wide", "narrow"),
        P("wide", "narrow"),
        P("wide"),
        P("wide", "narrow"),
        P("wide", "narrow"),
        P("wide", "narrow"),
    )
    return jax.shard_map(shards, mesh=mesh, in_specs=in_specs, out_specs=out_specs, check_vma=False)
```
